32 devices in a mesh: out: 4 (over x, core), in: 8 (over z, y).
Axes of the slice: x: 2, y: 2, z: 4, core: 2. Of those that a mesh axis runs over, the one named last changes fastest.
Arguments:
- kernel_weights: bfloat16 [2, 4096, 8192], P(None, 'out', 'in'), may hold values from -0.0625 to 0.0625
- mode_field: bfloat16 [8192, 1024], P('in', 'out'), may hold values from -6 to 6
- diff_blocks: bfloat16 [2, 4096, 1024], P(None, 'out', 'in'), may hold values from -6 to 6
- block_table: int32 [4, 8], replicated, may hold values from 0 to 3, as said below
Outputs:
- gain: bfloat16 [4096, 1024], P('out', 'in')
The draws below stay inside these ranges and needn't reach their ends.
Inputs may be any that keep to these rules, and one draw needn't show every extreme that they name: `block_table`: in every column the entries are 0 to 3, each once.
All inputs are finite; a program needn't handle non-finite values.
Results may differ from the reference program's by a relative error of at most 0.001.
Values may be sent and summed in bfloat16 or wider, within the bound.
No kernel may reach another device: no remote copies, remote signals or barrier semaphores. Data moves between devices by JAX's collectives and lax.ppermute only.
A program may use at most 64 MiB of HBM per device.

```python
import jax
import jax.numpy as jnp
from jax import lax

TO = 1024
TI = 1024
TERMS = 2
CELLS = 1024
K_OUT = 4096
L_IN = 8192
NBLK = 4
NCOL = 8


def draw_block_table(key, part):
    column_keys = jax.random.split(jax.random.fold_in(key, 7), NCOL)
    columns = jax.vmap(lambda column_key: jax.random.permutation(column_key, NBLK))(column_keys)
    return columns.T.astype(jnp.int32)


def block_scale(key, dims, shards, smallest, high):
    def one(axis_at, shards_of):
        draws = jax.random.uniform(jax.random.fold_in(jax.random.fold_in(key, 6), axis_at), (shards_of,), jnp.float32, smallest / len(shards), high / len(shards))
        return jnp.repeat(jnp.exp(draws), dims[axis_at] // shards_of).reshape((-1,) + (1,) * (len(dims) - axis_at - 1))

    gain = one(*shards[0])
    for cut in shards[1:]:
        gain = gain * one(*cut)
    return gain


def centred(own_key, extent, scale, most, shards=(), kind=jnp.bfloat16):
    values = jax.random.normal(own_key, extent, jnp.float32) * scale
    if len(shards) > 0:
        values = block_scale(own_key, extent, shards, -0.22, 0.18) * values
    return jnp.clip(values, min=-most, max=most).astype(kind)


def setup_inputs(seed: int = 0) -> dict:
    key_of = jax.random.split(jax.random.key(seed), 5)
    kernel_weights = centred(key_of[0], (TERMS, K_OUT, L_IN), L_IN ** -0.5, 0.0625, ((1, 4), (2, 8)))
    mode_field = centred(key_of[1], (L_IN, CELLS), 1.0, 6.0, ((0, 8), (1, 4)))
    diff_blocks = centred(key_of[2], (TERMS, NBLK * TO, CELLS), 1.0, 6.0, ((1, 4), (2, 8)))
    block_table = draw_block_table(jax.random.fold_in(key_of[4], 71), 0)
    return dict(kernel_weights=kernel_weights, mode_field=mode_field, diff_blocks=diff_blocks, block_table=block_table)


def reference(kernel_weights, mode_field, diff_blocks, block_table):
    def one_row(row_index):
        def accumulate(running, col_index):
            tile = lax.dynamic_slice(kernel_weights, (jnp.int32(0), (row_index * TO).astype(jnp.int32), (col_index * TI).astype(jnp.int32)), (TERMS, TO, TI))
            inputs = lax.dynamic_slice_in_dim(mode_field, (col_index * TI).astype(jnp.int32), TI, 0)
            wanted = block_table[row_index, col_index]
            chosen = lax.dynamic_slice_in_dim(diff_blocks, (wanted * TO).astype(jnp.int32), TO, 1)
            for term_index in range(TERMS):
                product = jnp.dot(tile[term_index], inputs, preferred_element_type=jnp.float32)
                running = running + chosen[term_index].astype(jnp.float32) * product
            return running, None
        total, _ = lax.scan(accumulate, jnp.zeros((TO, CELLS), jnp.float32), jnp.arange(NCOL, dtype=jnp.int32))
        return total.astype(jnp.bfloat16)
    rows_all = lax.map(one_row, jnp.arange(NBLK, dtype=jnp.int32))
    return rows_all.reshape(K_OUT, CELLS)
```

```python
import functools

import jax
import jax.numpy as jnp
from jax import lax
from jax.experimental import pallas as pl
from jax.experimental.pallas import tpu as pltpu
from jax.sharding import PartitionSpec as P

PAIR = 2
TOP = 32767.0
GROUPS = 4
LANES = 128


def routed_shards(kernel_weights, mode_field, diff_blocks, block_table):
    out_index = lax.axis_index("out")
    tile_rows = kernel_weights.shape[1]
    term_count = kernel_weights.shape[0]
    own_cells = diff_blocks.shape[2]
    needed_row = block_table[out_index]
    whole_field = lax.all_gather(mode_field, "out", axis=1, tiled=True)
    every_block = lax.all_gather(diff_blocks, "out", axis=1, tiled=True)
    block_count = every_block.shape[1] // tile_rows
    every_block = every_block.reshape(term_count, block_count, tile_rows, own_cells)
    arranged = jnp.take(every_block, needed_row, axis=1)
    routed = lax.all_to_all(arranged, "in", split_axis=1, concat_axis=3, tiled=True)
    partial_value = jnp.zeros((tile_rows, whole_field.shape[1]), jnp.float32)
    for term_index in range(term_count):
        product = jnp.dot(kernel_weights[term_index], whole_field, preferred_element_type=jnp.float32)
        partial_value = partial_value + routed[term_index, 0].astype(jnp.float32) * product
    summed = lax.psum_scatter(partial_value, "in", scatter_dimension=1, tiled=True)
    return summed.astype(jnp.bfloat16)


def encode(values):
    largest = jnp.maximum(jnp.max(jnp.abs(values), axis=0, keepdims=True), 1e-30)
    exponent = jnp.floor(jnp.log2(largest)) + 1.0
    share = jnp.abs(values) * jnp.exp2(-exponent)
    root = jnp.minimum(jnp.sqrt(share) * TOP, TOP)
    signed = jnp.round(jnp.where(values < 0, -root, root)).astype(jnp.int32)
    return signed, exponent.astype(jnp.int32)


def pack(high, low):
    return (high << 16) | (low & 0xFFFF)


def decode(codes, exponent):
    root = codes.astype(jnp.float32)
    return root * jnp.abs(root) * (jnp.exp2(exponent.astype(jnp.float32)) * (1.0 / (TOP * TOP)))


def unpack_high(packed, exponent):
    return decode(packed >> 16, exponent)


def unpack_low(packed, exponent):
    return decode((packed << 16) >> 16, exponent)


def choose(index, refs, *at):
    value = refs[0][at]
    for position in range(1, len(refs)):
        value = jnp.where(index == position, refs[position][at], value)
    return value


def multiply_kernel(place, weights, *refs):
    *fields, kept, sent, field, = refs
    group = pl.program_id(0)
    rows = weights.shape[1]
    total = GROUPS * rows
    half = kept.shape[2]

    @pl.when(group == 0)
    def _():
        for position, source in enumerate(fields):
            @pl.when(place[0] == position)
            def _():
                pltpu.sync_copy(source, field)

    first = place[1] == 0
    codes = []
    for term in range(weights.shape[0]):
        product = jnp.dot(weights[term], field[...], preferred_element_type=jnp.float32)
        low, high = product[:, :half], product[:, half:]
        kept[term] = jnp.where(first, low, high)
        code, exponent = encode(jnp.where(first, high, low))
        codes.append(code)
        sent[pl.ds(total + term * GROUPS + group, 1), :] = exponent
    sent[pl.ds(pl.multiple_of(group * rows, rows), rows), :] = pack(*codes)


def multiply(place, weights, fields):
    terms, rows, depth = weights.shape
    width = fields[0].shape[1]
    half = width // PAIR
    step = rows // GROUPS
    return pl.pallas_call(
        multiply_kernel,
        out_shape=(
            jax.ShapeDtypeStruct((terms, rows, half), jnp.float32),
            jax.ShapeDtypeStruct((rows + terms * GROUPS, half), jnp.int32),
        ),
        grid=(GROUPS,),
        in_specs=[
            pl.BlockSpec(memory_space=pltpu.SMEM),
            pl.BlockSpec((terms, step, depth), lambda g: (0, g, 0)),
        ] + [pl.BlockSpec(memory_space=pl.ANY)] * len(fields),
        out_specs=(
            pl.BlockSpec((terms, step, half), lambda g: (0, g, 0)),
            pl.BlockSpec((rows + terms * GROUPS, half), lambda g: (0, 0)),
        ),
        scratch_shapes=[pltpu.VMEM((depth, width), jnp.bfloat16)],
        compiler_params=pltpu.CompilerParams(vmem_limit_bytes=16 << 20),
        cost_estimate=pl.CostEstimate(
            flops=2 * terms * rows * depth * width,
            bytes_accessed=weights.size * 2 + rows * half * (4 * terms + 4),
            transcendentals=rows * half * terms,
        ),
    )(place, weights, *fields)


def blocks_times_products(place, kept, received, pieces, group, part):
    terms, _, step, _ = kept.shape
    rows = GROUPS * PAIR * step
    start = part * (rows // PAIR) + group * step
    packed = received[pl.ds(pl.multiple_of(start, step), step), :]
    scale = rows + start // (rows // GROUPS)
    mine = [kept[term, part] for term in range(terms)]
    other = [
        unpack_high(packed, received[pl.ds(scale, 1), :]),
        unpack_low(packed, received[pl.ds(scale + GROUPS, 1), :]),
    ]
    value = None
    for which, products in ((0, mine), (1, other)):
        for term in range(terms):
            chosen = choose(place[which], pieces, term, part).astype(jnp.float32)
            value = chosen * products[term] if value is None else value + chosen * products[term]
    return value


def partial_kernel(place, kept, received, *refs):
    *pieces, sent = refs
    group = pl.program_id(0)
    step = kept.shape[2]
    total = GROUPS * step
    codes = []
    for part in range(PAIR):
        value = blocks_times_products(place, kept, received, pieces, group, part)
        code, exponent = encode(value)
        codes.append(code)
        sent[pl.ds(total + part * GROUPS + group, 1), :] = exponent
    sent[pl.ds(pl.multiple_of(group * step, step), step), :] = pack(*codes)


def final_kernel(arrivals, place, kept, received, *refs):
    coming, pieces, gain = refs[:arrivals], refs[arrivals:-1], refs[-1]
    group = pl.program_id(0)
    step = kept.shape[2]
    total = GROUPS * step
    unpackers = (unpack_high, unpack_low)
    for part in range(PAIR):
        value = blocks_times_products(place, kept, received, pieces, group, part)
        for ref in coming:
            packed = ref[pl.ds(pl.multiple_of(group * step, step), step), :]
            value = value + unpackers[part](packed, ref[pl.ds(total + part * GROUPS + group, 1), :])
        gain[part] = value.astype(gain.dtype)


def product_call(kernel, name, place, kept, received, coming, pieces, out_shape, out_spec):
    terms, rows, cells = kept.shape
    step = rows // PAIR // GROUPS
    split = (terms, PAIR, rows // PAIR, cells)
    block = pl.BlockSpec((terms, PAIR, step, cells), lambda g: (0, 0, g, 0))
    whole = lambda array: pl.BlockSpec(array.shape, lambda g: (0, 0))
    return pl.pallas_call(
        kernel,
        name=name,
        out_shape=out_shape,
        grid=(GROUPS,),
        in_specs=[pl.BlockSpec(memory_space=pltpu.SMEM), block, whole(received)]
        + [whole(array) for array in coming] + [block] * len(pieces),
        out_specs=out_spec,
        compiler_params=pltpu.CompilerParams(vmem_limit_bytes=16 << 20),
        cost_estimate=pl.CostEstimate(
            flops=8 * terms * rows * cells,
            bytes_accessed=rows * cells * terms * (4 + 2 * len(pieces)) + rows * cells * 8,
            transcendentals=rows * cells,
        ),
    )(place, kept.reshape(split), received, *coming, *[piece.reshape(split) for piece in pieces])


def partial_sums(place, kept, received, pieces):
    terms, rows, cells = kept.shape
    shape = (rows // PAIR + PAIR * GROUPS, cells)
    return product_call(
        partial_kernel, "partial_sums", place, kept, received, [], pieces,
        jax.ShapeDtypeStruct(shape, jnp.int32), pl.BlockSpec(shape, lambda g: (0, 0)),
    )


def final_sums(place, kept, received, coming, pieces):
    terms, rows, cells = kept.shape
    step = rows // PAIR // GROUPS
    gain = product_call(
        functools.partial(final_kernel, len(coming)), "final_sums", place, kept, received, coming, pieces,
        jax.ShapeDtypeStruct((PAIR, rows // PAIR, cells), jnp.bfloat16),
        pl.BlockSpec((PAIR, step, cells), lambda g: (0, g, 0)),
    )
    return gain.reshape(rows, cells)


def gathered_shards(out_count, in_count, kernel_weights, mode_field, diff_blocks, block_table):
    chips, columns = out_count // PAIR, in_count // PAIR
    out_index, in_index = lax.axis_index("out"), lax.axis_index("in")
    chip, core = out_index // PAIR, out_index % PAIR
    column, side = in_index // PAIR, in_index % PAIR

    def across_cores(value):
        return lax.ppermute(value, "out", [(r, r ^ 1) for r in range(out_count)])

    def along_chips(value, shift):
        return lax.ppermute(value, "out", [(r, (r + PAIR * shift) % out_count) for r in range(out_count)])

    def across_sides(value):
        return lax.ppermute(value, "in", [(s, s ^ 1) for s in range(in_count)])

    def along_columns(value, shift):
        return lax.ppermute(value, "in", [(s, (s + PAIR * shift) % in_count) for s in range(in_count)])

    def from_every_chip(value):
        near = [value] + [along_chips(value, shift) for shift in range(1, chips)]
        return near + [across_cores(piece) for piece in near]

    def position(index):
        return (index % PAIR != core).astype(jnp.int32) * chips + (chip - index // PAIR) % chips

    fields = from_every_chip(mode_field)

    pieces, ring = [], diff_blocks
    for step in range(columns):
        if step > 0:
            ring = along_columns(ring, 1)
        pieces.append(from_every_chip(ring))

    row = lax.dynamic_index_in_dim(block_table, out_index, 0, keepdims=False)
    wanted = [position(row[column * PAIR + side]), position(row[column * PAIR + 1 - side])]
    product_place = jnp.stack(wanted).astype(jnp.int32)

    order = list(range(1, columns)) + [0]
    kept, received = {}, {}
    for step in order:
        target = (column - step) % columns
        place = jnp.stack([position(target), side]).astype(jnp.int32)
        kept[step], sent = multiply(place, kernel_weights, fields)
        received[step] = across_sides(sent)

    coming = []
    for step in order[:-1]:
        sent = partial_sums(product_place, kept[step], received[step], pieces[step])
        coming.append(along_columns(sent, -step))
    return final_sums(product_place, kept[0], received[0], coming, pieces[0])


def solution(mesh):
    out_count, in_count = mesh.shape["out"], mesh.shape["in"]
    in_specs = (P(None, "out", "in"), P("in", "out"), P(None, "out", "in"), P())
    out_specs = P("out", "in")

    def shards(kernel_weights, mode_field, diff_blocks, block_table):
        own_cells = diff_blocks.shape[2]
        gather = (
            kernel_weights.shape[0] == PAIR
            and own_cells % LANES == 0
            and mode_field.shape[1] == PAIR * own_cells
            and out_count % PAIR == 0
            and in_count == PAIR * out_count
        )
        if gather:
            return gathered_shards(out_count, in_count, kernel_weights, mode_field, diff_blocks, block_table)
        return routed_shards(kernel_weights, mode_field, diff_blocks, block_table)

    return jax.shard_map(shards, mesh=mesh, in_specs=in_specs, out_specs=out_specs, check_vma=False)
```

```python
import functools

import jax
import jax.numpy as jnp
from jax import lax
from jax.experimental import pallas as pl
from jax.experimental.pallas import tpu as pltpu
from jax.sharding import PartitionSpec as P

PAIR = 2
TOP = 32767.0
GROUPS = 4
STEPS = 2
KERNEL_MEMORY = 56 << 20
LANES = 128


def routed_shards(kernel_weights, mode_field, diff_blocks, block_table):
    out_index = lax.axis_index("out")
    tile_rows = kernel_weights.shape[1]
    term_count = kernel_weights.shape[0]
    own_cells = diff_blocks.shape[2]
    needed_row = block_table[out_index]
    whole_field = lax.all_gather(mode_field, "out", axis=1, tiled=True)
    every_block = lax.all_gather(diff_blocks, "out", axis=1, tiled=True)
    block_count = every_block.shape[1] // tile_rows
    every_block = every_block.reshape(term_count, block_count, tile_rows, own_cells)
    arranged = jnp.take(every_block, needed_row, axis=1)
    routed = lax.all_to_all(arranged, "in", split_axis=1, concat_axis=3, tiled=True)
    partial_value = jnp.zeros((tile_rows, whole_field.shape[1]), jnp.float32)
    for term_index in range(term_count):
        product = jnp.dot(kernel_weights[term_index], whole_field, preferred_element_type=jnp.float32)
        partial_value = partial_value + routed[term_index, 0].astype(jnp.float32) * product
    summed = lax.psum_scatter(partial_value, "in", scatter_dimension=1, tiled=True)
    return summed.astype(jnp.bfloat16)


def encode(values):
    largest = jnp.maximum(jnp.max(jnp.abs(values), axis=0, keepdims=True), 1e-30)
    exponent = jnp.floor(jnp.log2(largest)) + 1.0
    share = values * (jnp.exp2(-exponent) * (TOP * TOP))
    root = share * lax.rsqrt(jnp.abs(share) + 1e-9)
    return jnp.round(root).astype(jnp.int32), exponent.astype(jnp.int32)


def pack(high, low):
    return (high << 16) | (low & 0xFFFF)


def decode(codes, exponent):
    root = codes.astype(jnp.float32)
    return root * jnp.abs(root) * (jnp.exp2(exponent.astype(jnp.float32)) * (1.0 / (TOP * TOP)))


def unpack_high(packed, exponent):
    return decode(packed >> 16, exponent)


def unpack_low(packed, exponent):
    return decode((packed << 16) >> 16, exponent)


def position(index, out_index, chips):
    crossed = jnp.where(index % PAIR != out_index % PAIR, chips, 0)
    return crossed + (out_index // PAIR - index // PAIR + chips) % chips


def choose(index, refs, *at):
    value = refs[0][at]
    for place in range(1, len(refs)):
        value = jnp.where(index == place, refs[place][at], value)
    return value


def multiply_kernel(shift, columns, weights, *refs):
    *fields, kept, sent, field = refs
    step = pl.program_id(0)
    rows = weights.shape[1] * STEPS // GROUPS
    total = GROUPS * rows
    half = kept.shape[2]
    in_index = lax.axis_index("in")
    target = (in_index // PAIR - shift + columns) % columns
    source = position(target, lax.axis_index("out"), len(fields) // PAIR)

    @pl.when(step == 0)
    def _():
        for place, ref in enumerate(fields):
            @pl.when(source == place)
            def _():
                pltpu.sync_copy(ref, field)

    first = in_index % PAIR == 0
    for piece in range(GROUPS // STEPS):
        group = step * (GROUPS // STEPS) + piece
        codes = []
        for term in range(weights.shape[0]):
            tile = weights[term, piece * rows:(piece + 1) * rows]
            product = jnp.dot(tile, field[...], preferred_element_type=jnp.float32)
            low, high = product[:, :half], product[:, half:]
            kept[term, piece * rows:(piece + 1) * rows] = jnp.where(first, low, high)
            code, exponent = encode(jnp.where(first, high, low))
            codes.append(code)
            sent[pl.ds(total + term * GROUPS + group, 1), :] = exponent
        sent[pl.ds(pl.multiple_of(group * rows, rows), rows), :] = pack(*codes)


def multiply(shift, columns, weights, fields):
    terms, rows, depth = weights.shape
    width = fields[0].shape[1]
    half = width // PAIR
    step = rows // STEPS
    return pl.pallas_call(
        functools.partial(multiply_kernel, shift, columns),
        name="products",
        out_shape=(
            jax.ShapeDtypeStruct((terms, rows, half), jnp.float32),
            jax.ShapeDtypeStruct((rows + terms * GROUPS, half), jnp.int32),
        ),
        grid=(STEPS,),
        in_specs=[pl.BlockSpec((terms, step, depth), lambda g: (0, g, 0))]
        + [pl.BlockSpec(memory_space=pl.ANY)] * len(fields),
        out_specs=(
            pl.BlockSpec((terms, step, half), lambda g: (0, g, 0)),
            pl.BlockSpec((rows + terms * GROUPS, half), lambda g: (0, 0)),
        ),
        scratch_shapes=[pltpu.VMEM((depth, width), jnp.bfloat16)],
        compiler_params=pltpu.CompilerParams(vmem_limit_bytes=KERNEL_MEMORY),
        cost_estimate=pl.CostEstimate(
            flops=2 * terms * rows * depth * width,
            bytes_accessed=weights.size * 2 + rows * half * (4 * terms + 4),
            transcendentals=rows * half * terms,
        ),
    )(weights, *fields)


def wanted_blocks(table, chips):
    out_index, in_index = lax.axis_index("out"), lax.axis_index("in")
    column, side = in_index // PAIR, in_index % PAIR
    return [position(table[out_index, column * PAIR + near], out_index, chips) for near in (side, 1 - side)]


def blocks_times_products(wanted, kept, received, pieces, group, part):
    terms, _, step, _ = kept.shape
    rows = GROUPS * PAIR * step
    start = part * (rows // PAIR) + group * step
    packed = received[pl.ds(pl.multiple_of(start, step), step), :]
    scale = rows + start // (rows // GROUPS)
    mine = [kept[term, part] for term in range(terms)]
    other = [
        unpack_high(packed, received[pl.ds(scale, 1), :]),
        unpack_low(packed, received[pl.ds(scale + GROUPS, 1), :]),
    ]
    value = None
    for index, products in zip(wanted, (mine, other)):
        for term in range(terms):
            chosen = choose(index, pieces, term, part).astype(jnp.float32)
            value = chosen * products[term] if value is None else value + chosen * products[term]
    return value


def partial_kernel(table, kept, received, *refs):
    *pieces, sent = refs
    group = pl.program_id(0)
    step = kept.shape[2]
    total = GROUPS * step
    wanted = wanted_blocks(table, len(pieces) // PAIR)
    codes = []
    for part in range(PAIR):
        value = blocks_times_products(wanted, kept, received, pieces, group, part)
        code, exponent = encode(value)
        codes.append(code)
        sent[pl.ds(total + part * GROUPS + group, 1), :] = exponent
    sent[pl.ds(pl.multiple_of(group * step, step), step), :] = pack(*codes)


def final_kernel(arrivals, table, kept, received, *refs):
    coming, pieces, gain = refs[:arrivals], refs[arrivals:-1], refs[-1]
    group = pl.program_id(0)
    step = kept.shape[2]
    total = GROUPS * step
    wanted = wanted_blocks(table, len(pieces) // PAIR)
    unpackers = (unpack_high, unpack_low)
    for part in range(PAIR):
        value = blocks_times_products(wanted, kept, received, pieces, group, part)
        for ref in coming:
            packed = ref[pl.ds(pl.multiple_of(group * step, step), step), :]
            value = value + unpackers[part](packed, ref[pl.ds(total + part * GROUPS + group, 1), :])
        gain[part] = value.astype(gain.dtype)


def product_call(kernel, name, table, kept, received, coming, pieces, out_shape, out_spec):
    terms, rows, cells = kept.shape
    step = rows // PAIR // GROUPS
    split = (terms, PAIR, rows // PAIR, cells)
    block = pl.BlockSpec((terms, PAIR, step, cells), lambda g: (0, 0, g, 0))
    whole = lambda array: pl.BlockSpec(array.shape, lambda g: (0, 0))
    return pl.pallas_call(
        kernel,
        name=name,
        out_shape=out_shape,
        grid=(GROUPS,),
        in_specs=[pl.BlockSpec(memory_space=pltpu.SMEM), block, whole(received)]
        + [whole(array) for array in coming] + [block] * len(pieces),
        out_specs=out_spec,
        compiler_params=pltpu.CompilerParams(vmem_limit_bytes=KERNEL_MEMORY),
        cost_estimate=pl.CostEstimate(
            flops=8 * terms * rows * cells,
            bytes_accessed=rows * cells * terms * (4 + 2 * len(pieces)) + rows * cells * 8,
            transcendentals=rows * cells,
        ),
    )(table, kept.reshape(split), received, *coming, *[piece.reshape(split) for piece in pieces])


def partial_sums(table, kept, received, pieces):
    terms, rows, cells = kept.shape
    shape = (rows // PAIR + PAIR * GROUPS, cells)
    return product_call(
        partial_kernel, "partial_sums", table, kept, received, [], pieces,
        jax.ShapeDtypeStruct(shape, jnp.int32), pl.BlockSpec(shape, lambda g: (0, 0)),
    )


def final_sums(table, kept, received, coming, pieces):
    terms, rows, cells = kept.shape
    step = rows // PAIR // GROUPS
    gain = product_call(
        functools.partial(final_kernel, len(coming)), "final_sums", table, kept, received, coming, pieces,
        jax.ShapeDtypeStruct((PAIR, rows // PAIR, cells), jnp.bfloat16),
        pl.BlockSpec((PAIR, step, cells), lambda g: (0, g, 0)),
    )
    return gain.reshape(rows, cells)


def after(value, *earlier):
    return lax.optimization_barrier((value, *earlier))[0]


def gathered_shards(out_count, in_count, kernel_weights, mode_field, diff_blocks, block_table):
    chips, columns = out_count // PAIR, in_count // PAIR

    def across_cores(value):
        return lax.ppermute(value, "out", [(r, r ^ 1) for r in range(out_count)])

    def along_chips(value):
        return [
            lax.ppermute(value, "out", [(r, (r + PAIR * shift) % out_count) for r in range(out_count)])
            for shift in range(1, chips)
        ]

    def across_sides(value):
        return lax.ppermute(value, "in", [(s, s ^ 1) for s in range(in_count)])

    def along_columns(value, shift):
        return lax.ppermute(value, "in", [(s, (s + PAIR * shift) % in_count) for s in range(in_count)])

    def from_every_chip(value, far):
        near = [value] + far
        return near + [across_cores(piece) for piece in near]

    far_fields = along_chips(mode_field)
    fields = from_every_chip(mode_field, far_fields)

    rings, far = [diff_blocks], [None]
    for step in range(1, columns):
        rings.append(along_columns(rings[-1], 1))
        far.append(along_chips(after(rings[step], *far_fields) if step == 1 else rings[step]))
    far[0] = along_chips(after(diff_blocks, *far[-1]))
    pieces = [from_every_chip(rings[step], far[step]) for step in range(columns)]

    order = list(range(1, columns)) + [0]
    kept, received = {}, {}
    for place, step in enumerate(order):
        weights = kernel_weights if place < 2 else after(kernel_weights, received[order[place - 2]])
        kept[step], sent = multiply(step, columns, weights, fields)
        received[step] = across_sides(sent)

    coming = []
    for step in order[:-1]:
        sent = partial_sums(block_table, kept[step], received[step], pieces[step])
        coming.append(along_columns(sent, -step))
    return final_sums(block_table, kept[0], received[0], coming, pieces[0])


def solution(mesh):
    out_count, in_count = mesh.shape["out"], mesh.shape["in"]
    in_specs = (P(None, "out", "in"), P("in", "out"), P(None, "out", "in"), P())
    out_specs = P("out", "in")

    def shards(kernel_weights, mode_field, diff_blocks, block_table):
        own_cells = diff_blocks.shape[2]
        gather = (
            kernel_weights.shape[0] == PAIR
            and own_cells % LANES == 0
            and mode_field.shape[1] == PAIR * own_cells
            and out_count % PAIR == 0
            and in_count == PAIR * out_count
        )
        if gather:
            return gathered_shards(out_count, in_count, kernel_weights, mode_field, diff_blocks, block_table)
        return routed_shards(kernel_weights, mode_field, diff_blocks, block_table)

    return jax.shard_map(shards, mesh=mesh, in_specs=in_specs, out_specs=out_specs, check_vma=False)
```

```python
import functools
import math

import jax
import jax.numpy as jnp
from jax import lax
from jax.experimental import pallas as pl
from jax.experimental.pallas import tpu as pltpu
from jax.sharding import PartitionSpec as P

PAIR = 2
TOP = 32767.0
GROUPS = 4
KERNEL_MEMORY = 24 << 20
LANES = 128


def routed_shards(kernel_weights, mode_field, diff_blocks, block_table):
    out_index = lax.axis_index("out")
    tile_rows = kernel_weights.shape[1]
    term_count = kernel_weights.shape[0]
    own_cells = diff_blocks.shape[2]
    needed_row = block_table[out_index]
    whole_field = lax.all_gather(mode_field, "out", axis=1, tiled=True)
    every_block = lax.all_gather(diff_blocks, "out", axis=1, tiled=True)
    block_count = every_block.shape[1] // tile_rows
    every_block = every_block.reshape(term_count, block_count, tile_rows, own_cells)
    arranged = jnp.take(every_block, needed_row, axis=1)
    routed = lax.all_to_all(arranged, "in", split_axis=1, concat_axis=3, tiled=True)
    partial_value = jnp.zeros((tile_rows, whole_field.shape[1]), jnp.float32)
    for term_index in range(term_count):
        product = jnp.dot(kernel_weights[term_index], whole_field, preferred_element_type=jnp.float32)
        partial_value = partial_value + routed[term_index, 0].astype(jnp.float32) * product
    summed = lax.psum_scatter(partial_value, "in", scatter_dimension=1, tiled=True)
    return summed.astype(jnp.bfloat16)


def encode(values):
    largest = jnp.maximum(jnp.max(jnp.abs(values), axis=0, keepdims=True), 1e-30)
    exponent = jnp.floor(jnp.log2(largest)) + 1.0
    share = values * (jnp.exp2(-exponent) * (TOP * TOP))
    root = share * lax.rsqrt(jnp.abs(share) + 1e-9)
    return jnp.round(root).astype(jnp.int32), exponent.astype(jnp.int32)


def pack(high, low):
    return (high << 16) | (low & 0xFFFF)


def decode(codes, exponent):
    root = codes.astype(jnp.float32)
    return root * jnp.abs(root) * (jnp.exp2(exponent.astype(jnp.float32)) * (1.0 / (TOP * TOP)))


def unpack_high(packed, exponent):
    return decode(packed >> 16, exponent)


def unpack_low(packed, exponent):
    return decode((packed << 16) >> 16, exponent)


def position(index, out_index, chips):
    crossed = jnp.where(index % PAIR != out_index % PAIR, chips, 0)
    return crossed + (out_index // PAIR - index // PAIR + chips) % chips


def choose(index, refs, *at):
    value = refs[0][at]
    for place in range(1, len(refs)):
        value = jnp.where(index == place, refs[place][at], value)
    return value


def near(value):
    return pltpu.with_memory_space_constraint(value, pltpu.VMEM)


def kernel_call(kernel, name, inputs, in_table, outputs, scratch, flops, transcendentals):
    moved = sum(math.prod(array.shape) * jnp.dtype(array.dtype).itemsize for array in [*inputs, *outputs])
    memory = pl.BlockSpec(memory_space=pltpu.VMEM)
    return pl.pallas_call(
        kernel,
        name=name,
        out_shape=outputs,
        in_specs=[pl.BlockSpec(memory_space=pltpu.SMEM)] * in_table + [memory] * (len(inputs) - in_table),
        out_specs=[memory] * len(outputs),
        scratch_shapes=scratch,
        compiler_params=pltpu.CompilerParams(vmem_limit_bytes=KERNEL_MEMORY),
        cost_estimate=pl.CostEstimate(flops=flops, bytes_accessed=moved, transcendentals=transcendentals),
    )(*inputs)


def multiply_kernel(shift, columns, weights, *refs):
    *fields, kept, sent, field = refs
    terms, total, _ = weights.shape
    rows = total // GROUPS
    half = kept.shape[2]
    in_index = lax.axis_index("in")
    target = (in_index // PAIR - shift + columns) % columns
    source = position(target, lax.axis_index("out"), len(fields) // PAIR)
    side = in_index % PAIR

    for place, ref in enumerate(fields):
        for first in range(PAIR):
            @pl.when((source == place) & (side == first))
            def _():
                field[:, :half] = ref[:, first * half:(first + 1) * half]
                field[:, half:] = ref[:, (1 - first) * half:(2 - first) * half]

    for group in range(GROUPS):
        chosen = slice(group * rows, (group + 1) * rows)
        codes = []
        for term in range(terms):
            product = jnp.dot(weights[term, chosen], field[...], preferred_element_type=jnp.float32)
            kept[term, chosen] = product[:, :half]
            code, exponent = encode(product[:, half:])
            codes.append(code)
            place = total + term * GROUPS + group
            sent[place:place + 1, :] = exponent
        sent[chosen, :] = pack(*codes)


def multiply(shift, columns, weights, fields):
    terms, rows, depth = weights.shape
    width = fields[0].shape[1]
    half = width // PAIR
    return kernel_call(
        functools.partial(multiply_kernel, shift, columns),
        "products",
        [weights, *fields],
        0,
        [
            pltpu.VMEM((terms, rows, half), jnp.float32),
            pltpu.VMEM((rows + terms * GROUPS, half), jnp.int32),
        ],
        [pltpu.VMEM((depth, width), jnp.bfloat16)],
        2 * terms * rows * depth * width,
        rows * half * terms,
    )


def wanted_blocks(table, chips):
    out_index, in_index = lax.axis_index("out"), lax.axis_index("in")
    column, side = in_index // PAIR, in_index % PAIR
    return [position(table[out_index, column * PAIR + which], out_index, chips) for which in (side, 1 - side)]


def blocks_times_products(wanted, kept, received, pieces, rows, total):
    packed = received[rows, :]
    scale = total + rows.start // (total // GROUPS)
    mine = [kept[0, rows], kept[1, rows]]
    other = [
        unpack_high(packed, received[scale:scale + 1, :]),
        unpack_low(packed, received[scale + GROUPS:scale + GROUPS + 1, :]),
    ]
    value = None
    for index, products in zip(wanted, (mine, other)):
        for term, product in enumerate(products):
            chosen = choose(index, pieces, term, rows).astype(jnp.float32)
            value = chosen * product if value is None else value + chosen * product
    return value


def row_ranges(total):
    half = total // PAIR
    step = half // GROUPS
    return [
        [slice(part * half + group * step, part * half + (group + 1) * step) for part in range(PAIR)]
        for group in range(GROUPS)
    ]


def partial_kernel(table, kept, received, *refs):
    *pieces, sent = refs
    total = kept.shape[1]
    wanted = wanted_blocks(table, len(pieces) // PAIR)
    for group, parts in enumerate(row_ranges(total)):
        codes = []
        for part, rows in enumerate(parts):
            code, exponent = encode(blocks_times_products(wanted, kept, received, pieces, rows, total))
            codes.append(code)
            place = total // PAIR + part * GROUPS + group
            sent[place:place + 1, :] = exponent
        sent[parts[0], :] = pack(*codes)


def final_kernel(arrivals, table, kept, received, *refs):
    coming, pieces, gain = refs[:arrivals], refs[arrivals:-1], refs[-1]
    total = kept.shape[1]
    wanted = wanted_blocks(table, len(pieces) // PAIR)
    for group, parts in enumerate(row_ranges(total)):
        for part, (rows, unpack) in enumerate(zip(parts, (unpack_high, unpack_low))):
            value = blocks_times_products(wanted, kept, received, pieces, rows, total)
            place = total // PAIR + part * GROUPS + group
            for ref in coming:
                value = value + unpack(ref[parts[0], :], ref[place:place + 1, :])
            gain[rows, :] = value.astype(gain.dtype)


def partial_sums(table, kept, received, pieces):
    terms, rows, cells = kept.shape
    shape = (rows // PAIR + PAIR * GROUPS, cells)
    return kernel_call(
        partial_kernel, "partial_sums", [table, kept, received, *pieces], 1,
        [pltpu.VMEM(shape, jnp.int32)], [], 8 * terms * rows * cells, rows * cells,
    )[0]


def final_sums(table, kept, received, coming, pieces):
    terms, rows, cells = kept.shape
    return kernel_call(
        functools.partial(final_kernel, len(coming)), "final_sums", [table, kept, received, *coming, *pieces], 1,
        [jax.ShapeDtypeStruct((rows, cells), jnp.bfloat16)], [], 8 * terms * rows * cells, 0,
    )[0]


def together(values):
    return dict(zip(values, lax.optimization_barrier(list(values.values()))))


def gathered_shards(out_count, in_count, kernel_weights, mode_field, diff_blocks, block_table):
    columns = in_count // PAIR

    def across_cores(value):
        return lax.ppermute(value, "out", [(r, r ^ 1) for r in range(out_count)])

    def along_chips(value):
        return lax.ppermute(value, "out", [(r, (r + PAIR) % out_count) for r in range(out_count)])

    def across_sides(value):
        return lax.ppermute(value, "in", [(s, s ^ 1) for s in range(in_count)])

    def along_columns(value, shift):
        return lax.ppermute(value, "in", [(s, (s + PAIR * shift) % in_count) for s in range(in_count)])

    def product_step(place, state):
        step = order[place]
        state["kept", step], state["coded", step] = multiply(step, columns, state["weights"], fields)

    def sum_step(place, state):
        step = order[place]
        pieces = [near(state[name, step]) for name in ("ring", "far", "core", "core far")]
        received = near(state["received", step])
        state["partial", step] = partial_sums(block_table, state["kept", step], received, pieces)

    order = list(range(1, columns)) + [0]

    state = {
        "weights": near(kernel_weights),
        "far field": along_chips(mode_field),
        "core field": across_cores(mode_field),
        ("ring", 0): diff_blocks,
        ("ring", 1): along_columns(diff_blocks, 1),
        ("core", 0): across_cores(diff_blocks),
    }
    state = together(state)
    far_field = state["far field"]
    fields = [near(field) for field in [mode_field, far_field, state["core field"], across_cores(far_field)]]
    for phase in range(1, columns + 1):
        step = order[phase - 1]
        if phase == 1:
            product_step(0, state)
        if phase > 2:
            before = order[phase - 3]
            state["arrived", before] = along_columns(state["partial", before], -before)
        state["received", step] = across_sides(state["coded", step])
        if phase + 1 < columns:
            state["ring", phase + 1] = along_columns(state["ring", phase], 1)
        state["far", step] = along_chips(state["ring", step])
        if step > 0:
            state["core", step] = across_cores(state["ring", step])
        if phase > 1:
            before = order[phase - 2]
            state["core far", before] = across_cores(state["far", before])
        if phase < columns:
            product_step(phase, state)
        if phase > 1:
            sum_step(phase - 2, state)
        if phase == columns:
            before = order[phase - 2]
            state["arrived", before] = along_columns(state["partial", before], -before)
        else:
            state = together(state)

    far = state["far", 0]
    pieces = [near(piece) for piece in [diff_blocks, far, state["core", 0], across_cores(far)]]
    coming = [near(state["arrived", step]) for step in order[:-1]]
    return final_sums(block_table, state["kept", 0], near(state["received", 0]), coming, pieces)


def solution(mesh):
    out_count, in_count = mesh.shape["out"], mesh.shape["in"]
    in_specs = (P(None, "out", "in"), P("in", "out"), P(None, "out", "in"), P())
    out_specs = P("out", "in")

    def shards(kernel_weights, mode_field, diff_blocks, block_table):
        own_cells = diff_blocks.shape[2]
        gather = (
            kernel_weights.shape[0] == PAIR
            and own_cells % LANES == 0
            and mode_field.shape[1] == PAIR * own_cells
            and out_count == PAIR * PAIR
            and in_count == PAIR * out_count
        )
        if gather:
            return gathered_shards(out_count, in_count, kernel_weights, mode_field, diff_blocks, block_table)
        return routed_shards(kernel_weights, mode_field, diff_blocks, block_table)

    return jax.shard_map(shards, mesh=mesh, in_specs=in_specs, out_specs=out_specs, check_vma=False)
```

```python
import functools
import math

import jax
import jax.numpy as jnp
from jax import lax
from jax.experimental import pallas as pl
from jax.experimental.pallas import tpu as pltpu
from jax.sharding import PartitionSpec as P

PAIR = 2
TOP = 32767.0
GROUPS = 4
KERNEL_MEMORY = 24 << 20
LANES = 128


def routed_shards(kernel_weights, mode_field, diff_blocks, block_table):
    out_index = lax.axis_index("out")
    tile_rows = kernel_weights.shape[1]
    term_count = kernel_weights.shape[0]
    own_cells = diff_blocks.shape[2]
    needed_row = block_table[out_index]
    whole_field = lax.all_gather(mode_field, "out", axis=1, tiled=True)
    every_block = lax.all_gather(diff_blocks, "out", axis=1, tiled=True)
    block_count = every_block.shape[1] // tile_rows
    every_block = every_block.reshape(term_count, block_count, tile_rows, own_cells)
    arranged = jnp.take(every_block, needed_row, axis=1)
    routed = lax.all_to_all(arranged, "in", split_axis=1, concat_axis=3, tiled=True)
    partial_value = jnp.zeros((tile_rows, whole_field.shape[1]), jnp.float32)
    for term_index in range(term_count):
        product = jnp.dot(kernel_weights[term_index], whole_field, preferred_element_type=jnp.float32)
        partial_value = partial_value + routed[term_index, 0].astype(jnp.float32) * product
    summed = lax.psum_scatter(partial_value, "in", scatter_dimension=1, tiled=True)
    return summed.astype(jnp.bfloat16)


def encode(values):
    largest = jnp.maximum(jnp.max(jnp.abs(values), axis=0, keepdims=True), 1e-30)
    exponent = jnp.floor(jnp.log2(largest)) + 1.0
    share = values * (jnp.exp2(-exponent) * (TOP * TOP))
    root = share * lax.rsqrt(jnp.abs(share) + 1e-9)
    return jnp.round(root).astype(jnp.int32), exponent.astype(jnp.int32)


def pack(high, low):
    return (high << 16) | (low & 0xFFFF)


def decode(codes, exponent):
    root = codes.astype(jnp.float32)
    return root * jnp.abs(root) * (jnp.exp2(exponent.astype(jnp.float32)) * (1.0 / (TOP * TOP)))


def unpack_high(packed, exponent):
    return decode(packed >> 16, exponent)


def unpack_low(packed, exponent):
    return decode((packed << 16) >> 16, exponent)


def position(index, out_index, chips):
    crossed = jnp.where(index % PAIR != out_index % PAIR, chips, 0)
    return crossed + (out_index // PAIR - index // PAIR + chips) % chips


def choose(index, refs, *at):
    value = refs[0][at]
    for place in range(1, len(refs)):
        value = jnp.where(index == place, refs[place][at], value)
    return value


def near(value):
    return pltpu.with_memory_space_constraint(value, pltpu.VMEM)


def kernel_call(kernel, name, inputs, in_table, outputs, scratch, flops, transcendentals):
    moved = sum(math.prod(array.shape) * jnp.dtype(array.dtype).itemsize for array in [*inputs, *outputs])
    memory = pl.BlockSpec(memory_space=pltpu.VMEM)
    return pl.pallas_call(
        kernel,
        name=name,
        out_shape=outputs,
        in_specs=[pl.BlockSpec(memory_space=pltpu.SMEM)] * in_table + [memory] * (len(inputs) - in_table),
        out_specs=[memory] * len(outputs),
        scratch_shapes=scratch,
        compiler_params=pltpu.CompilerParams(vmem_limit_bytes=KERNEL_MEMORY),
        cost_estimate=pl.CostEstimate(flops=flops, bytes_accessed=moved, transcendentals=transcendentals),
    )(*inputs)


def load_kernel(*refs):
    count = len(refs) // 2
    for source, place in zip(refs[:count], refs[count:]):
        place[...] = source[...]


def load(arrays):
    return kernel_call(
        load_kernel, "load", [near(array) for array in arrays], 0,
        [pltpu.VMEM(array.shape, array.dtype) for array in arrays], [], 0, 0,
    )


def multiply_kernel(shift, columns, weights, *refs):
    *fields, kept, sent, field = refs
    terms, total, _ = weights.shape
    rows = total // GROUPS
    half = kept.shape[2]
    in_index = lax.axis_index("in")
    target = (in_index // PAIR - shift + columns) % columns
    source = position(target, lax.axis_index("out"), len(fields) // PAIR)
    side = in_index % PAIR

    for place, ref in enumerate(fields):
        for first in range(PAIR):
            @pl.when((source == place) & (side == first))
            def _():
                field[:, :half] = ref[:, first * half:(first + 1) * half]
                field[:, half:] = ref[:, (1 - first) * half:(2 - first) * half]

    for group in range(GROUPS):
        chosen = slice(group * rows, (group + 1) * rows)
        codes = []
        for term in range(terms):
            product = jnp.dot(weights[term, chosen], field[...], preferred_element_type=jnp.float32)
            kept[term, chosen] = product[:, :half]
            code, exponent = encode(product[:, half:])
            codes.append(code)
            place = total + term * GROUPS + group
            sent[place:place + 1, :] = exponent
        sent[chosen, :] = pack(*codes)


def multiply(shift, columns, weights, fields):
    terms, rows, depth = weights.shape
    width = fields[0].shape[1]
    half = width // PAIR
    return kernel_call(
        functools.partial(multiply_kernel, shift, columns),
        "products",
        [weights, *fields],
        0,
        [
            pltpu.VMEM((terms, rows, half), jnp.float32),
            pltpu.VMEM((rows + terms * GROUPS, half), jnp.int32),
        ],
        [pltpu.VMEM((depth, width), jnp.bfloat16)],
        2 * terms * rows * depth * width,
        rows * half * terms,
    )


def wanted_blocks(table, chips):
    out_index, in_index = lax.axis_index("out"), lax.axis_index("in")
    column, side = in_index // PAIR, in_index % PAIR
    return [position(table[out_index, column * PAIR + which], out_index, chips) for which in (side, 1 - side)]


def blocks_times_products(wanted, kept, received, pieces, rows, total):
    packed = received[rows, :]
    scale = total + rows.start // (total // GROUPS)
    mine = [kept[0, rows], kept[1, rows]]
    other = [
        unpack_high(packed, received[scale:scale + 1, :]),
        unpack_low(packed, received[scale + GROUPS:scale + GROUPS + 1, :]),
    ]
    value = None
    for index, products in zip(wanted, (mine, other)):
        for term, product in enumerate(products):
            chosen = choose(index, pieces, term, rows).astype(jnp.float32)
            value = chosen * product if value is None else value + chosen * product
    return value


def row_ranges(total):
    half = total // PAIR
    step = half // GROUPS
    return [
        [slice(part * half + group * step, part * half + (group + 1) * step) for part in range(PAIR)]
        for group in range(GROUPS)
    ]


def partial_kernel(table, kept, received, *refs):
    *pieces, sent = refs
    total = kept.shape[1]
    wanted = wanted_blocks(table, len(pieces) // PAIR)
    for group, parts in enumerate(row_ranges(total)):
        codes = []
        for part, rows in enumerate(parts):
            code, exponent = encode(blocks_times_products(wanted, kept, received, pieces, rows, total))
            codes.append(code)
            place = total // PAIR + part * GROUPS + group
            sent[place:place + 1, :] = exponent
        sent[parts[0], :] = pack(*codes)


def final_kernel(arrivals, table, kept, received, *refs):
    coming, pieces, gain = refs[:arrivals], refs[arrivals:-1], refs[-1]
    total = kept.shape[1]
    wanted = wanted_blocks(table, len(pieces) // PAIR)
    for group, parts in enumerate(row_ranges(total)):
        for part, (rows, unpack) in enumerate(zip(parts, (unpack_high, unpack_low))):
            value = blocks_times_products(wanted, kept, received, pieces, rows, total)
            place = total // PAIR + part * GROUPS + group
            for ref in coming:
                value = value + unpack(ref[parts[0], :], ref[place:place + 1, :])
            gain[rows, :] = value.astype(gain.dtype)


def partial_sums(table, kept, received, pieces):
    terms, rows, cells = kept.shape
    shape = (rows // PAIR + PAIR * GROUPS, cells)
    return kernel_call(
        partial_kernel, "partial_sums", [table, kept, received, *pieces], 1,
        [pltpu.VMEM(shape, jnp.int32)], [], 8 * terms * rows * cells, rows * cells,
    )[0]


def final_sums(table, kept, received, coming, pieces):
    terms, rows, cells = kept.shape
    return kernel_call(
        functools.partial(final_kernel, len(coming)), "final_sums", [table, kept, received, *coming, *pieces], 1,
        [jax.ShapeDtypeStruct((rows, cells), jnp.bfloat16)], [], 8 * terms * rows * cells, 0,
    )[0]


def after(value, *earlier):
    return lax.optimization_barrier((value, *earlier))[0]


def gathered_shards(out_count, in_count, kernel_weights, mode_field, diff_blocks, block_table):
    columns = in_count // PAIR

    def across_cores(value):
        return lax.ppermute(value, "out", [(r, r ^ 1) for r in range(out_count)])

    def along_chips(value):
        return lax.ppermute(value, "out", [(r, (r + PAIR) % out_count) for r in range(out_count)])

    def across_sides(value):
        return lax.ppermute(value, "in", [(s, s ^ 1) for s in range(in_count)])

    def along_columns(value, shift):
        return lax.ppermute(value, "in", [(s, (s + PAIR * shift) % in_count) for s in range(in_count)])

    order = list(range(1, columns)) + [0]
    weights, own_field, own_blocks = load([kernel_weights, mode_field, diff_blocks])
    far_field = after(along_chips(mode_field), weights)
    fields = [own_field] + [near(field) for field in (far_field, across_cores(mode_field), across_cores(far_field))]

    rings = [diff_blocks]
    for step in range(1, columns):
        rings.append(along_columns(rings[-1], 1))
    crossed, pieces = far_field, {}
    for step in order:
        crossed = along_chips(after(rings[step], crossed))
        pieces[step] = [near(rings[step]) if step > 0 else own_blocks, near(crossed)]
        pieces[step] += [near(across_cores(piece)) for piece in (rings[step], crossed)]

    kept, received, coming, earlier = {}, {}, [], []
    for place, step in enumerate(order):
        kept[step], sent = multiply(step, columns, weights, fields)
        if place > 1:
            before = order[place - 2]
            partial = partial_sums(block_table, kept[before], received[before], pieces[before])
            coming.append(near(along_columns(partial, -before)))
            earlier.append(partial)
        swapped = across_sides(after(sent, *earlier))
        received[step] = near(swapped)
        earlier = [swapped]
    before = order[-2]
    partial = partial_sums(block_table, kept[before], received[before], pieces[before])
    coming.append(near(along_columns(partial, -before)))
    return final_sums(block_table, kept[0], received[0], coming, pieces[0])


def solution(mesh):
    out_count, in_count = mesh.shape["out"], mesh.shape["in"]
    in_specs = (P(None, "out", "in"), P("in", "out"), P(None, "out", "in"), P())
    out_specs = P("out", "in")

    def shards(kernel_weights, mode_field, diff_blocks, block_table):
        own_cells = diff_blocks.shape[2]
        gather = (
            kernel_weights.shape[0] == PAIR
            and own_cells % LANES == 0
            and mode_field.shape[1] == PAIR * own_cells
            and out_count == PAIR * PAIR
            and in_count == PAIR * out_count
        )
        if gather:
            return gathered_shards(out_count, in_count, kernel_weights, mode_field, diff_blocks, block_table)
        return routed_shards(kernel_weights, mode_field, diff_blocks, block_table)

    return jax.shard_map(shards, mesh=mesh, in_specs=in_specs, out_specs=out_specs, check_vma=False)
```

```python
import functools
import math

import jax
import jax.numpy as jnp
from jax import lax
from jax.experimental import pallas as pl
from jax.experimental.pallas import tpu as pltpu
from jax.sharding import PartitionSpec as P

PAIR = 2
TOP = 32767.0
GROUPS = 4
KERNEL_MEMORY = 24 << 20
LANES = 128


def routed_shards(kernel_weights, mode_field, diff_blocks, block_table):
    out_index = lax.axis_index("out")
    tile_rows = kernel_weights.shape[1]
    term_count = kernel_weights.shape[0]
    own_cells = diff_blocks.shape[2]
    needed_row = block_table[out_index]
    whole_field = lax.all_gather(mode_field, "out", axis=1, tiled=True)
    every_block = lax.all_gather(diff_blocks, "out", axis=1, tiled=True)
    block_count = every_block.shape[1] // tile_rows
    every_block = every_block.reshape(term_count, block_count, tile_rows, own_cells)
    arranged = jnp.take(every_block, needed_row, axis=1)
    routed = lax.all_to_all(arranged, "in", split_axis=1, concat_axis=3, tiled=True)
    partial_value = jnp.zeros((tile_rows, whole_field.shape[1]), jnp.float32)
    for term_index in range(term_count):
        product = jnp.dot(kernel_weights[term_index], whole_field, preferred_element_type=jnp.float32)
        partial_value = partial_value + routed[term_index, 0].astype(jnp.float32) * product
    summed = lax.psum_scatter(partial_value, "in", scatter_dimension=1, tiled=True)
    return summed.astype(jnp.bfloat16)


def encode(values):
    largest = jnp.maximum(jnp.max(jnp.abs(values), axis=0, keepdims=True), 1e-30)
    exponent = jnp.floor(jnp.log2(largest)) + 1.0
    share = values * (jnp.exp2(-exponent) * (TOP * TOP))
    root = share * lax.rsqrt(jnp.abs(share) + 1e-9)
    return jnp.round(root).astype(jnp.int32), exponent.astype(jnp.int32)


def pack(high, low):
    return (high << 16) | (low & 0xFFFF)


def decode(codes, exponent):
    root = codes.astype(jnp.float32)
    return root * jnp.abs(root) * (jnp.exp2(exponent.astype(jnp.float32)) * (1.0 / (TOP * TOP)))


def unpack_high(packed, exponent):
    return decode(packed >> 16, exponent)


def unpack_low(packed, exponent):
    return decode((packed << 16) >> 16, exponent)


def position(index, out_index, chips):
    crossed = jnp.where(index % PAIR != out_index % PAIR, chips, 0)
    return crossed + (out_index // PAIR - index // PAIR + chips) % chips


def choose(index, refs, *at):
    value = refs[0][at]
    for place in range(1, len(refs)):
        value = jnp.where(index == place, refs[place][at], value)
    return value


def near(value):
    return pltpu.with_memory_space_constraint(value, pltpu.VMEM)


def kernel_call(kernel, name, inputs, in_table, outputs, scratch, flops, transcendentals):
    moved = sum(math.prod(array.shape) * jnp.dtype(array.dtype).itemsize for array in [*inputs, *outputs])
    memory = pl.BlockSpec(memory_space=pltpu.VMEM)
    return pl.pallas_call(
        kernel,
        name=name,
        out_shape=outputs,
        in_specs=[pl.BlockSpec(memory_space=pltpu.SMEM)] * in_table + [memory] * (len(inputs) - in_table),
        out_specs=[memory] * len(outputs),
        scratch_shapes=scratch,
        compiler_params=pltpu.CompilerParams(vmem_limit_bytes=KERNEL_MEMORY),
        cost_estimate=pl.CostEstimate(flops=flops, bytes_accessed=moved, transcendentals=transcendentals),
    )(*inputs)


def load_kernel(*refs):
    count = len(refs) // 2
    for source, place in zip(refs[:count], refs[count:]):
        place[...] = source[...]


def load(arrays):
    return kernel_call(
        load_kernel, "load", [near(array) for array in arrays], 0,
        [pltpu.VMEM(array.shape, array.dtype) for array in arrays], [], 0, 0,
    )


def multiply_kernel(shift, columns, weights, *refs):
    *fields, kept, sent, field = refs
    terms, total, _ = weights.shape
    rows = total // GROUPS
    half = kept.shape[2]
    in_index = lax.axis_index("in")
    target = (in_index // PAIR - shift + columns) % columns
    source = position(target, lax.axis_index("out"), len(fields) // PAIR)
    side = in_index % PAIR

    for place, ref in enumerate(fields):
        for first in range(PAIR):
            @pl.when((source == place) & (side == first))
            def _():
                field[:, :half] = ref[:, first * half:(first + 1) * half]
                field[:, half:] = ref[:, (1 - first) * half:(2 - first) * half]

    for group in range(GROUPS):
        chosen = slice(group * rows, (group + 1) * rows)
        codes = []
        for term in range(terms):
            product = jnp.dot(weights[term, chosen], field[...], preferred_element_type=jnp.float32)
            kept[term, chosen] = product[:, :half]
            code, exponent = encode(product[:, half:])
            codes.append(code)
            place = total + term * GROUPS + group
            sent[place:place + 1, :] = exponent
        sent[chosen, :] = pack(*codes)


def multiply(shift, columns, weights, fields):
    terms, rows, depth = weights.shape
    width = fields[0].shape[1]
    half = width // PAIR
    return kernel_call(
        functools.partial(multiply_kernel, shift, columns),
        "products",
        [weights, *fields],
        0,
        [
            pltpu.VMEM((terms, rows, half), jnp.float32),
            pltpu.VMEM((rows + terms * GROUPS, half), jnp.int32),
        ],
        [pltpu.VMEM((depth, width), jnp.bfloat16)],
        2 * terms * rows * depth * width,
        rows * half * terms,
    )


def wanted_blocks(table, chips):
    out_index, in_index = lax.axis_index("out"), lax.axis_index("in")
    column, side = in_index // PAIR, in_index % PAIR
    return [position(table[out_index, column * PAIR + which], out_index, chips) for which in (side, 1 - side)]


def blocks_times_products(wanted, kept, received, pieces, rows, total):
    packed = received[rows, :]
    scale = total + rows.start // (total // GROUPS)
    mine = [kept[0, rows], kept[1, rows]]
    other = [
        unpack_high(packed, received[scale:scale + 1, :]),
        unpack_low(packed, received[scale + GROUPS:scale + GROUPS + 1, :]),
    ]
    value = None
    for index, products in zip(wanted, (mine, other)):
        for term, product in enumerate(products):
            chosen = choose(index, pieces, term, rows).astype(jnp.float32)
            value = chosen * product if value is None else value + chosen * product
    return value


def row_ranges(total):
    half = total // PAIR
    step = half // GROUPS
    return [
        [slice(part * half + group * step, part * half + (group + 1) * step) for part in range(PAIR)]
        for group in range(GROUPS)
    ]


def partial_kernel(table, kept, received, *refs):
    *pieces, sent = refs
    total = kept.shape[1]
    wanted = wanted_blocks(table, len(pieces) // PAIR)
    for group, parts in enumerate(row_ranges(total)):
        codes = []
        for part, rows in enumerate(parts):
            code, exponent = encode(blocks_times_products(wanted, kept, received, pieces, rows, total))
            codes.append(code)
            place = total // PAIR + part * GROUPS + group
            sent[place:place + 1, :] = exponent
        sent[parts[0], :] = pack(*codes)


def final_kernel(arrivals, table, kept, received, *refs):
    coming, pieces, gain = refs[:arrivals], refs[arrivals:-1], refs[-1]
    total = kept.shape[1]
    wanted = wanted_blocks(table, len(pieces) // PAIR)
    for group, parts in enumerate(row_ranges(total)):
        for part, (rows, unpack) in enumerate(zip(parts, (unpack_high, unpack_low))):
            value = blocks_times_products(wanted, kept, received, pieces, rows, total)
            place = total // PAIR + part * GROUPS + group
            for ref in coming:
                value = value + unpack(ref[parts[0], :], ref[place:place + 1, :])
            gain[rows, :] = value.astype(gain.dtype)


def partial_sums(table, kept, received, pieces):
    terms, rows, cells = kept.shape
    shape = (rows // PAIR + PAIR * GROUPS, cells)
    return kernel_call(
        partial_kernel, "partial_sums", [table, kept, received, *pieces], 1,
        [pltpu.VMEM(shape, jnp.int32)], [], 8 * terms * rows * cells, rows * cells,
    )[0]


def final_sums(table, kept, received, coming, pieces):
    terms, rows, cells = kept.shape
    return kernel_call(
        functools.partial(final_kernel, len(coming)), "final_sums", [table, kept, received, *coming, *pieces], 1,
        [jax.ShapeDtypeStruct((rows, cells), jnp.bfloat16)], [], 8 * terms * rows * cells, 0,
    )[0]


def after(value, *earlier):
    return lax.optimization_barrier((value, *earlier))[0]


def gathered_shards(out_count, in_count, kernel_weights, mode_field, diff_blocks, block_table):
    columns = in_count // PAIR

    def across_cores(value):
        return lax.ppermute(value, "out", [(r, r ^ 1) for r in range(out_count)])

    def along_chips(value):
        return lax.ppermute(value, "out", [(r, (r + PAIR) % out_count) for r in range(out_count)])

    def across_sides(value):
        return lax.ppermute(value, "in", [(s, s ^ 1) for s in range(in_count)])

    def along_columns(value, shift):
        return lax.ppermute(value, "in", [(s, (s + PAIR * shift) % in_count) for s in range(in_count)])

    order = list(range(1, columns)) + [0]
    weights, own_field, own_blocks = load([kernel_weights, mode_field, diff_blocks])
    far_field = after(along_chips(mode_field), weights)
    fields = [own_field] + [near(field) for field in (far_field, across_cores(mode_field), across_cores(far_field))]

    rings = [diff_blocks]
    for step in range(1, columns):
        rings.append(along_columns(rings[-1], 1))
    kept, sent = {}, {}
    for step in order:
        kept[step], sent[step] = multiply(step, columns, weights, fields)
    crossed, pieces = far_field, {}
    for place, step in enumerate(order):
        crossed = along_chips(after(rings[step], crossed, *([sent[order[place - 1]]] if place > 0 else [])))
        pieces[step] = [near(rings[step]) if step > 0 else own_blocks, near(crossed)]
        pieces[step] += [near(across_cores(piece)) for piece in (rings[step], crossed)]

    received, coming = {}, []

    def send_sums(place):
        step = order[place]
        ready = after(kept[step], *coming[-1:])
        partial = partial_sums(block_table, ready, received[step], pieces[step])
        coming.append(near(along_columns(partial, -step)))
        return partial

    for place, step in enumerate(order):
        earlier = [received[order[place - 1]]] if place > 0 else []
        if place > 1:
            earlier.append(send_sums(place - 2))
        received[step] = near(across_sides(after(sent[step], *earlier)))
    send_sums(len(order) - 2)
    return final_sums(block_table, kept[0], received[0], coming, pieces[0])


def solution(mesh):
    out_count, in_count = mesh.shape["out"], mesh.shape["in"]
    in_specs = (P(None, "out", "in"), P("in", "out"), P(None, "out", "in"), P())
    out_specs = P("out", "in")

    def shards(kernel_weights, mode_field, diff_blocks, block_table):
        own_cells = diff_blocks.shape[2]
        gather = (
            kernel_weights.shape[0] == PAIR
            and own_cells % LANES == 0
            and mode_field.shape[1] == PAIR * own_cells
            and out_count == PAIR * PAIR
            and in_count == PAIR * out_count
        )
        if gather:
            return gathered_shards(out_count, in_count, kernel_weights, mode_field, diff_blocks, block_table)
        return routed_shards(kernel_weights, mode_field, diff_blocks, block_table)

    return jax.shard_map(shards, mesh=mesh, in_specs=in_specs, out_specs=out_specs, check_vma=False)
```

```python
import functools
import math

import jax
import jax.numpy as jnp
from jax import lax
from jax.experimental import pallas as pl
from jax.experimental.pallas import tpu as pltpu
from jax.sharding import PartitionSpec as P

PAIR = 2
TOP = 32767.0
GROUPS = 4
KERNEL_MEMORY = 24 << 20
LANES = 128


def routed_shards(kernel_weights, mode_field, diff_blocks, block_table):
    out_index = lax.axis_index("out")
    tile_rows = kernel_weights.shape[1]
    term_count = kernel_weights.shape[0]
    own_cells = diff_blocks.shape[2]
    needed_row = block_table[out_index]
    whole_field = lax.all_gather(mode_field, "out", axis=1, tiled=True)
    every_block = lax.all_gather(diff_blocks, "out", axis=1, tiled=True)
    block_count = every_block.shape[1] // tile_rows
    every_block = every_block.reshape(term_count, block_count, tile_rows, own_cells)
    arranged = jnp.take(every_block, needed_row, axis=1)
    routed = lax.all_to_all(arranged, "in", split_axis=1, concat_axis=3, tiled=True)
    partial_value = jnp.zeros((tile_rows, whole_field.shape[1]), jnp.float32)
    for term_index in range(term_count):
        product = jnp.dot(kernel_weights[term_index], whole_field, preferred_element_type=jnp.float32)
        partial_value = partial_value + routed[term_index, 0].astype(jnp.float32) * product
    summed = lax.psum_scatter(partial_value, "in", scatter_dimension=1, tiled=True)
    return summed.astype(jnp.bfloat16)


def encode(values):
    largest = jnp.maximum(jnp.max(jnp.abs(values), axis=0, keepdims=True), 1e-30)
    exponent = jnp.floor(jnp.log2(largest)) + 1.0
    share = values * (jnp.exp2(-exponent) * (TOP * TOP))
    root = share * lax.rsqrt(jnp.abs(share) + 1e-9)
    return jnp.round(root).astype(jnp.int32), exponent.astype(jnp.int32)


def pack(high, low):
    return (high << 16) | (low & 0xFFFF)


def decode(codes, exponent):
    root = codes.astype(jnp.float32)
    return root * jnp.abs(root) * (jnp.exp2(exponent.astype(jnp.float32)) * (1.0 / (TOP * TOP)))


def unpack_high(packed, exponent):
    return decode(packed >> 16, exponent)


def unpack_low(packed, exponent):
    return decode((packed << 16) >> 16, exponent)


def position(index, out_index, chips):
    crossed = jnp.where(index % PAIR != out_index % PAIR, chips, 0)
    return crossed + (out_index // PAIR - index // PAIR + chips) % chips


def choose(index, refs, *at):
    value = refs[0][at]
    for place in range(1, len(refs)):
        value = jnp.where(index == place, refs[place][at], value)
    return value


def near(value):
    return pltpu.with_memory_space_constraint(value, pltpu.VMEM)


def kernel_call(kernel, name, inputs, in_table, outputs, scratch, flops, transcendentals):
    moved = sum(math.prod(array.shape) * jnp.dtype(array.dtype).itemsize for array in [*inputs, *outputs])
    memory = pl.BlockSpec(memory_space=pltpu.VMEM)
    return pl.pallas_call(
        kernel,
        name=name,
        out_shape=outputs,
        in_specs=[pl.BlockSpec(memory_space=pltpu.SMEM)] * in_table + [memory] * (len(inputs) - in_table),
        out_specs=[memory] * len(outputs),
        scratch_shapes=scratch,
        compiler_params=pltpu.CompilerParams(vmem_limit_bytes=KERNEL_MEMORY),
        cost_estimate=pl.CostEstimate(flops=3 * flops, bytes_accessed=3 * moved, transcendentals=transcendentals),
    )(*inputs)


def load_kernel(*refs):
    count = len(refs) // 2
    for source, place in zip(refs[:count], refs[count:]):
        place[...] = source[...]


def load(arrays):
    return kernel_call(
        load_kernel, "load", [near(array) for array in arrays], 0,
        [pltpu.VMEM(array.shape, array.dtype) for array in arrays], [], 0, 0,
    )


def multiply_kernel(shift, columns, weights, *refs):
    *fields, kept, sent, field = refs
    terms, total, _ = weights.shape
    rows = total // GROUPS
    half = kept.shape[2]
    in_index = lax.axis_index("in")
    target = (in_index // PAIR - shift + columns) % columns
    source = position(target, lax.axis_index("out"), len(fields) // PAIR)
    side = in_index % PAIR

    for place, ref in enumerate(fields):
        for first in range(PAIR):
            @pl.when((source == place) & (side == first))
            def _():
                field[:, :half] = ref[:, first * half:(first + 1) * half]
                field[:, half:] = ref[:, (1 - first) * half:(2 - first) * half]

    for group in range(GROUPS):
        chosen = slice(group * rows, (group + 1) * rows)
        codes = []
        for term in range(terms):
            product = jnp.dot(weights[term, chosen], field[...], preferred_element_type=jnp.float32)
            kept[term, chosen] = product[:, :half]
            code, exponent = encode(product[:, half:])
            codes.append(code)
            place = total + term * GROUPS + group
            sent[place:place + 1, :] = exponent
        sent[chosen, :] = pack(*codes)


def multiply(shift, columns, weights, fields):
    terms, rows, depth = weights.shape
    width = fields[0].shape[1]
    half = width // PAIR
    return kernel_call(
        functools.partial(multiply_kernel, shift, columns),
        "products",
        [weights, *fields],
        0,
        [
            pltpu.VMEM((terms, rows, half), jnp.float32),
            pltpu.VMEM((rows + terms * GROUPS, half), jnp.int32),
        ],
        [pltpu.VMEM((depth, width), jnp.bfloat16)],
        2 * terms * rows * depth * width,
        rows * half * terms,
    )


def wanted_blocks(table, chips):
    out_index, in_index = lax.axis_index("out"), lax.axis_index("in")
    column, side = in_index // PAIR, in_index % PAIR
    return [position(table[out_index, column * PAIR + which], out_index, chips) for which in (side, 1 - side)]


def blocks_times_products(wanted, kept, received, pieces, rows, total):
    packed = received[rows, :]
    scale = total + rows.start // (total // GROUPS)
    mine = [kept[0, rows], kept[1, rows]]
    other = [
        unpack_high(packed, received[scale:scale + 1, :]),
        unpack_low(packed, received[scale + GROUPS:scale + GROUPS + 1, :]),
    ]
    value = None
    for index, products in zip(wanted, (mine, other)):
        for term, product in enumerate(products):
            chosen = choose(index, pieces, term, rows).astype(jnp.float32)
            value = chosen * product if value is None else value + chosen * product
    return value


def row_ranges(total):
    half = total // PAIR
    step = half // GROUPS
    return [
        [slice(part * half + group * step, part * half + (group + 1) * step) for part in range(PAIR)]
        for group in range(GROUPS)
    ]


def partial_kernel(table, kept, received, *refs):
    *pieces, sent = refs
    total = kept.shape[1]
    wanted = wanted_blocks(table, len(pieces) // PAIR)
    for group, parts in enumerate(row_ranges(total)):
        codes = []
        for part, rows in enumerate(parts):
            code, exponent = encode(blocks_times_products(wanted, kept, received, pieces, rows, total))
            codes.append(code)
            place = total // PAIR + part * GROUPS + group
            sent[place:place + 1, :] = exponent
        sent[parts[0], :] = pack(*codes)


def final_kernel(arrivals, table, kept, received, *refs):
    coming, pieces, gain = refs[:arrivals], refs[arrivals:-1], refs[-1]
    total = kept.shape[1]
    wanted = wanted_blocks(table, len(pieces) // PAIR)
    for group, parts in enumerate(row_ranges(total)):
        for part, (rows, unpack) in enumerate(zip(parts, (unpack_high, unpack_low))):
            value = blocks_times_products(wanted, kept, received, pieces, rows, total)
            place = total // PAIR + part * GROUPS + group
            for ref in coming:
                value = value + unpack(ref[parts[0], :], ref[place:place + 1, :])
            gain[rows, :] = value.astype(gain.dtype)


def partial_sums(table, kept, received, pieces):
    terms, rows, cells = kept.shape
    shape = (rows // PAIR + PAIR * GROUPS, cells)
    return kernel_call(
        partial_kernel, "partial_sums", [table, kept, received, *pieces], 1,
        [pltpu.VMEM(shape, jnp.int32)], [], 8 * terms * rows * cells, rows * cells,
    )[0]


def final_sums(table, kept, received, coming, pieces):
    terms, rows, cells = kept.shape
    return kernel_call(
        functools.partial(final_kernel, len(coming)), "final_sums", [table, kept, received, *coming, *pieces], 1,
        [jax.ShapeDtypeStruct((rows, cells), jnp.bfloat16)], [], 8 * terms * rows * cells, 0,
    )[0]


def after(value, *earlier):
    return lax.optimization_barrier((value, *earlier))[0]


def gathered_shards(out_count, in_count, kernel_weights, mode_field, diff_blocks, block_table):
    columns = in_count // PAIR

    def across_cores(value):
        return lax.ppermute(value, "out", [(r, r ^ 1) for r in range(out_count)])

    def along_chips(value):
        return lax.ppermute(value, "out", [(r, (r + PAIR) % out_count) for r in range(out_count)])

    def across_sides(value):
        return lax.ppermute(value, "in", [(s, s ^ 1) for s in range(in_count)])

    def along_columns(value, shift):
        return lax.ppermute(value, "in", [(s, (s + PAIR * shift) % in_count) for s in range(in_count)])

    order = list(range(1, columns)) + [0]
    weights, own_field, own_blocks = load([kernel_weights, mode_field, diff_blocks])
    rings = [diff_blocks]
    for step in range(1, columns):
        rings.append(along_columns(rings[-1], 1))
    far_field = after(along_chips(mode_field), weights)
    core_field = after(across_cores(mode_field), rings[1])
    fields = [own_field] + [near(field) for field in (far_field, core_field, across_cores(far_field))]

    kept, sent = {}, {}
    for step in order:
        kept[step], sent[step] = multiply(step, columns, weights, fields)

    far, received, coming = {}, {}, []
    core = {step: across_cores(rings[step]) for step in (0, order[0])}
    early, crossed, sums = [*sent.values(), *core.values()], far_field, []
    for place, step in enumerate(order):
        last = place == columns - 1
        filling = [[], early][place] if place < 2 else [core[order[place - 1]]]
        filling = filling + (coming[:1] if last else [])
        crossed = far[step] = along_chips(after(rings[step], crossed, *filling))
        received[step] = near(across_sides(after(sent[step], *[received[before] for before in order[max(place - 1, 0):place]])))
        earlier = coming[1:2] if last else sums if place > 0 else list(sent.values())
        core_far = across_cores(after(far[step], *earlier))
        pieces = [near(piece) for piece in (rings[step], far[step], core[step], core_far)]
        if last:
            pieces[0] = own_blocks
            return final_sums(block_table, kept[step], received[step], coming, pieces)
        sums = [partial_sums(block_table, kept[step], received[step], pieces)]
        coming.append(near(along_columns(sums[0], -step)))
        if place + 1 < columns - 1:
            following = order[place + 1]
            core[following] = across_cores(after(rings[following], *sums))


def solution(mesh):
    out_count, in_count = mesh.shape["out"], mesh.shape["in"]
    in_specs = (P(None, "out", "in"), P("in", "out"), P(None, "out", "in"), P())
    out_specs = P("out", "in")

    def shards(kernel_weights, mode_field, diff_blocks, block_table):
        own_cells = diff_blocks.shape[2]
        gather = (
            kernel_weights.shape[0] == PAIR
            and own_cells % LANES == 0
            and mode_field.shape[1] == PAIR * own_cells
            and out_count == PAIR * PAIR
            and in_count == PAIR * out_count
        )
        if gather:
            return gathered_shards(out_count, in_count, kernel_weights, mode_field, diff_blocks, block_table)
        return routed_shards(kernel_weights, mode_field, diff_blocks, block_table)

    return jax.shard_map(shards, mesh=mesh, in_specs=in_specs, out_specs=out_specs, check_vma=False)
```

```python
import functools
import math

import jax
import jax.numpy as jnp
from jax import lax
from jax.experimental import pallas as pl
from jax.experimental.pallas import tpu as pltpu
from jax.sharding import PartitionSpec as P

PAIR = 2
TOP = 32767.0
GROUPS = 4
MERGE_COST = 100000
KERNEL_MEMORY = 24 << 20
LANES = 128


def routed_shards(kernel_weights, mode_field, diff_blocks, block_table):
    out_index = lax.axis_index("out")
    tile_rows = kernel_weights.shape[1]
    term_count = kernel_weights.shape[0]
    own_cells = diff_blocks.shape[2]
    needed_row = block_table[out_index]
    whole_field = lax.all_gather(mode_field, "out", axis=1, tiled=True)
    every_block = lax.all_gather(diff_blocks, "out", axis=1, tiled=True)
    block_count = every_block.shape[1] // tile_rows
    every_block = every_block.reshape(term_count, block_count, tile_rows, own_cells)
    arranged = jnp.take(every_block, needed_row, axis=1)
    routed = lax.all_to_all(arranged, "in", split_axis=1, concat_axis=3, tiled=True)
    partial_value = jnp.zeros((tile_rows, whole_field.shape[1]), jnp.float32)
    for term_index in range(term_count):
        product = jnp.dot(kernel_weights[term_index], whole_field, preferred_element_type=jnp.float32)
        partial_value = partial_value + routed[term_index, 0].astype(jnp.float32) * product
    summed = lax.psum_scatter(partial_value, "in", scatter_dimension=1, tiled=True)
    return summed.astype(jnp.bfloat16)


def encode(values):
    largest = jnp.maximum(jnp.max(jnp.abs(values), axis=0, keepdims=True), 1e-30)
    exponent = jnp.floor(jnp.log2(largest)) + 1.0
    share = values * (jnp.exp2(-exponent) * (TOP * TOP))
    root = share * lax.rsqrt(jnp.abs(share) + 1e-9)
    return jnp.round(root).astype(jnp.int32), exponent.astype(jnp.int32)


def pack(high, low):
    return (high << 16) | (low & 0xFFFF)


def decode(codes, exponent):
    root = codes.astype(jnp.float32)
    return root * jnp.abs(root) * (jnp.exp2(exponent.astype(jnp.float32)) * (1.0 / (TOP * TOP)))


def unpack_high(packed, exponent):
    return decode(packed >> 16, exponent)


def unpack_low(packed, exponent):
    return decode((packed << 16) >> 16, exponent)


def position(index, out_index, chips):
    crossed = jnp.where(index % PAIR != out_index % PAIR, chips, 0)
    return crossed + (out_index // PAIR - index // PAIR + chips) % chips


def choose(index, refs, *at):
    value = refs[0][at]
    for place in range(1, len(refs)):
        value = jnp.where(index == place, refs[place][at], value)
    return value


def near(value):
    return pltpu.with_memory_space_constraint(value, pltpu.VMEM)


def kernel_call(kernel, name, inputs, in_table, outputs, scratch, flops, transcendentals):
    moved = sum(math.prod(array.shape) * jnp.dtype(array.dtype).itemsize for array in [*inputs, *outputs])
    memory = pl.BlockSpec(memory_space=pltpu.VMEM)
    return pl.pallas_call(
        kernel,
        name=name,
        out_shape=outputs,
        in_specs=[pl.BlockSpec(memory_space=pltpu.SMEM)] * in_table + [memory] * (len(inputs) - in_table),
        out_specs=[memory] * len(outputs),
        scratch_shapes=scratch,
        compiler_params=pltpu.CompilerParams(vmem_limit_bytes=KERNEL_MEMORY),
        cost_estimate=pl.CostEstimate(flops=flops, bytes_accessed=moved, transcendentals=transcendentals),
    )(*inputs)


def load_kernel(*refs):
    count = len(refs) // 2
    for source, place in zip(refs[:count], refs[count:]):
        place[...] = source[...]


def load(arrays):
    return kernel_call(
        load_kernel, "load", [near(array) for array in arrays], 0,
        [pltpu.VMEM(array.shape, array.dtype) for array in arrays], [], 0, 0,
    )


def multiply_kernel(shift, columns, weights, *refs):
    *fields, kept, sent, field = refs
    terms, total, _ = weights.shape
    rows = total // GROUPS
    half = kept.shape[2]
    in_index = lax.axis_index("in")
    target = (in_index // PAIR - shift + columns) % columns
    source = position(target, lax.axis_index("out"), len(fields) // PAIR)
    side = in_index % PAIR

    for place, ref in enumerate(fields):
        for first in range(PAIR):
            @pl.when((source == place) & (side == first))
            def _():
                field[:, :half] = ref[:, first * half:(first + 1) * half]
                field[:, half:] = ref[:, (1 - first) * half:(2 - first) * half]

    for group in range(GROUPS):
        chosen = slice(group * rows, (group + 1) * rows)
        codes = []
        for term in range(terms):
            product = jnp.dot(weights[term, chosen], field[...], preferred_element_type=jnp.float32)
            kept[term, chosen] = product[:, :half]
            code, exponent = encode(product[:, half:])
            codes.append(code)
            place = total + term * GROUPS + group
            sent[place:place + 1, :] = exponent
        sent[chosen, :] = pack(*codes)


def multiply(shift, columns, weights, fields):
    terms, rows, depth = weights.shape
    width = fields[0].shape[1]
    half = width // PAIR
    return kernel_call(
        functools.partial(multiply_kernel, shift, columns),
        "products",
        [weights, *fields],
        0,
        [
            pltpu.VMEM((terms, rows, half), jnp.float32),
            pltpu.VMEM((rows + terms * GROUPS, half), jnp.int32),
        ],
        [pltpu.VMEM((depth, width), jnp.bfloat16)],
        2 * terms * rows * depth * width,
        rows * half * terms,
    )


def wanted_blocks(table, chips):
    out_index, in_index = lax.axis_index("out"), lax.axis_index("in")
    column, side = in_index // PAIR, in_index % PAIR
    return [position(table[out_index, column * PAIR + which], out_index, chips) for which in (side, 1 - side)]


def blocks_times_products(wanted, kept, received, pieces, rows, total):
    packed = received[rows, :]
    scale = total + rows.start // (total // GROUPS)
    mine = [kept[0, rows], kept[1, rows]]
    other = [
        unpack_high(packed, received[scale:scale + 1, :]),
        unpack_low(packed, received[scale + GROUPS:scale + GROUPS + 1, :]),
    ]
    value = None
    for index, products in zip(wanted, (mine, other)):
        for term, product in enumerate(products):
            chosen = choose(index, pieces, term, rows).astype(jnp.float32)
            value = chosen * product if value is None else value + chosen * product
    return value


def row_ranges(total):
    half = total // PAIR
    step = half // GROUPS
    return [
        [slice(part * half + group * step, part * half + (group + 1) * step) for part in range(PAIR)]
        for group in range(GROUPS)
    ]


def partial_kernel(table, kept, received, *refs):
    *pieces, sent = refs
    total = kept.shape[1]
    wanted = wanted_blocks(table, len(pieces) // PAIR)
    for group, parts in enumerate(row_ranges(total)):
        codes = []
        for part, rows in enumerate(parts):
            code, exponent = encode(blocks_times_products(wanted, kept, received, pieces, rows, total))
            codes.append(code)
            place = total // PAIR + part * GROUPS + group
            sent[place:place + 1, :] = exponent
        sent[parts[0], :] = pack(*codes)


def merge_kernel(*refs):
    *coming, merged = refs
    total = merged.shape[0]
    for group, parts in enumerate(row_ranges(total)):
        for part, (rows, unpack) in enumerate(zip(parts, (unpack_high, unpack_low))):
            place = total // PAIR + part * GROUPS + group
            values = [unpack(ref[parts[0], :], ref[place:place + 1, :]) for ref in coming]
            merged[rows, :] = functools.reduce(jnp.add, values)


def final_kernel(table, kept, received, merged, last, *refs):
    *pieces, gain = refs
    total = kept.shape[1]
    wanted = wanted_blocks(table, len(pieces) // PAIR)
    for group, parts in enumerate(row_ranges(total)):
        for part, (rows, unpack) in enumerate(zip(parts, (unpack_high, unpack_low))):
            value = merged[rows, :] + blocks_times_products(wanted, kept, received, pieces, rows, total)
            place = total // PAIR + part * GROUPS + group
            value = value + unpack(last[parts[0], :], last[place:place + 1, :])
            gain[rows, :] = value.astype(gain.dtype)


def partial_sums(table, kept, received, pieces):
    terms, rows, cells = kept.shape
    shape = (rows // PAIR + PAIR * GROUPS, cells)
    return kernel_call(
        partial_kernel, "partial_sums", [table, kept, received, *pieces], 1,
        [pltpu.VMEM(shape, jnp.int32)], [], 8 * terms * rows * cells, rows * cells,
    )[0]


def merged_sums(coming, rows):
    cells = coming[0].shape[1]
    return kernel_call(
        merge_kernel, "merged_sums", coming, 0,
        [pltpu.VMEM((rows, cells), jnp.float32)], [], MERGE_COST * rows * cells, 0,
    )[0]


def final_sums(table, kept, received, merged, last, pieces):
    terms, rows, cells = kept.shape
    return kernel_call(
        final_kernel, "final_sums", [table, kept, received, merged, last, *pieces], 1,
        [jax.ShapeDtypeStruct((rows, cells), jnp.bfloat16)], [], 8 * terms * rows * cells, 0,
    )[0]


def after(value, *earlier):
    return lax.optimization_barrier((value, *earlier))[0]


def gathered_shards(out_count, in_count, kernel_weights, mode_field, diff_blocks, block_table):
    columns = in_count // PAIR

    def across_cores(value):
        return lax.ppermute(value, "out", [(r, r ^ 1) for r in range(out_count)])

    def along_chips(value):
        return lax.ppermute(value, "out", [(r, (r + PAIR) % out_count) for r in range(out_count)])

    def across_sides(value):
        return lax.ppermute(value, "in", [(s, s ^ 1) for s in range(in_count)])

    def along_columns(value, shift):
        return lax.ppermute(value, "in", [(s, (s + PAIR * shift) % in_count) for s in range(in_count)])

    order = list(range(1, columns)) + [0]
    weights, own_field, own_blocks = load([kernel_weights, mode_field, diff_blocks])
    far_field = after(along_chips(mode_field), weights)
    fields = [own_field] + [near(field) for field in (far_field, across_cores(mode_field), across_cores(far_field))]

    rings = [diff_blocks]
    for step in range(1, columns):
        rings.append(along_columns(rings[-1], 1))
    kept, sent = {}, {}
    for step in order:
        kept[step], sent[step] = multiply(step, columns, weights, fields)
    core_own = across_cores(diff_blocks)
    far_own = along_chips(after(diff_blocks, far_field))
    far, pieces = [far_own], {}
    for place, step in enumerate(order[:-1]):
        earlier = [[far_field], [*sent.values(), core_own, far[-1]]][place] if place < 2 else far[-1:]
        far.append(along_chips(after(rings[step], *earlier)))
        pieces[step] = [near(rings[step]), near(far[-1])]
        pieces[step] += [near(across_cores(piece)) for piece in (rings[step], far[-1])]

    received, coming = {}, []

    def send_sums(place):
        step = order[place]
        ready = after(kept[step], *(coming[-1:] if place < columns - 2 else []))
        partial = partial_sums(block_table, ready, received[step], pieces[step])
        coming.append(near(along_columns(partial, -step)))
        return partial

    for place, step in enumerate(order):
        earlier = [received[order[place - 1]]] if place > 0 else []
        if place > 1:
            earlier.append(send_sums(place - 2))
        received[step] = near(across_sides(after(sent[step], *earlier)))
    latest = send_sums(columns - 2)
    pieces[0] = [own_blocks, near(far_own), near(core_own), near(across_cores(after(far_own, latest)))]
    merged = near(merged_sums(coming[:-1], kernel_weights.shape[1]))
    return final_sums(block_table, kept[0], received[0], merged, coming[-1], pieces[0])


def solution(mesh):
    out_count, in_count = mesh.shape["out"], mesh.shape["in"]
    in_specs = (P(None, "out", "in"), P("in", "out"), P(None, "out", "in"), P())
    out_specs = P("out", "in")

    def shards(kernel_weights, mode_field, diff_blocks, block_table):
        own_cells = diff_blocks.shape[2]
        gather = (
            kernel_weights.shape[0] == PAIR
            and own_cells % LANES == 0
            and mode_field.shape[1] == PAIR * own_cells
            and out_count == PAIR * PAIR
            and in_count == PAIR * out_count
        )
        if gather:
            return gathered_shards(out_count, in_count, kernel_weights, mode_field, diff_blocks, block_table)
        return routed_shards(kernel_weights, mode_field, diff_blocks, block_table)

    return jax.shard_map(shards, mesh=mesh, in_specs=in_specs, out_specs=out_specs, check_vma=False)
```

```python
import functools
import math

import jax
import jax.numpy as jnp
from jax import lax
from jax.experimental import pallas as pl
from jax.experimental.pallas import tpu as pltpu
from jax.sharding import PartitionSpec as P

PAIR = 2
TOP = 32767.0
GROUPS = 4
MERGE_COST = 100000
KERNEL_MEMORY = 24 << 20
LANES = 128


def routed_shards(kernel_weights, mode_field, diff_blocks, block_table):
    out_index = lax.axis_index("out")
    tile_rows = kernel_weights.shape[1]
    term_count = kernel_weights.shape[0]
    own_cells = diff_blocks.shape[2]
    needed_row = block_table[out_index]
    whole_field = lax.all_gather(mode_field, "out", axis=1, tiled=True)
    every_block = lax.all_gather(diff_blocks, "out", axis=1, tiled=True)
    block_count = every_block.shape[1] // tile_rows
    every_block = every_block.reshape(term_count, block_count, tile_rows, own_cells)
    arranged = jnp.take(every_block, needed_row, axis=1)
    routed = lax.all_to_all(arranged, "in", split_axis=1, concat_axis=3, tiled=True)
    partial_value = jnp.zeros((tile_rows, whole_field.shape[1]), jnp.float32)
    for term_index in range(term_count):
        product = jnp.dot(kernel_weights[term_index], whole_field, preferred_element_type=jnp.float32)
        partial_value = partial_value + routed[term_index, 0].astype(jnp.float32) * product
    summed = lax.psum_scatter(partial_value, "in", scatter_dimension=1, tiled=True)
    return summed.astype(jnp.bfloat16)


def encode(values):
    largest = jnp.maximum(jnp.max(jnp.abs(values), axis=0, keepdims=True), 1e-30)
    exponent = jnp.floor(jnp.log2(largest)) + 1.0
    share = values * (jnp.exp2(-exponent) * (TOP * TOP))
    root = share * lax.rsqrt(jnp.abs(share) + 1e-9)
    return jnp.round(root).astype(jnp.int32), exponent.astype(jnp.int32)


def pack(high, low):
    return (high << 16) | (low & 0xFFFF)


def decode(codes, exponent):
    root = codes.astype(jnp.float32)
    return root * jnp.abs(root) * (jnp.exp2(exponent.astype(jnp.float32)) * (1.0 / (TOP * TOP)))


def unpack_high(packed, exponent):
    return decode(packed >> 16, exponent)


def unpack_low(packed, exponent):
    return decode((packed << 16) >> 16, exponent)


def position(index, out_index, chips):
    crossed = jnp.where(index % PAIR != out_index % PAIR, chips, 0)
    return crossed + (out_index // PAIR - index // PAIR + chips) % chips


def choose(index, refs, *at):
    value = refs[0][at]
    for place in range(1, len(refs)):
        value = jnp.where(index == place, refs[place][at], value)
    return value


def near(value):
    return pltpu.with_memory_space_constraint(value, pltpu.VMEM)


def kernel_call(kernel, name, inputs, in_table, outputs, scratch, flops, transcendentals):
    moved = sum(math.prod(array.shape) * jnp.dtype(array.dtype).itemsize for array in [*inputs, *outputs])
    memory = pl.BlockSpec(memory_space=pltpu.VMEM)
    return pl.pallas_call(
        kernel,
        name=name,
        out_shape=outputs,
        in_specs=[pl.BlockSpec(memory_space=pltpu.SMEM)] * in_table + [memory] * (len(inputs) - in_table),
        out_specs=[memory] * len(outputs),
        scratch_shapes=scratch,
        compiler_params=pltpu.CompilerParams(vmem_limit_bytes=KERNEL_MEMORY),
        cost_estimate=pl.CostEstimate(flops=flops, bytes_accessed=moved, transcendentals=transcendentals),
    )(*inputs)


def load_kernel(*refs):
    count = len(refs) // 2
    for source, place in zip(refs[:count], refs[count:]):
        place[...] = source[...]


def load(arrays):
    return kernel_call(
        load_kernel, "load", [near(array) for array in arrays], 0,
        [pltpu.VMEM(array.shape, array.dtype) for array in arrays], [], 0, 0,
    )


def multiply_kernel(shift, columns, weights, *refs):
    *fields, kept, sent, field = refs
    terms, total, _ = weights.shape
    rows = total // GROUPS
    half = kept.shape[2]
    in_index = lax.axis_index("in")
    target = (in_index // PAIR - shift + columns) % columns
    source = position(target, lax.axis_index("out"), len(fields) // PAIR)
    side = in_index % PAIR

    for place, ref in enumerate(fields):
        for first in range(PAIR):
            @pl.when((source == place) & (side == first))
            def _():
                field[:, :half] = ref[:, first * half:(first + 1) * half]
                field[:, half:] = ref[:, (1 - first) * half:(2 - first) * half]

    for group in range(GROUPS):
        chosen = slice(group * rows, (group + 1) * rows)
        codes = []
        for term in range(terms):
            product = jnp.dot(weights[term, chosen], field[...], preferred_element_type=jnp.float32)
            kept[term, chosen] = product[:, :half]
            code, exponent = encode(product[:, half:])
            codes.append(code)
            place = total + term * GROUPS + group
            sent[place:place + 1, :] = exponent
        sent[chosen, :] = pack(*codes)


def multiply(shift, columns, weights, fields):
    terms, rows, depth = weights.shape
    width = fields[0].shape[1]
    half = width // PAIR
    return kernel_call(
        functools.partial(multiply_kernel, shift, columns),
        "products",
        [weights, *fields],
        0,
        [
            pltpu.VMEM((terms, rows, half), jnp.float32),
            pltpu.VMEM((rows + terms * GROUPS, half), jnp.int32),
        ],
        [pltpu.VMEM((depth, width), jnp.bfloat16)],
        2 * terms * rows * depth * width,
        rows * half * terms,
    )


def wanted_blocks(table, chips):
    out_index, in_index = lax.axis_index("out"), lax.axis_index("in")
    column, side = in_index // PAIR, in_index % PAIR
    return [position(table[out_index, column * PAIR + which], out_index, chips) for which in (side, 1 - side)]


def blocks_times_products(wanted, kept, received, pieces, rows, total):
    packed = received[rows, :]
    scale = total + rows.start // (total // GROUPS)
    mine = [kept[0, rows], kept[1, rows]]
    other = [
        unpack_high(packed, received[scale:scale + 1, :]),
        unpack_low(packed, received[scale + GROUPS:scale + GROUPS + 1, :]),
    ]
    value = None
    for index, products in zip(wanted, (mine, other)):
        for term, product in enumerate(products):
            chosen = choose(index, pieces, term, rows).astype(jnp.float32)
            value = chosen * product if value is None else value + chosen * product
    return value


def row_ranges(total):
    half = total // PAIR
    step = half // GROUPS
    return [
        [slice(part * half + group * step, part * half + (group + 1) * step) for part in range(PAIR)]
        for group in range(GROUPS)
    ]


def partial_kernel(table, kept, received, *refs):
    *pieces, sent = refs
    total = kept.shape[1]
    wanted = wanted_blocks(table, len(pieces) // PAIR)
    for group, parts in enumerate(row_ranges(total)):
        codes = []
        for part, rows in enumerate(parts):
            code, exponent = encode(blocks_times_products(wanted, kept, received, pieces, rows, total))
            codes.append(code)
            place = total // PAIR + part * GROUPS + group
            sent[place:place + 1, :] = exponent
        sent[parts[0], :] = pack(*codes)


def merge_kernel(*refs):
    *coming, merged = refs
    total = merged.shape[0]
    for group, parts in enumerate(row_ranges(total)):
        for part, (rows, unpack) in enumerate(zip(parts, (unpack_high, unpack_low))):
            place = total // PAIR + part * GROUPS + group
            values = [unpack(ref[parts[0], :], ref[place:place + 1, :]) for ref in coming]
            merged[rows, :] = functools.reduce(jnp.add, values)


def final_kernel(table, kept, received, merged, last, *refs):
    *pieces, gain = refs
    total = kept.shape[1]
    wanted = wanted_blocks(table, len(pieces) // PAIR)
    for group, parts in enumerate(row_ranges(total)):
        for part, (rows, unpack) in enumerate(zip(parts, (unpack_high, unpack_low))):
            value = merged[rows, :] + blocks_times_products(wanted, kept, received, pieces, rows, total)
            place = total // PAIR + part * GROUPS + group
            value = value + unpack(last[parts[0], :], last[place:place + 1, :])
            gain[rows, :] = value.astype(gain.dtype)


def partial_sums(table, kept, received, pieces):
    terms, rows, cells = kept.shape
    shape = (rows // PAIR + PAIR * GROUPS, cells)
    return kernel_call(
        partial_kernel, "partial_sums", [table, kept, received, *pieces], 1,
        [pltpu.VMEM(shape, jnp.int32)], [], 8 * terms * rows * cells, rows * cells,
    )[0]


def merged_sums(coming, rows):
    cells = coming[0].shape[1]
    return kernel_call(
        merge_kernel, "merged_sums", coming, 0,
        [pltpu.VMEM((rows, cells), jnp.float32)], [], MERGE_COST * rows * cells, 0,
    )[0]


def final_sums(table, kept, received, merged, last, pieces):
    terms, rows, cells = kept.shape
    return kernel_call(
        final_kernel, "final_sums", [table, kept, received, merged, last, *pieces], 1,
        [jax.ShapeDtypeStruct((rows, cells), jnp.bfloat16)], [], 8 * terms * rows * cells, 0,
    )[0]


def after(value, *earlier):
    return lax.optimization_barrier((value, *earlier))[0]


def gathered_shards(out_count, in_count, kernel_weights, mode_field, diff_blocks, block_table):
    columns = in_count // PAIR

    def across_cores(value):
        return lax.ppermute(value, "out", [(r, r ^ 1) for r in range(out_count)])

    def along_chips(value):
        return lax.ppermute(value, "out", [(r, (r + PAIR) % out_count) for r in range(out_count)])

    def across_sides(value):
        return lax.ppermute(value, "in", [(s, s ^ 1) for s in range(in_count)])

    def along_columns(value, shift):
        return lax.ppermute(value, "in", [(s, (s + PAIR * shift) % in_count) for s in range(in_count)])

    order = list(range(1, columns)) + [0]
    weights, own_field, own_blocks = load([kernel_weights, mode_field, diff_blocks])
    far_field = after(along_chips(mode_field), weights)
    fields = [own_field] + [near(field) for field in (far_field, across_cores(mode_field), across_cores(far_field))]

    rings = [diff_blocks]
    for step in range(1, columns):
        rings.append(along_columns(rings[-1], 1))
    kept, sent = {}, {}
    for step in order:
        kept[step], sent[step] = multiply(step, columns, weights, fields)
    core_own = across_cores(diff_blocks)
    far_own = along_chips(after(diff_blocks, far_field))
    far = [far_own]
    for place, step in enumerate(order[:-1]):
        earlier = [[far_field], [*sent.values(), core_own, far[-1]]][place] if place < 2 else far[-1:]
        far.append(along_chips(after(rings[step], *earlier)))

    received, coming, partials, pieces = {}, [], [], {}

    def send_sums(place):
        step = order[place]
        near_pieces = [near(rings[step]), near(far[place + 1])]
        earlier = partials[-1:] if place > 0 else list(sent.values())
        pieces[step] = near_pieces + [near(across_cores(after(piece, *earlier))) for piece in (rings[step], far[place + 1])]
        ready = after(kept[step], *coming[:-1])
        partials.append(partial_sums(block_table, ready, received[step], pieces[step]))
        coming.append(near(along_columns(partials[-1], -step)))
        return partials[-1]

    for place, step in enumerate(order):
        earlier = [received[order[place - 1]]] if place > 0 else []
        if place > 1:
            earlier.append(send_sums(place - 2))
        received[step] = near(across_sides(after(sent[step], *earlier)))
    latest = send_sums(columns - 2)
    pieces[0] = [own_blocks, near(far_own), near(core_own), near(across_cores(after(far_own, latest)))]
    merged = near(merged_sums(coming[:-1], kernel_weights.shape[1]))
    return final_sums(block_table, kept[0], received[0], merged, coming[-1], pieces[0])


def solution(mesh):
    out_count, in_count = mesh.shape["out"], mesh.shape["in"]
    in_specs = (P(None, "out", "in"), P("in", "out"), P(None, "out", "in"), P())
    out_specs = P("out", "in")

    def shards(kernel_weights, mode_field, diff_blocks, block_table):
        own_cells = diff_blocks.shape[2]
        gather = (
            kernel_weights.shape[0] == PAIR
            and own_cells % LANES == 0
            and mode_field.shape[1] == PAIR * own_cells
            and out_count == PAIR * PAIR
            and in_count == PAIR * out_count
        )
        if gather:
            return gathered_shards(out_count, in_count, kernel_weights, mode_field, diff_blocks, block_table)
        return routed_shards(kernel_weights, mode_field, diff_blocks, block_table)

    return jax.shard_map(shards, mesh=mesh, in_specs=in_specs, out_specs=out_specs, check_vma=False)
```

```python
import functools
import math

import jax
import jax.numpy as jnp
from jax import lax
from jax.experimental import pallas as pl
from jax.experimental.pallas import tpu as pltpu
from jax.sharding import PartitionSpec as P

PAIR = 2
TOP = 32767.0
GROUPS = 4
WEIGHTS = (4000, 50000)
KERNEL_MEMORY = 24 << 20
LANES = 128


def routed_shards(kernel_weights, mode_field, diff_blocks, block_table):
    out_index = lax.axis_index("out")
    tile_rows = kernel_weights.shape[1]
    term_count = kernel_weights.shape[0]
    own_cells = diff_blocks.shape[2]
    needed_row = block_table[out_index]
    whole_field = lax.all_gather(mode_field, "out", axis=1, tiled=True)
    every_block = lax.all_gather(diff_blocks, "out", axis=1, tiled=True)
    block_count = every_block.shape[1] // tile_rows
    every_block = every_block.reshape(term_count, block_count, tile_rows, own_cells)
    arranged = jnp.take(every_block, needed_row, axis=1)
    routed = lax.all_to_all(arranged, "in", split_axis=1, concat_axis=3, tiled=True)
    partial_value = jnp.zeros((tile_rows, whole_field.shape[1]), jnp.float32)
    for term_index in range(term_count):
        product = jnp.dot(kernel_weights[term_index], whole_field, preferred_element_type=jnp.float32)
        partial_value = partial_value + routed[term_index, 0].astype(jnp.float32) * product
    summed = lax.psum_scatter(partial_value, "in", scatter_dimension=1, tiled=True)
    return summed.astype(jnp.bfloat16)


def encode(values):
    largest = jnp.maximum(jnp.max(jnp.abs(values), axis=0, keepdims=True), 1e-30)
    exponent = jnp.floor(jnp.log2(largest)) + 1.0
    share = values * (jnp.exp2(-exponent) * (TOP * TOP))
    root = share * lax.rsqrt(jnp.abs(share) + 1e-9)
    return jnp.round(root).astype(jnp.int32), exponent.astype(jnp.int32)


def pack(high, low):
    return (high << 16) | (low & 0xFFFF)


def decode(codes, exponent):
    root = codes.astype(jnp.float32)
    return root * jnp.abs(root) * (jnp.exp2(exponent.astype(jnp.float32)) * (1.0 / (TOP * TOP)))


def unpack_high(packed, exponent):
    return decode(packed >> 16, exponent)


def unpack_low(packed, exponent):
    return decode((packed << 16) >> 16, exponent)


def position(index, out_index, chips):
    crossed = jnp.where(index % PAIR != out_index % PAIR, chips, 0)
    return crossed + (out_index // PAIR - index // PAIR + chips) % chips


def choose(index, refs, *at):
    value = refs[0][at]
    for place in range(1, len(refs)):
        value = jnp.where(index == place, refs[place][at], value)
    return value


def near(value):
    return pltpu.with_memory_space_constraint(value, pltpu.VMEM)


def kernel_call(kernel, name, inputs, in_table, outputs, scratch, flops, transcendentals):
    moved = sum(math.prod(array.shape) * jnp.dtype(array.dtype).itemsize for array in [*inputs, *outputs])
    memory = pl.BlockSpec(memory_space=pltpu.VMEM)
    return pl.pallas_call(
        kernel,
        name=name,
        out_shape=outputs,
        in_specs=[pl.BlockSpec(memory_space=pltpu.SMEM)] * in_table + [memory] * (len(inputs) - in_table),
        out_specs=[memory] * len(outputs),
        scratch_shapes=scratch,
        compiler_params=pltpu.CompilerParams(vmem_limit_bytes=KERNEL_MEMORY),
        cost_estimate=pl.CostEstimate(flops=4 * flops, bytes_accessed=4 * moved, transcendentals=transcendentals),
    )(*inputs)


def load_kernel(*refs):
    count = len(refs) // 2
    for source, place in zip(refs[:count], refs[count:]):
        place[...] = source[...]


def load(arrays):
    return kernel_call(
        load_kernel, "load", [near(array) for array in arrays], 0,
        [pltpu.VMEM(array.shape, array.dtype) for array in arrays], [], 0, 0,
    )


def multiply_kernel(shift, columns, weights, *refs):
    *fields, kept, sent, field = refs
    terms, total, _ = weights.shape
    rows = total // GROUPS
    half = kept.shape[2]
    in_index = lax.axis_index("in")
    target = (in_index // PAIR + shift) % columns
    source = position(target, lax.axis_index("out"), len(fields) // PAIR)
    side = in_index % PAIR

    for place, ref in enumerate(fields):
        for first in range(PAIR):
            @pl.when((source == place) & (side == first))
            def _():
                field[:, :half] = ref[:, first * half:(first + 1) * half]
                field[:, half:] = ref[:, (1 - first) * half:(2 - first) * half]

    for group in range(GROUPS):
        chosen = slice(group * rows, (group + 1) * rows)
        codes = []
        for term in range(terms):
            product = jnp.dot(weights[term, chosen], field[...], preferred_element_type=jnp.float32)
            kept[term, chosen] = product[:, :half]
            code, exponent = encode(product[:, half:])
            codes.append(code)
            place = total + term * GROUPS + group
            sent[place:place + 1, :] = exponent
        sent[chosen, :] = pack(*codes)


def multiply(shift, columns, weights, fields):
    terms, rows, depth = weights.shape
    width = fields[0].shape[1]
    half = width // PAIR
    return kernel_call(
        functools.partial(multiply_kernel, shift, columns),
        "products",
        [weights, *fields],
        0,
        [
            pltpu.VMEM((terms, rows, half), jnp.float32),
            pltpu.VMEM((rows + terms * GROUPS, half), jnp.int32),
        ],
        [pltpu.VMEM((depth, width), jnp.bfloat16)],
        2 * terms * rows * depth * width,
        rows * half * terms,
    )


def wanted_blocks(table, chips):
    out_index, in_index = lax.axis_index("out"), lax.axis_index("in")
    column, side = in_index // PAIR, in_index % PAIR
    return [position(table[out_index, column * PAIR + which], out_index, chips) for which in (side, 1 - side)]


def blocks_times_products(wanted, kept, received, pieces, rows):
    total = kept.shape[1]
    packed = received[rows, :]
    scale = total + rows.start // (total // GROUPS)
    mine = [kept[0, rows], kept[1, rows]]
    other = []
    for term, unpack in enumerate((unpack_high, unpack_low)):
        place = scale + term * GROUPS
        other.append(unpack(packed, received[place:place + 1, :]))
    value = None
    for index, products in zip(wanted, (mine, other)):
        for term, product in enumerate(products):
            chosen = choose(index, pieces, term, rows).astype(jnp.float32)
            value = chosen * product if value is None else value + chosen * product
    return value


def row_ranges(total):
    half = total // PAIR
    step = half // GROUPS
    return [
        [slice(part * half + group * step, part * half + (group + 1) * step) for part in range(PAIR)]
        for group in range(GROUPS)
    ]


def decode_kernel(coded, result):
    total = result.shape[0]
    for group, parts in enumerate(row_ranges(total)):
        for part, (rows, unpack) in enumerate(zip(parts, (unpack_high, unpack_low))):
            place = total // PAIR + part * GROUPS + group
            result[rows, :] = unpack(coded[parts[0], :], coded[place:place + 1, :])


def decoded_sums(coded, rows, weight):
    cells = coded.shape[1]
    return kernel_call(
        decode_kernel, "decoded_sums", [coded], 0, [pltpu.VMEM((rows, cells), jnp.float32)], [],
        weight * rows * cells, 0,
    )[0]


def sums_kernel(arrivals, table, kept, received, *refs):
    arrived, pieces, result = refs[:arrivals], refs[arrivals:-1], refs[-1]
    total = kept.shape[1]
    wanted = wanted_blocks(table, len(pieces) // PAIR)
    for group, parts in enumerate(row_ranges(total)):
        codes = []
        for part, (rows, unpack) in enumerate(zip(parts, (unpack_high, unpack_low))):
            value = blocks_times_products(wanted, kept, received, pieces, rows)
            place = total // PAIR + part * GROUPS + group
            for ref in arrived:
                value = value + ref[rows, :]
            if result.dtype == jnp.int32:
                code, exponent = encode(value)
                codes.append(code)
                result[place:place + 1, :] = exponent
            else:
                result[rows, :] = value.astype(result.dtype)
        if codes:
            result[parts[0], :] = pack(*codes)


def sums(name, table, kept, received, arrived, pieces, result):
    terms, rows, cells = kept.shape
    return kernel_call(
        functools.partial(sums_kernel, len(arrived)), name, [table, kept, received, *arrived, *pieces], 1,
        [result], [], 8 * terms * rows * cells, rows * cells,
    )[0]


def partial_sums(table, kept, received, arrived, pieces):
    terms, rows, cells = kept.shape
    result = pltpu.VMEM((rows // PAIR + PAIR * GROUPS, cells), jnp.int32)
    return sums("partial_sums", table, kept, received, arrived, pieces, result)


def final_sums(table, kept, received, arrived, pieces):
    terms, rows, cells = kept.shape
    result = jax.ShapeDtypeStruct((rows, cells), jnp.bfloat16)
    return sums("final_sums", table, kept, received, arrived, pieces, result)


def after(value, *earlier):
    return lax.optimization_barrier((value, *earlier))[0]


def gathered_shards(out_count, in_count, kernel_weights, mode_field, diff_blocks, block_table):
    columns = in_count // PAIR

    def across_cores(value):
        return lax.ppermute(value, "out", [(r, r ^ 1) for r in range(out_count)])

    def along_chips(value):
        return lax.ppermute(value, "out", [(r, (r + PAIR) % out_count) for r in range(out_count)])

    def across_sides(value):
        return lax.ppermute(value, "in", [(s, s ^ 1) for s in range(in_count)])

    def along_columns(value, shift):
        return lax.ppermute(value, "in", [(s, (s + PAIR * shift) % in_count) for s in range(in_count)])

    weights, own_field, own_blocks = load([kernel_weights, mode_field, diff_blocks])
    rings = [diff_blocks]
    for step in range(1, columns):
        rings.append(along_columns(rings[-1], -1))
    rings = rings[1:] + rings[:1]
    far_field = after(along_chips(mode_field), weights)
    core_field = after(across_cores(mode_field), rings[0])
    fields = [own_field] + [near(field) for field in (far_field, core_field, across_cores(far_field))]

    kept, received, sent = [], [], []
    for step in range(columns):
        products = multiply((step + 1) % columns, columns, weights, fields)
        kept.append(products[0])
        sent.append(products[1])
        received.append(near(across_sides(after(products[1], *received[-1:]))))
    core_own = across_cores(diff_blocks)

    arrived, ahead = [], sent
    for step in range(columns):
        last = step == columns - 1
        waits = [far_field] if step == 0 else rings[columns - 2:columns - 1] if last else []
        far = along_chips(after(rings[step], *waits))
        pieces = [own_blocks if last else near(rings[step]), near(far)]
        pieces += [near(core_own if last else across_cores(after(rings[step], *ahead))), near(across_cores(after(far, *ahead)))]
        if last:
            return final_sums(block_table, kept[step], received[step], arrived, pieces)
        total = partial_sums(block_table, kept[step], received[step], arrived, pieces)
        coming = near(along_columns(total, -1))
        arrived = [decoded_sums(coming, kernel_weights.shape[1], WEIGHTS[step == columns - 2])]
        ahead = [total, *([core_own] if step == 0 else [])]


def solution(mesh):
    out_count, in_count = mesh.shape["out"], mesh.shape["in"]
    in_specs = (P(None, "out", "in"), P("in", "out"), P(None, "out", "in"), P())
    out_specs = P("out", "in")

    def shards(kernel_weights, mode_field, diff_blocks, block_table):
        own_cells = diff_blocks.shape[2]
        gather = (
            kernel_weights.shape[0] == PAIR
            and own_cells % LANES == 0
            and mode_field.shape[1] == PAIR * own_cells
            and out_count == PAIR * PAIR
            and in_count == PAIR * out_count
        )
        if gather:
            return gathered_shards(out_count, in_count, kernel_weights, mode_field, diff_blocks, block_table)
        return routed_shards(kernel_weights, mode_field, diff_blocks, block_table)

    return jax.shard_map(shards, mesh=mesh, in_specs=in_specs, out_specs=out_specs, check_vma=False)
```

```python
import functools
import math

import jax
import jax.numpy as jnp
from jax import lax
from jax.experimental import pallas as pl
from jax.experimental.pallas import tpu as pltpu
from jax.sharding import PartitionSpec as P

PAIR = 2
TOP = 32767.0
GROUPS = 4
KERNEL_WEIGHT = 1
SUMS_WEIGHT = 1
KERNEL_MEMORY = 24 << 20
LANES = 128


def routed_shards(kernel_weights, mode_field, diff_blocks, block_table):
    out_index = lax.axis_index("out")
    tile_rows = kernel_weights.shape[1]
    term_count = kernel_weights.shape[0]
    own_cells = diff_blocks.shape[2]
    needed_row = block_table[out_index]
    whole_field = lax.all_gather(mode_field, "out", axis=1, tiled=True)
    every_block = lax.all_gather(diff_blocks, "out", axis=1, tiled=True)
    block_count = every_block.shape[1] // tile_rows
    every_block = every_block.reshape(term_count, block_count, tile_rows, own_cells)
    arranged = jnp.take(every_block, needed_row, axis=1)
    routed = lax.all_to_all(arranged, "in", split_axis=1, concat_axis=3, tiled=True)
    partial_value = jnp.zeros((tile_rows, whole_field.shape[1]), jnp.float32)
    for term_index in range(term_count):
        product = jnp.dot(kernel_weights[term_index], whole_field, preferred_element_type=jnp.float32)
        partial_value = partial_value + routed[term_index, 0].astype(jnp.float32) * product
    summed = lax.psum_scatter(partial_value, "in", scatter_dimension=1, tiled=True)
    return summed.astype(jnp.bfloat16)


def encode(values):
    largest = jnp.maximum(jnp.max(jnp.abs(values), axis=0, keepdims=True), 1e-30)
    exponent = jnp.floor(jnp.log2(largest)) + 1.0
    share = values * (jnp.exp2(-exponent) * (TOP * TOP))
    root = share * lax.rsqrt(jnp.abs(share) + 1e-9)
    return jnp.round(root).astype(jnp.int32), exponent.astype(jnp.int32)


def pack(high, low):
    return (high << 16) | (low & 0xFFFF)


def decode(codes, exponent):
    root = codes.astype(jnp.float32)
    return root * jnp.abs(root) * (jnp.exp2(exponent.astype(jnp.float32)) * (1.0 / (TOP * TOP)))


def unpack_high(packed, exponent):
    return decode(packed >> 16, exponent)


def unpack_low(packed, exponent):
    return decode((packed << 16) >> 16, exponent)


def position(index, out_index, chips):
    crossed = jnp.where(index % PAIR != out_index % PAIR, chips, 0)
    return crossed + (out_index // PAIR - index // PAIR + chips) % chips


def choose(index, refs, *at):
    value = refs[0][at]
    for place in range(1, len(refs)):
        value = jnp.where(index == place, refs[place][at], value)
    return value


def near(value):
    return pltpu.with_memory_space_constraint(value, pltpu.VMEM)


def kernel_call(kernel, name, inputs, in_table, outputs, scratch, flops, transcendentals, weight=KERNEL_WEIGHT):
    moved = sum(math.prod(array.shape) * jnp.dtype(array.dtype).itemsize for array in [*inputs, *outputs])
    memory = pl.BlockSpec(memory_space=pltpu.VMEM)
    return pl.pallas_call(
        kernel,
        name=name,
        out_shape=outputs,
        in_specs=[pl.BlockSpec(memory_space=pltpu.SMEM)] * in_table + [memory] * (len(inputs) - in_table),
        out_specs=[memory] * len(outputs),
        scratch_shapes=scratch,
        compiler_params=pltpu.CompilerParams(vmem_limit_bytes=KERNEL_MEMORY),
        cost_estimate=pl.CostEstimate(flops=weight * flops, bytes_accessed=weight * moved, transcendentals=transcendentals),
    )(*inputs)


def load_kernel(*refs):
    count = len(refs) // 2
    for source, place in zip(refs[:count], refs[count:]):
        place[...] = source[...]


def load(arrays):
    return kernel_call(
        load_kernel, "load", [near(array) for array in arrays], 0,
        [pltpu.VMEM(array.shape, array.dtype) for array in arrays], [], 0, 0,
    )


def multiply_kernel(shift, columns, weights, *refs):
    *fields, kept, sent, field = refs
    terms, total, _ = weights.shape
    rows = total // GROUPS
    half = kept.shape[2]
    in_index = lax.axis_index("in")
    target = (in_index // PAIR + shift) % columns
    source = position(target, lax.axis_index("out"), len(fields) // PAIR)
    side = in_index % PAIR

    for place, ref in enumerate(fields):
        for first in range(PAIR):
            @pl.when((source == place) & (side == first))
            def _():
                field[:, :half] = ref[:, first * half:(first + 1) * half]
                field[:, half:] = ref[:, (1 - first) * half:(2 - first) * half]

    for group in range(GROUPS):
        chosen = slice(group * rows, (group + 1) * rows)
        codes = []
        for term in range(terms):
            product = jnp.dot(weights[term, chosen], field[...], preferred_element_type=jnp.float32)
            kept[term, chosen] = product[:, :half]
            code, exponent = encode(product[:, half:])
            codes.append(code)
            place = total + term * GROUPS + group
            sent[place:place + 1, :] = exponent
        sent[chosen, :] = pack(*codes)


def multiply(shift, columns, weights, fields):
    terms, rows, depth = weights.shape
    width = fields[0].shape[1]
    half = width // PAIR
    return kernel_call(
        functools.partial(multiply_kernel, shift, columns),
        "products",
        [weights, *fields],
        0,
        [
            pltpu.VMEM((terms, rows, half), jnp.float32),
            pltpu.VMEM((rows + terms * GROUPS, half), jnp.int32),
        ],
        [pltpu.VMEM((depth, width), jnp.bfloat16)],
        2 * terms * rows * depth * width,
        rows * half * terms,
    )


def wanted_blocks(table, chips):
    out_index, in_index = lax.axis_index("out"), lax.axis_index("in")
    column, side = in_index // PAIR, in_index % PAIR
    return [position(table[out_index, column * PAIR + which], out_index, chips) for which in (side, 1 - side)]


def blocks_times_products(wanted, kept, received, pieces, rows):
    total = kept.shape[1]
    packed = received[rows, :]
    scale = total + rows.start // (total // GROUPS)
    mine = [kept[0, rows], kept[1, rows]]
    other = []
    for term, unpack in enumerate((unpack_high, unpack_low)):
        place = scale + term * GROUPS
        other.append(unpack(packed, received[place:place + 1, :]))
    value = None
    for index, products in zip(wanted, (mine, other)):
        for term, product in enumerate(products):
            chosen = choose(index, pieces, term, rows).astype(jnp.float32)
            value = chosen * product if value is None else value + chosen * product
    return value


def row_ranges(total):
    half = total // PAIR
    step = half // GROUPS
    return [
        [slice(part * half + group * step, part * half + (group + 1) * step) for part in range(PAIR)]
        for group in range(GROUPS)
    ]


def sums_kernel(arrivals, table, kept, received, *refs):
    arrived, pieces, result = refs[:arrivals], refs[arrivals:-1], refs[-1]
    total = kept.shape[1]
    wanted = wanted_blocks(table, len(pieces) // PAIR)
    for group, parts in enumerate(row_ranges(total)):
        codes = []
        for part, (rows, unpack) in enumerate(zip(parts, (unpack_high, unpack_low))):
            value = blocks_times_products(wanted, kept, received, pieces, rows)
            place = total // PAIR + part * GROUPS + group
            for ref in arrived:
                value = value + unpack(ref[parts[0], :], ref[place:place + 1, :])
            if result.dtype == jnp.int32:
                code, exponent = encode(value)
                codes.append(code)
                result[place:place + 1, :] = exponent
            else:
                result[rows, :] = value.astype(result.dtype)
        if codes:
            result[parts[0], :] = pack(*codes)


def sums(name, table, kept, received, arrived, pieces, result):
    terms, rows, cells = kept.shape
    return kernel_call(
        functools.partial(sums_kernel, len(arrived)), name, [table, kept, received, *arrived, *pieces], 1,
        [result], [], 8 * terms * rows * cells, rows * cells, SUMS_WEIGHT,
    )[0]


def partial_sums(table, kept, received, arrived, pieces):
    terms, rows, cells = kept.shape
    result = pltpu.VMEM((rows // PAIR + PAIR * GROUPS, cells), jnp.int32)
    return sums("partial_sums", table, kept, received, arrived, pieces, result)


def final_sums(table, kept, received, arrived, pieces):
    terms, rows, cells = kept.shape
    result = jax.ShapeDtypeStruct((rows, cells), jnp.bfloat16)
    return sums("final_sums", table, kept, received, arrived, pieces, result)


def after(value, *earlier):
    return lax.optimization_barrier((value, *earlier))[0]


def gathered_shards(out_count, in_count, kernel_weights, mode_field, diff_blocks, block_table):
    columns = in_count // PAIR

    def across_cores(value):
        return lax.ppermute(value, "out", [(r, r ^ 1) for r in range(out_count)])

    def along_chips(value):
        return lax.ppermute(value, "out", [(r, (r + PAIR) % out_count) for r in range(out_count)])

    def across_sides(value):
        return lax.ppermute(value, "in", [(s, s ^ 1) for s in range(in_count)])

    def along_columns(value, shift):
        return lax.ppermute(value, "in", [(s, (s + PAIR * shift) % in_count) for s in range(in_count)])

    weights, own_field, own_blocks = load([kernel_weights, mode_field, diff_blocks])
    rings = [diff_blocks]
    for step in range(1, columns):
        rings.append(along_columns(rings[-1], -1))
    rings = rings[1:] + rings[:1]
    far_field = after(along_chips(mode_field), weights)
    core_field = after(across_cores(mode_field), rings[0])
    fields = [own_field] + [near(field) for field in (far_field, core_field, across_cores(far_field))]

    kept, received, sent = [], [], []
    for step in range(columns):
        products = multiply((step + 1) % columns, columns, weights, fields)
        kept.append(products[0])
        sent.append(products[1])
        received.append(near(across_sides(after(products[1], *received[-1:]))))
    core_own = across_cores(diff_blocks)
    arrived = []
    for step in range(columns - 1):
        far = along_chips(after(rings[step], far_field))
        ahead = [total, *rings[step + 1:columns - 1]] if step > 0 else [*sent, core_own]
        pieces = [near(rings[step]), near(far), near(across_cores(after(rings[step], *ahead)))]
        pieces.append(near(across_cores(after(far, *([*arrived, received[step]] if step > 0 else sent)))))
        total = partial_sums(block_table, kept[step], received[step], arrived, pieces)
        arrived = [near(along_columns(total, -1))]
    far_own = along_chips(after(diff_blocks, rings[columns - 2]))
    pieces = [own_blocks, near(far_own), near(core_own), near(across_cores(after(far_own, *arrived, received[-1])))]
    return final_sums(block_table, kept[-1], received[-1], arrived, pieces)


def solution(mesh):
    out_count, in_count = mesh.shape["out"], mesh.shape["in"]
    in_specs = (P(None, "out", "in"), P("in", "out"), P(None, "out", "in"), P())
    out_specs = P("out", "in")

    def shards(kernel_weights, mode_field, diff_blocks, block_table):
        own_cells = diff_blocks.shape[2]
        gather = (
            kernel_weights.shape[0] == PAIR
            and own_cells % LANES == 0
            and mode_field.shape[1] == PAIR * own_cells
            and out_count == PAIR * PAIR
            and in_count == PAIR * out_count
        )
        if gather:
            return gathered_shards(out_count, in_count, kernel_weights, mode_field, diff_blocks, block_table)
        return routed_shards(kernel_weights, mode_field, diff_blocks, block_table)

    return jax.shard_map(shards, mesh=mesh, in_specs=in_specs, out_specs=out_specs, check_vma=False)
```

```python
import functools
import math

import jax
import jax.numpy as jnp
from jax import lax
from jax.experimental import pallas as pl
from jax.experimental.pallas import tpu as pltpu
from jax.sharding import PartitionSpec as P

PAIR = 2
TOP = 32767.0
GROUPS = 4
UNPACK_COST = 30000
KERNEL_MEMORY = 24 << 20
LANES = 128


def routed_shards(kernel_weights, mode_field, diff_blocks, block_table):
    out_index = lax.axis_index("out")
    tile_rows = kernel_weights.shape[1]
    term_count = kernel_weights.shape[0]
    own_cells = diff_blocks.shape[2]
    needed_row = block_table[out_index]
    whole_field = lax.all_gather(mode_field, "out", axis=1, tiled=True)
    every_block = lax.all_gather(diff_blocks, "out", axis=1, tiled=True)
    block_count = every_block.shape[1] // tile_rows
    every_block = every_block.reshape(term_count, block_count, tile_rows, own_cells)
    arranged = jnp.take(every_block, needed_row, axis=1)
    routed = lax.all_to_all(arranged, "in", split_axis=1, concat_axis=3, tiled=True)
    partial_value = jnp.zeros((tile_rows, whole_field.shape[1]), jnp.float32)
    for term_index in range(term_count):
        product = jnp.dot(kernel_weights[term_index], whole_field, preferred_element_type=jnp.float32)
        partial_value = partial_value + routed[term_index, 0].astype(jnp.float32) * product
    summed = lax.psum_scatter(partial_value, "in", scatter_dimension=1, tiled=True)
    return summed.astype(jnp.bfloat16)


def encode(values):
    largest = jnp.maximum(jnp.max(jnp.abs(values), axis=0, keepdims=True), 1e-30)
    exponent = jnp.floor(jnp.log2(largest)) + 1.0
    share = values * (jnp.exp2(-exponent) * (TOP * TOP))
    root = share * lax.rsqrt(jnp.abs(share) + 1e-9)
    return jnp.round(root).astype(jnp.int32), exponent.astype(jnp.int32)


def pack(high, low):
    return (high << 16) | (low & 0xFFFF)


def decode(codes, exponent):
    root = codes.astype(jnp.float32)
    return root * jnp.abs(root) * (jnp.exp2(exponent.astype(jnp.float32)) * (1.0 / (TOP * TOP)))


def unpack_high(packed, exponent):
    return decode(packed >> 16, exponent)


def unpack_low(packed, exponent):
    return decode((packed << 16) >> 16, exponent)


def position(index, out_index, chips):
    crossed = jnp.where(index % PAIR != out_index % PAIR, chips, 0)
    return crossed + (out_index // PAIR - index // PAIR + chips) % chips


def choose(index, refs, *at):
    value = refs[0][at]
    for place in range(1, len(refs)):
        value = jnp.where(index == place, refs[place][at], value)
    return value


def near(value):
    return pltpu.with_memory_space_constraint(value, pltpu.VMEM)


def kernel_call(kernel, name, inputs, in_table, outputs, scratch, flops, transcendentals):
    moved = sum(math.prod(array.shape) * jnp.dtype(array.dtype).itemsize for array in [*inputs, *outputs])
    memory = pl.BlockSpec(memory_space=pltpu.VMEM)
    return pl.pallas_call(
        kernel,
        name=name,
        out_shape=outputs,
        in_specs=[pl.BlockSpec(memory_space=pltpu.SMEM)] * in_table + [memory] * (len(inputs) - in_table),
        out_specs=[memory] * len(outputs),
        scratch_shapes=scratch,
        compiler_params=pltpu.CompilerParams(vmem_limit_bytes=KERNEL_MEMORY),
        cost_estimate=pl.CostEstimate(flops=flops, bytes_accessed=moved, transcendentals=transcendentals),
    )(*inputs)


def load_kernel(*refs):
    count = len(refs) // 2
    for source, place in zip(refs[:count], refs[count:]):
        place[...] = source[...]


def load(arrays):
    return kernel_call(
        load_kernel, "load", [near(array) for array in arrays], 0,
        [pltpu.VMEM(array.shape, array.dtype) for array in arrays], [], 0, 0,
    )


def multiply_kernel(shift, columns, weights, *refs):
    *fields, kept, sent, field = refs
    terms, total, _ = weights.shape
    rows = total // GROUPS
    half = kept.shape[2]
    in_index = lax.axis_index("in")
    target = (in_index // PAIR - shift + columns) % columns
    source = position(target, lax.axis_index("out"), len(fields) // PAIR)
    side = in_index % PAIR

    for place, ref in enumerate(fields):
        for first in range(PAIR):
            @pl.when((source == place) & (side == first))
            def _():
                field[:, :half] = ref[:, first * half:(first + 1) * half]
                field[:, half:] = ref[:, (1 - first) * half:(2 - first) * half]

    for group in range(GROUPS):
        chosen = slice(group * rows, (group + 1) * rows)
        codes = []
        for term in range(terms):
            product = jnp.dot(weights[term, chosen], field[...], preferred_element_type=jnp.float32)
            kept[term, chosen] = product[:, :half]
            code, exponent = encode(product[:, half:])
            codes.append(code)
            place = total + term * GROUPS + group
            sent[place:place + 1, :] = exponent
        sent[chosen, :] = pack(*codes)


def multiply(shift, columns, weights, fields):
    terms, rows, depth = weights.shape
    width = fields[0].shape[1]
    half = width // PAIR
    return kernel_call(
        functools.partial(multiply_kernel, shift, columns),
        "products",
        [weights, *fields],
        0,
        [
            pltpu.VMEM((terms, rows, half), jnp.float32),
            pltpu.VMEM((rows + terms * GROUPS, half), jnp.int32),
        ],
        [pltpu.VMEM((depth, width), jnp.bfloat16)],
        2 * terms * rows * depth * width,
        rows * half * terms,
    )


def wanted_blocks(table, chips):
    out_index, in_index = lax.axis_index("out"), lax.axis_index("in")
    column, side = in_index // PAIR, in_index % PAIR
    return [position(table[out_index, column * PAIR + which], out_index, chips) for which in (side, 1 - side)]


def unpacked_products(received, rows, total):
    packed = received[rows, :]
    scale = total + rows.start // (total // GROUPS)
    scales = [received[place:place + 1, :] for place in (scale, scale + GROUPS)]
    return [unpack_high(packed, scales[0]), unpack_low(packed, scales[1])]


def unpack_kernel(received, result):
    total = result.shape[1]
    for parts in row_ranges(total):
        for rows in parts:
            for term, product in enumerate(unpacked_products(received, rows, total)):
                result[term, rows] = product


def unpacked(received, like):
    return kernel_call(
        unpack_kernel, "unpacked_products", [received], 0, [pltpu.VMEM(like.shape, like.dtype)], [],
        UNPACK_COST * like.size, 0,
    )[0]


def blocks_times_products(wanted, kept, received, pieces, rows, total):
    mine = [kept[0, rows], kept[1, rows]]
    if received.dtype == kept.dtype:
        other = [received[0, rows], received[1, rows]]
    else:
        other = unpacked_products(received, rows, total)
    value = None
    for index, products in zip(wanted, (mine, other)):
        for term, product in enumerate(products):
            chosen = choose(index, pieces, term, rows).astype(jnp.float32)
            value = chosen * product if value is None else value + chosen * product
    return value


def row_ranges(total):
    half = total // PAIR
    step = half // GROUPS
    return [
        [slice(part * half + group * step, part * half + (group + 1) * step) for part in range(PAIR)]
        for group in range(GROUPS)
    ]


def sums_kernel(arrivals, table, kept, received, *refs):
    arrived, pieces, result = refs[:arrivals], refs[arrivals:-1], refs[-1]
    total = kept.shape[1]
    wanted = wanted_blocks(table, len(pieces) // PAIR)
    for group, parts in enumerate(row_ranges(total)):
        codes = []
        for part, (rows, unpack) in enumerate(zip(parts, (unpack_high, unpack_low))):
            value = blocks_times_products(wanted, kept, received, pieces, rows, total)
            place = total // PAIR + part * GROUPS + group
            for ref in arrived:
                value = value + unpack(ref[parts[0], :], ref[place:place + 1, :])
            if result.dtype == jnp.int32:
                code, exponent = encode(value)
                codes.append(code)
                result[place:place + 1, :] = exponent
            else:
                result[rows, :] = value.astype(result.dtype)
        if codes:
            result[parts[0], :] = pack(*codes)


def sums(name, table, kept, received, arrived, pieces, result):
    terms, rows, cells = kept.shape
    return kernel_call(
        functools.partial(sums_kernel, len(arrived)), name, [table, kept, received, *arrived, *pieces], 1,
        [result], [], 8 * terms * rows * cells, rows * cells,
    )[0]


def partial_sums(table, kept, received, arrived, pieces):
    terms, rows, cells = kept.shape
    result = pltpu.VMEM((rows // PAIR + PAIR * GROUPS, cells), jnp.int32)
    return sums("partial_sums", table, kept, received, arrived, pieces, result)


def final_sums(table, kept, received, arrived, pieces):
    terms, rows, cells = kept.shape
    result = jax.ShapeDtypeStruct((rows, cells), jnp.bfloat16)
    return sums("final_sums", table, kept, received, arrived, pieces, result)


def after(value, *earlier):
    return lax.optimization_barrier((value, *earlier))[0]


def gathered_shards(out_count, in_count, kernel_weights, mode_field, diff_blocks, block_table):
    columns = in_count // PAIR

    def across_cores(value):
        return lax.ppermute(value, "out", [(r, r ^ 1) for r in range(out_count)])

    def along_chips(value):
        return lax.ppermute(value, "out", [(r, (r + PAIR) % out_count) for r in range(out_count)])

    def across_sides(value):
        return lax.ppermute(value, "in", [(s, s ^ 1) for s in range(in_count)])

    def along_columns(value, shift):
        return lax.ppermute(value, "in", [(s, (s + PAIR * shift) % in_count) for s in range(in_count)])

    order = list(range(1, columns)) + [0]
    weights, own_field, own_blocks = load([kernel_weights, mode_field, diff_blocks])
    far_field = after(along_chips(mode_field), weights)
    fields = [own_field] + [near(field) for field in (far_field, across_cores(mode_field), across_cores(far_field))]

    rings = [diff_blocks]
    for step in range(1, columns):
        rings.append(along_columns(rings[-1], -1))
    kept, sent = {}, {}
    for step in order:
        kept[step], sent[step] = multiply(-step, columns, weights, fields)
    core_own = across_cores(diff_blocks)
    far_own = along_chips(after(diff_blocks, far_field))
    far = [far_own]
    for place, step in enumerate(order[:-1]):
        earlier = [[far_field], [*sent.values(), core_own, far[-1]]][place] if place < 2 else far[-1:]
        far.append(along_chips(after(rings[step], *earlier)))

    received, coming, partials, pieces = {}, [], [], {}

    def send_sums(place):
        step = order[place]
        near_pieces = [rings[step], far[place + 1]]
        earlier = partials[-1:] if place == columns - 2 else []
        pieces[step] = [near(piece) for piece in near_pieces]
        pieces[step] += [near(across_cores(after(piece, *earlier))) for piece in near_pieces]
        partials.append(partial_sums(block_table, kept[step], received[step], coming[-1:], pieces[step]))
        coming.append(near(along_columns(partials[-1], -1)))
        return partials[-1]

    for place, step in enumerate(order):
        earlier = [received[order[place - 1]]] if place > 0 else []
        if place > 1:
            earlier.append(send_sums(place - 2))
        received[step] = near(across_sides(after(sent[step], *earlier)))
    send_sums(columns - 2)
    pieces[0] = [own_blocks, near(far_own), near(core_own), near(across_cores(after(far_own, coming[-1])))]
    others = near(unpacked(received[0], kept[0]))
    return final_sums(block_table, kept[0], others, coming[-1:], pieces[0])


def solution(mesh):
    out_count, in_count = mesh.shape["out"], mesh.shape["in"]
    in_specs = (P(None, "out", "in"), P("in", "out"), P(None, "out", "in"), P())
    out_specs = P("out", "in")

    def shards(kernel_weights, mode_field, diff_blocks, block_table):
        own_cells = diff_blocks.shape[2]
        gather = (
            kernel_weights.shape[0] == PAIR
            and own_cells % LANES == 0
            and mode_field.shape[1] == PAIR * own_cells
            and out_count == PAIR * PAIR
            and in_count == PAIR * out_count
        )
        if gather:
            return gathered_shards(out_count, in_count, kernel_weights, mode_field, diff_blocks, block_table)
        return routed_shards(kernel_weights, mode_field, diff_blocks, block_table)

    return jax.shard_map(shards, mesh=mesh, in_specs=in_specs, out_specs=out_specs, check_vma=False)
```

```python
import functools
import math

import jax
import jax.numpy as jnp
from jax import lax
from jax.experimental import pallas as pl
from jax.experimental.pallas import tpu as pltpu
from jax.sharding import PartitionSpec as P

PAIR = 2
TOP = 32767.0
GROUPS = 4
MERGE_COST = 100000
KERNEL_MEMORY = 24 << 20
LANES = 128


def routed_shards(kernel_weights, mode_field, diff_blocks, block_table):
    out_index = lax.axis_index("out")
    tile_rows = kernel_weights.shape[1]
    term_count = kernel_weights.shape[0]
    own_cells = diff_blocks.shape[2]
    needed_row = block_table[out_index]
    whole_field = lax.all_gather(mode_field, "out", axis=1, tiled=True)
    every_block = lax.all_gather(diff_blocks, "out", axis=1, tiled=True)
    block_count = every_block.shape[1] // tile_rows
    every_block = every_block.reshape(term_count, block_count, tile_rows, own_cells)
    arranged = jnp.take(every_block, needed_row, axis=1)
    routed = lax.all_to_all(arranged, "in", split_axis=1, concat_axis=3, tiled=True)
    partial_value = jnp.zeros((tile_rows, whole_field.shape[1]), jnp.float32)
    for term_index in range(term_count):
        product = jnp.dot(kernel_weights[term_index], whole_field, preferred_element_type=jnp.float32)
        partial_value = partial_value + routed[term_index, 0].astype(jnp.float32) * product
    summed = lax.psum_scatter(partial_value, "in", scatter_dimension=1, tiled=True)
    return summed.astype(jnp.bfloat16)


def encode(values):
    largest = jnp.maximum(jnp.max(jnp.abs(values), axis=0, keepdims=True), 1e-30)
    exponent = jnp.floor(jnp.log2(largest)) + 1.0
    share = values * (jnp.exp2(-exponent) * (TOP * TOP))
    root = share * lax.rsqrt(jnp.abs(share) + 1e-9)
    return jnp.round(root).astype(jnp.int32), exponent.astype(jnp.int32)


def pack(high, low):
    return (high << 16) | (low & 0xFFFF)


def decode(codes, exponent):
    root = codes.astype(jnp.float32)
    return root * jnp.abs(root) * (jnp.exp2(exponent.astype(jnp.float32)) * (1.0 / (TOP * TOP)))


def unpack_high(packed, exponent):
    return decode(packed >> 16, exponent)


def unpack_low(packed, exponent):
    return decode((packed << 16) >> 16, exponent)


def position(index, out_index, chips):
    crossed = jnp.where(index % PAIR != out_index % PAIR, chips, 0)
    return crossed + (out_index // PAIR - index // PAIR + chips) % chips


def choose(index, refs, *at):
    value = refs[0][at]
    for place in range(1, len(refs)):
        value = jnp.where(index == place, refs[place][at], value)
    return value


def near(value):
    return pltpu.with_memory_space_constraint(value, pltpu.VMEM)


def kernel_call(kernel, name, inputs, in_table, outputs, scratch, flops, transcendentals):
    moved = sum(math.prod(array.shape) * jnp.dtype(array.dtype).itemsize for array in [*inputs, *outputs])
    memory = pl.BlockSpec(memory_space=pltpu.VMEM)
    return pl.pallas_call(
        kernel,
        name=name,
        out_shape=outputs,
        in_specs=[pl.BlockSpec(memory_space=pltpu.SMEM)] * in_table + [memory] * (len(inputs) - in_table),
        out_specs=[memory] * len(outputs),
        scratch_shapes=scratch,
        compiler_params=pltpu.CompilerParams(vmem_limit_bytes=KERNEL_MEMORY),
        cost_estimate=pl.CostEstimate(flops=flops, bytes_accessed=moved, transcendentals=transcendentals),
    )(*inputs)


def load_kernel(*refs):
    count = len(refs) // 2
    for source, place in zip(refs[:count], refs[count:]):
        place[...] = source[...]


def load(arrays):
    return kernel_call(
        load_kernel, "load", [near(array) for array in arrays], 0,
        [pltpu.VMEM(array.shape, array.dtype) for array in arrays], [], 0, 0,
    )


def multiply_kernel(shift, columns, weights, *refs):
    *fields, kept, sent, field = refs
    terms, total, _ = weights.shape
    rows = total // GROUPS
    half = kept.shape[2]
    in_index = lax.axis_index("in")
    target = (in_index // PAIR - shift + columns) % columns
    source = position(target, lax.axis_index("out"), len(fields) // PAIR)
    side = in_index % PAIR

    for place, ref in enumerate(fields):
        for first in range(PAIR):
            @pl.when((source == place) & (side == first))
            def _():
                field[:, :half] = ref[:, first * half:(first + 1) * half]
                field[:, half:] = ref[:, (1 - first) * half:(2 - first) * half]

    for group in range(GROUPS):
        chosen = slice(group * rows, (group + 1) * rows)
        codes = []
        for term in range(terms):
            product = jnp.dot(weights[term, chosen], field[...], preferred_element_type=jnp.float32)
            kept[term, chosen] = product[:, :half]
            code, exponent = encode(product[:, half:])
            codes.append(code)
            place = total + term * GROUPS + group
            sent[place:place + 1, :] = exponent
        sent[chosen, :] = pack(*codes)


def multiply(shift, columns, weights, fields):
    terms, rows, depth = weights.shape
    width = fields[0].shape[1]
    half = width // PAIR
    return kernel_call(
        functools.partial(multiply_kernel, shift, columns),
        "products",
        [weights, *fields],
        0,
        [
            pltpu.VMEM((terms, rows, half), jnp.float32),
            pltpu.VMEM((rows + terms * GROUPS, half), jnp.int32),
        ],
        [pltpu.VMEM((depth, width), jnp.bfloat16)],
        2 * terms * rows * depth * width,
        rows * half * terms,
    )


def wanted_blocks(table, chips):
    out_index, in_index = lax.axis_index("out"), lax.axis_index("in")
    column, side = in_index // PAIR, in_index % PAIR
    return [position(table[out_index, column * PAIR + which], out_index, chips) for which in (side, 1 - side)]


def blocks_times_products(wanted, kept, received, pieces, rows, total):
    packed = received[rows, :]
    scale = total + rows.start // (total // GROUPS)
    mine = [kept[0, rows], kept[1, rows]]
    other = [
        unpack_high(packed, received[scale:scale + 1, :]),
        unpack_low(packed, received[scale + GROUPS:scale + GROUPS + 1, :]),
    ]
    value = None
    for index, products in zip(wanted, (mine, other)):
        for term, product in enumerate(products):
            chosen = choose(index, pieces, term, rows).astype(jnp.float32)
            value = chosen * product if value is None else value + chosen * product
    return value


def row_ranges(total):
    half = total // PAIR
    step = half // GROUPS
    return [
        [slice(part * half + group * step, part * half + (group + 1) * step) for part in range(PAIR)]
        for group in range(GROUPS)
    ]


def partial_kernel(table, kept, received, *refs):
    *pieces, sent = refs
    total = kept.shape[1]
    wanted = wanted_blocks(table, len(pieces) // PAIR)
    for group, parts in enumerate(row_ranges(total)):
        codes = []
        for part, rows in enumerate(parts):
            code, exponent = encode(blocks_times_products(wanted, kept, received, pieces, rows, total))
            codes.append(code)
            place = total // PAIR + part * GROUPS + group
            sent[place:place + 1, :] = exponent
        sent[parts[0], :] = pack(*codes)


def merge_kernel(*refs):
    *coming, merged = refs
    total = merged.shape[0]
    for group, parts in enumerate(row_ranges(total)):
        for part, (rows, unpack) in enumerate(zip(parts, (unpack_high, unpack_low))):
            place = total // PAIR + part * GROUPS + group
            values = [unpack(ref[parts[0], :], ref[place:place + 1, :]) for ref in coming]
            merged[rows, :] = functools.reduce(jnp.add, values)


def own_kernel(table, kept, received, merged, *refs):
    *pieces, result = refs
    total = kept.shape[1]
    wanted = wanted_blocks(table, len(pieces) // PAIR)
    for parts in row_ranges(total):
        for rows in parts:
            result[rows, :] = merged[rows, :] + blocks_times_products(wanted, kept, received, pieces, rows, total)


def final_kernel(own, last, gain):
    total = own.shape[0]
    for group, parts in enumerate(row_ranges(total)):
        for part, (rows, unpack) in enumerate(zip(parts, (unpack_high, unpack_low))):
            place = total // PAIR + part * GROUPS + group
            value = own[rows, :] + unpack(last[parts[0], :], last[place:place + 1, :])
            gain[rows, :] = value.astype(gain.dtype)


def partial_sums(table, kept, received, pieces):
    terms, rows, cells = kept.shape
    shape = (rows // PAIR + PAIR * GROUPS, cells)
    return kernel_call(
        partial_kernel, "partial_sums", [table, kept, received, *pieces], 1,
        [pltpu.VMEM(shape, jnp.int32)], [], 8 * terms * rows * cells, rows * cells,
    )[0]


def merged_sums(coming, rows):
    cells = coming[0].shape[1]
    return kernel_call(
        merge_kernel, "merged_sums", coming, 0,
        [pltpu.VMEM((rows, cells), jnp.float32)], [], MERGE_COST * rows * cells, 0,
    )[0]


def own_sums(table, kept, received, merged, pieces):
    terms, rows, cells = kept.shape
    return kernel_call(
        own_kernel, "own_sums", [table, kept, received, merged, *pieces], 1,
        [pltpu.VMEM((rows, cells), jnp.float32)], [], 8 * terms * rows * cells, 0,
    )[0]


def final_sums(own, last):
    rows, cells = own.shape
    return kernel_call(
        final_kernel, "final_sums", [own, last], 0,
        [jax.ShapeDtypeStruct((rows, cells), jnp.bfloat16)], [], 4 * rows * cells, 0,
    )[0]


def after(value, *earlier):
    return lax.optimization_barrier((value, *earlier))[0]


def gathered_shards(out_count, in_count, kernel_weights, mode_field, diff_blocks, block_table):
    columns = in_count // PAIR

    def across_cores(value):
        return lax.ppermute(value, "out", [(r, r ^ 1) for r in range(out_count)])

    def along_chips(value):
        return lax.ppermute(value, "out", [(r, (r + PAIR) % out_count) for r in range(out_count)])

    def across_sides(value):
        return lax.ppermute(value, "in", [(s, s ^ 1) for s in range(in_count)])

    def along_columns(value, shift):
        return lax.ppermute(value, "in", [(s, (s + PAIR * shift) % in_count) for s in range(in_count)])

    order = list(range(1, columns)) + [0]
    weights, own_field, own_blocks = load([kernel_weights, mode_field, diff_blocks])
    far_field = after(along_chips(mode_field), weights)
    fields = [own_field] + [near(field) for field in (far_field, across_cores(mode_field), across_cores(far_field))]

    rings = [diff_blocks]
    for step in range(1, columns):
        rings.append(along_columns(rings[-1], 1))
    kept, sent = {}, {}
    for step in order:
        kept[step], sent[step] = multiply(step, columns, weights, fields)
    core_own = across_cores(diff_blocks)
    far_own = along_chips(after(diff_blocks, far_field))
    far, pieces = [far_own], {}
    for place, step in enumerate(order[:-1]):
        earlier = [[far_field], [*sent.values(), core_own, far[-1]]][place] if place < 2 else far[-1:]
        far.append(along_chips(after(rings[step], *earlier)))
        pieces[step] = [near(rings[step]), near(far[-1])]
        pieces[step] += [near(across_cores(piece)) for piece in (rings[step], far[-1])]

    received, coming = {}, []

    def send_sums(place):
        step = order[place]
        ready = after(kept[step], *(coming[-1:] if place < columns - 2 else []))
        partial = partial_sums(block_table, ready, received[step], pieces[step])
        coming.append(near(along_columns(partial, -step)))
        return partial

    for place, step in enumerate(order):
        earlier = [received[order[place - 1]]] if place > 0 else []
        if place > 1:
            earlier.append(send_sums(place - 2))
        received[step] = near(across_sides(after(sent[step], *earlier)))
    latest = send_sums(columns - 2)
    pieces[0] = [own_blocks, near(far_own), near(core_own), near(across_cores(after(far_own, latest)))]
    merged = near(merged_sums(coming[:-1], kernel_weights.shape[1]))
    own = near(own_sums(block_table, kept[0], received[0], merged, pieces[0]))
    return final_sums(own, coming[-1])


def solution(mesh):
    out_count, in_count = mesh.shape["out"], mesh.shape["in"]
    in_specs = (P(None, "out", "in"), P("in", "out"), P(None, "out", "in"), P())
    out_specs = P("out", "in")

    def shards(kernel_weights, mode_field, diff_blocks, block_table):
        own_cells = diff_blocks.shape[2]
        gather = (
            kernel_weights.shape[0] == PAIR
            and own_cells % LANES == 0
            and mode_field.shape[1] == PAIR * own_cells
            and out_count == PAIR * PAIR
            and in_count == PAIR * out_count
        )
        if gather:
            return gathered_shards(out_count, in_count, kernel_weights, mode_field, diff_blocks, block_table)
        return routed_shards(kernel_weights, mode_field, diff_blocks, block_table)

    return jax.shard_map(shards, mesh=mesh, in_specs=in_specs, out_specs=out_specs, check_vma=False)
```

```python
import functools
import math

import jax
import jax.numpy as jnp
from jax import lax
from jax.experimental import pallas as pl
from jax.experimental.pallas import tpu as pltpu
from jax.sharding import PartitionSpec as P

PAIR = 2
TOP = 32767.0
GROUPS = 4
MERGE_COST = 100000
KERNEL_MEMORY = 24 << 20
LANES = 128


def routed_shards(kernel_weights, mode_field, diff_blocks, block_table):
    out_index = lax.axis_index("out")
    tile_rows = kernel_weights.shape[1]
    term_count = kernel_weights.shape[0]
    own_cells = diff_blocks.shape[2]
    needed_row = block_table[out_index]
    whole_field = lax.all_gather(mode_field, "out", axis=1, tiled=True)
    every_block = lax.all_gather(diff_blocks, "out", axis=1, tiled=True)
    block_count = every_block.shape[1] // tile_rows
    every_block = every_block.reshape(term_count, block_count, tile_rows, own_cells)
    arranged = jnp.take(every_block, needed_row, axis=1)
    routed = lax.all_to_all(arranged, "in", split_axis=1, concat_axis=3, tiled=True)
    partial_value = jnp.zeros((tile_rows, whole_field.shape[1]), jnp.float32)
    for term_index in range(term_count):
        product = jnp.dot(kernel_weights[term_index], whole_field, preferred_element_type=jnp.float32)
        partial_value = partial_value + routed[term_index, 0].astype(jnp.float32) * product
    summed = lax.psum_scatter(partial_value, "in", scatter_dimension=1, tiled=True)
    return summed.astype(jnp.bfloat16)


def encode(values):
    largest = jnp.maximum(jnp.max(jnp.abs(values), axis=0, keepdims=True), 1e-30)
    exponent = jnp.floor(jnp.log2(largest)) + 1.0
    share = values * (jnp.exp2(-exponent) * (TOP * TOP))
    root = share * lax.rsqrt(jnp.abs(share) + 1e-9)
    return jnp.round(root).astype(jnp.int32), exponent.astype(jnp.int32)


def pack(high, low):
    return (high << 16) | (low & 0xFFFF)


def decode(codes, exponent):
    root = codes.astype(jnp.float32)
    return root * jnp.abs(root) * (jnp.exp2(exponent.astype(jnp.float32)) * (1.0 / (TOP * TOP)))


def unpack_high(packed, exponent):
    return decode(packed >> 16, exponent)


def unpack_low(packed, exponent):
    return decode((packed << 16) >> 16, exponent)


def position(index, out_index, chips):
    crossed = jnp.where(index % PAIR != out_index % PAIR, chips, 0)
    return crossed + (out_index // PAIR - index // PAIR + chips) % chips


def choose(index, refs, *at):
    value = refs[0][at]
    for place in range(1, len(refs)):
        value = jnp.where(index == place, refs[place][at], value)
    return value


def near(value):
    return pltpu.with_memory_space_constraint(value, pltpu.VMEM)


def kernel_call(kernel, name, inputs, in_table, outputs, scratch, flops, transcendentals):
    moved = sum(math.prod(array.shape) * jnp.dtype(array.dtype).itemsize for array in [*inputs, *outputs])
    memory = pl.BlockSpec(memory_space=pltpu.VMEM)
    return pl.pallas_call(
        kernel,
        name=name,
        out_shape=outputs,
        in_specs=[pl.BlockSpec(memory_space=pltpu.SMEM)] * in_table + [memory] * (len(inputs) - in_table),
        out_specs=[memory] * len(outputs),
        scratch_shapes=scratch,
        compiler_params=pltpu.CompilerParams(vmem_limit_bytes=KERNEL_MEMORY),
        cost_estimate=pl.CostEstimate(flops=flops, bytes_accessed=moved, transcendentals=transcendentals),
    )(*inputs)


def load_kernel(*refs):
    count = len(refs) // 2
    for source, place in zip(refs[:count], refs[count:]):
        place[...] = source[...]


def load(arrays):
    return kernel_call(
        load_kernel, "load", [near(array) for array in arrays], 0,
        [pltpu.VMEM(array.shape, array.dtype) for array in arrays], [], 0, 0,
    )


def multiply_kernel(shift, columns, weights, *refs):
    *fields, kept, sent, field = refs
    terms, total, _ = weights.shape
    rows = total // GROUPS
    half = kept.shape[2]
    in_index = lax.axis_index("in")
    target = (in_index // PAIR - shift + columns) % columns
    source = position(target, lax.axis_index("out"), len(fields) // PAIR)
    side = in_index % PAIR

    for place, ref in enumerate(fields):
        for first in range(PAIR):
            @pl.when((source == place) & (side == first))
            def _():
                field[:, :half] = ref[:, first * half:(first + 1) * half]
                field[:, half:] = ref[:, (1 - first) * half:(2 - first) * half]

    for group in range(GROUPS):
        chosen = slice(group * rows, (group + 1) * rows)
        codes = []
        for term in range(terms):
            product = jnp.dot(weights[term, chosen], field[...], preferred_element_type=jnp.float32)
            kept[term, chosen] = product[:, :half]
            code, exponent = encode(product[:, half:])
            codes.append(code)
            place = total + term * GROUPS + group
            sent[place:place + 1, :] = exponent
        sent[chosen, :] = pack(*codes)


def multiply(shift, columns, weights, fields):
    terms, rows, depth = weights.shape
    width = fields[0].shape[1]
    half = width // PAIR
    return kernel_call(
        functools.partial(multiply_kernel, shift, columns),
        "products",
        [weights, *fields],
        0,
        [
            pltpu.VMEM((terms, rows, half), jnp.float32),
            pltpu.VMEM((rows + terms * GROUPS, half), jnp.int32),
        ],
        [pltpu.VMEM((depth, width), jnp.bfloat16)],
        2 * terms * rows * depth * width,
        rows * half * terms,
    )


def wanted_blocks(table, chips):
    out_index, in_index = lax.axis_index("out"), lax.axis_index("in")
    column, side = in_index // PAIR, in_index % PAIR
    return [position(table[out_index, column * PAIR + which], out_index, chips) for which in (side, 1 - side)]


def blocks_times_products(wanted, kept, received, pieces, rows, total):
    packed = received[rows, :]
    scale = total + rows.start // (total // GROUPS)
    mine = [kept[0, rows], kept[1, rows]]
    other = [
        unpack_high(packed, received[scale:scale + 1, :]),
        unpack_low(packed, received[scale + GROUPS:scale + GROUPS + 1, :]),
    ]
    value = None
    for index, products in zip(wanted, (mine, other)):
        for term, product in enumerate(products):
            chosen = choose(index, pieces, term, rows).astype(jnp.float32)
            value = chosen * product if value is None else value + chosen * product
    return value


def row_ranges(total):
    half = total // PAIR
    step = half // GROUPS
    return [
        [slice(part * half + group * step, part * half + (group + 1) * step) for part in range(PAIR)]
        for group in range(GROUPS)
    ]


def partial_kernel(table, kept, received, *refs):
    *pieces, sent = refs
    total = kept.shape[1]
    wanted = wanted_blocks(table, len(pieces) // PAIR)
    for group, parts in enumerate(row_ranges(total)):
        codes = []
        for part, rows in enumerate(parts):
            code, exponent = encode(blocks_times_products(wanted, kept, received, pieces, rows, total))
            codes.append(code)
            place = total // PAIR + part * GROUPS + group
            sent[place:place + 1, :] = exponent
        sent[parts[0], :] = pack(*codes)


def merge_kernel(*refs):
    *coming, merged = refs
    total = merged.shape[0]
    for group, parts in enumerate(row_ranges(total)):
        for part, (rows, unpack) in enumerate(zip(parts, (unpack_high, unpack_low))):
            place = total // PAIR + part * GROUPS + group
            values = [unpack(ref[parts[0], :], ref[place:place + 1, :]) for ref in coming]
            merged[rows, :] = functools.reduce(jnp.add, values)


def own_kernel(table, kept, received, merged, *refs):
    *pieces, result = refs
    total = kept.shape[1]
    wanted = wanted_blocks(table, len(pieces) // PAIR)
    for parts in row_ranges(total):
        for rows in parts:
            result[rows, :] = merged[rows, :] + blocks_times_products(wanted, kept, received, pieces, rows, total)


def final_kernel(own, last, gain):
    total = own.shape[0]
    for group, parts in enumerate(row_ranges(total)):
        for part, (rows, unpack) in enumerate(zip(parts, (unpack_high, unpack_low))):
            place = total // PAIR + part * GROUPS + group
            value = own[rows, :] + unpack(last[parts[0], :], last[place:place + 1, :])
            gain[rows, :] = value.astype(gain.dtype)


def partial_sums(table, kept, received, pieces):
    terms, rows, cells = kept.shape
    shape = (rows // PAIR + PAIR * GROUPS, cells)
    return kernel_call(
        partial_kernel, "partial_sums", [table, kept, received, *pieces], 1,
        [pltpu.VMEM(shape, jnp.int32)], [], 8 * terms * rows * cells, rows * cells,
    )[0]


def merged_sums(coming, rows):
    cells = coming[0].shape[1]
    return kernel_call(
        merge_kernel, "merged_sums", coming, 0,
        [pltpu.VMEM((rows, cells), jnp.float32)], [], MERGE_COST * rows * cells, 0,
    )[0]


def own_sums(table, kept, received, merged, pieces):
    terms, rows, cells = kept.shape
    return kernel_call(
        own_kernel, "own_sums", [table, kept, received, merged, *pieces], 1,
        [pltpu.VMEM((rows, cells), jnp.float32)], [], 8 * terms * rows * cells, 0,
    )[0]


def final_sums(own, last):
    rows, cells = own.shape
    return kernel_call(
        final_kernel, "final_sums", [own, last], 0,
        [jax.ShapeDtypeStruct((rows, cells), jnp.bfloat16)], [], 4 * rows * cells, 0,
    )[0]


def after(value, *earlier):
    return lax.optimization_barrier((value, *earlier))[0]


def gathered_shards(out_count, in_count, kernel_weights, mode_field, diff_blocks, block_table):
    columns = in_count // PAIR

    def across_cores(value):
        return lax.ppermute(value, "out", [(r, r ^ 1) for r in range(out_count)])

    def along_chips(value):
        return lax.ppermute(value, "out", [(r, (r + PAIR) % out_count) for r in range(out_count)])

    def across_sides(value):
        return lax.ppermute(value, "in", [(s, s ^ 1) for s in range(in_count)])

    def along_columns(value, shift):
        return lax.ppermute(value, "in", [(s, (s + PAIR * shift) % in_count) for s in range(in_count)])

    order = list(range(1, columns)) + [0]
    weights, own_field, own_blocks = load([kernel_weights, mode_field, diff_blocks])
    far_field = after(along_chips(mode_field), weights)
    fields = [own_field] + [near(field) for field in (far_field, across_cores(mode_field), across_cores(far_field))]

    rings = [diff_blocks]
    for step in range(1, columns):
        rings.append(along_columns(rings[-1], 1))
    kept, sent = {}, {}
    for step in order:
        kept[step], sent[step] = multiply(step, columns, weights, fields)
    core_own = across_cores(diff_blocks)
    far_own = along_chips(after(diff_blocks, far_field))
    far, pieces = [far_own], {}
    for place, step in enumerate(order[:-1]):
        earlier = [[far_field], [*sent.values(), core_own, far[-1]]][place] if place < 2 else far[-1:]
        far.append(along_chips(after(rings[step], *earlier)))

    received, coming = {}, []

    def send_sums(place):
        step = order[place]
        swapped = [received[step]] if place == 1 else []
        pieces[step] = [near(rings[step]), near(far[place + 1]), near(across_cores(rings[step]))]
        pieces[step].append(near(across_cores(after(far[place + 1], *swapped))))
        ready = after(kept[step], *(coming[-1:] if place < columns - 2 else []))
        partial = partial_sums(block_table, ready, received[step], pieces[step])
        coming.append(near(along_columns(partial, -step)))
        return partial

    for place, step in enumerate(order):
        earlier = [received[order[place - 1]]] if place > 0 else []
        if place > 1:
            earlier.append(send_sums(place - 2))
        received[step] = near(across_sides(after(sent[step], *earlier)))
    latest = send_sums(columns - 2)
    pieces[0] = [own_blocks, near(far_own), near(core_own), near(across_cores(after(far_own, latest)))]
    merged = near(merged_sums(coming[:-1], kernel_weights.shape[1]))
    own = near(own_sums(block_table, kept[0], received[0], merged, pieces[0]))
    return final_sums(own, coming[-1])


def solution(mesh):
    out_count, in_count = mesh.shape["out"], mesh.shape["in"]
    in_specs = (P(None, "out", "in"), P("in", "out"), P(None, "out", "in"), P())
    out_specs = P("out", "in")

    def shards(kernel_weights, mode_field, diff_blocks, block_table):
        own_cells = diff_blocks.shape[2]
        gather = (
            kernel_weights.shape[0] == PAIR
            and own_cells % LANES == 0
            and mode_field.shape[1] == PAIR * own_cells
            and out_count == PAIR * PAIR
            and in_count == PAIR * out_count
        )
        if gather:
            return gathered_shards(out_count, in_count, kernel_weights, mode_field, diff_blocks, block_table)
        return routed_shards(kernel_weights, mode_field, diff_blocks, block_table)

    return jax.shard_map(shards, mesh=mesh, in_specs=in_specs, out_specs=out_specs, check_vma=False)
```

```python
import functools
import math

import jax
import jax.numpy as jnp
from jax import lax
from jax.experimental import pallas as pl
from jax.experimental.pallas import tpu as pltpu
from jax.sharding import PartitionSpec as P

PAIR = 2
TOP = 32767.0
GROUPS = 4
MERGE_COST = 100000
KERNEL_MEMORY = 24 << 20
LANES = 128


def routed_shards(kernel_weights, mode_field, diff_blocks, block_table):
    out_index = lax.axis_index("out")
    tile_rows = kernel_weights.shape[1]
    term_count = kernel_weights.shape[0]
    own_cells = diff_blocks.shape[2]
    needed_row = block_table[out_index]
    whole_field = lax.all_gather(mode_field, "out", axis=1, tiled=True)
    every_block = lax.all_gather(diff_blocks, "out", axis=1, tiled=True)
    block_count = every_block.shape[1] // tile_rows
    every_block = every_block.reshape(term_count, block_count, tile_rows, own_cells)
    arranged = jnp.take(every_block, needed_row, axis=1)
    routed = lax.all_to_all(arranged, "in", split_axis=1, concat_axis=3, tiled=True)
    partial_value = jnp.zeros((tile_rows, whole_field.shape[1]), jnp.float32)
    for term_index in range(term_count):
        product = jnp.dot(kernel_weights[term_index], whole_field, preferred_element_type=jnp.float32)
        partial_value = partial_value + routed[term_index, 0].astype(jnp.float32) * product
    summed = lax.psum_scatter(partial_value, "in", scatter_dimension=1, tiled=True)
    return summed.astype(jnp.bfloat16)


def encode(values):
    largest = jnp.maximum(jnp.max(jnp.abs(values), axis=0, keepdims=True), 1e-30)
    exponent = jnp.floor(jnp.log2(largest)) + 1.0
    share = values * (jnp.exp2(-exponent) * (TOP * TOP))
    root = share * lax.rsqrt(jnp.abs(share) + 1e-9)
    return jnp.round(root).astype(jnp.int32), exponent.astype(jnp.int32)


def pack(high, low):
    return (high << 16) | (low & 0xFFFF)


def decode(codes, exponent):
    root = codes.astype(jnp.float32)
    return root * jnp.abs(root) * (jnp.exp2(exponent.astype(jnp.float32)) * (1.0 / (TOP * TOP)))


def unpack_high(packed, exponent):
    return decode(packed >> 16, exponent)


def unpack_low(packed, exponent):
    return decode((packed << 16) >> 16, exponent)


def position(index, out_index, chips):
    crossed = jnp.where(index % PAIR != out_index % PAIR, chips, 0)
    return crossed + (out_index // PAIR - index // PAIR + chips) % chips


def choose(index, refs, *at):
    value = refs[0][at]
    for place in range(1, len(refs)):
        value = jnp.where(index == place, refs[place][at], value)
    return value


def near(value):
    return pltpu.with_memory_space_constraint(value, pltpu.VMEM)


def kernel_call(kernel, name, inputs, in_table, outputs, scratch, flops, transcendentals):
    moved = sum(math.prod(array.shape) * jnp.dtype(array.dtype).itemsize for array in [*inputs, *outputs])
    memory = pl.BlockSpec(memory_space=pltpu.VMEM)
    return pl.pallas_call(
        kernel,
        name=name,
        out_shape=outputs,
        in_specs=[pl.BlockSpec(memory_space=pltpu.SMEM)] * in_table + [memory] * (len(inputs) - in_table),
        out_specs=[memory] * len(outputs),
        scratch_shapes=scratch,
        compiler_params=pltpu.CompilerParams(vmem_limit_bytes=KERNEL_MEMORY),
        cost_estimate=pl.CostEstimate(flops=flops, bytes_accessed=moved, transcendentals=transcendentals),
    )(*inputs)


def load_kernel(*refs):
    count = len(refs) // 2
    for source, place in zip(refs[:count], refs[count:]):
        place[...] = source[...]


def load(arrays):
    return kernel_call(
        load_kernel, "load", [near(array) for array in arrays], 0,
        [pltpu.VMEM(array.shape, array.dtype) for array in arrays], [], 0, 0,
    )


def multiply_kernel(shift, columns, weights, *refs):
    *fields, kept, sent, field = refs
    terms, total, _ = weights.shape
    rows = total // GROUPS
    half = kept.shape[2]
    in_index = lax.axis_index("in")
    target = (in_index // PAIR - shift + columns) % columns
    source = position(target, lax.axis_index("out"), len(fields) // PAIR)
    side = in_index % PAIR

    for place, ref in enumerate(fields):
        for first in range(PAIR):
            @pl.when((source == place) & (side == first))
            def _():
                field[:, :half] = ref[:, first * half:(first + 1) * half]
                field[:, half:] = ref[:, (1 - first) * half:(2 - first) * half]

    for group in range(GROUPS):
        chosen = slice(group * rows, (group + 1) * rows)
        codes = []
        for term in range(terms):
            product = jnp.dot(weights[term, chosen], field[...], preferred_element_type=jnp.float32)
            kept[term, chosen] = product[:, :half]
            code, exponent = encode(product[:, half:])
            codes.append(code)
            place = total + term * GROUPS + group
            sent[place:place + 1, :] = exponent
        sent[chosen, :] = pack(*codes)


def multiply(shift, columns, weights, fields):
    terms, rows, depth = weights.shape
    width = fields[0].shape[1]
    half = width // PAIR
    return kernel_call(
        functools.partial(multiply_kernel, shift, columns),
        "products",
        [weights, *fields],
        0,
        [
            pltpu.VMEM((terms, rows, half), jnp.float32),
            pltpu.VMEM((rows + terms * GROUPS, half), jnp.int32),
        ],
        [pltpu.VMEM((depth, width), jnp.bfloat16)],
        2 * terms * rows * depth * width,
        rows * half * terms,
    )


def wanted_blocks(table, chips):
    out_index, in_index = lax.axis_index("out"), lax.axis_index("in")
    column, side = in_index // PAIR, in_index % PAIR
    return [position(table[out_index, column * PAIR + which], out_index, chips) for which in (side, 1 - side)]


def blocks_times_products(wanted, kept, received, pieces, rows, total):
    packed = received[rows, :]
    scale = total + rows.start // (total // GROUPS)
    mine = [kept[0, rows], kept[1, rows]]
    other = [
        unpack_high(packed, received[scale:scale + 1, :]),
        unpack_low(packed, received[scale + GROUPS:scale + GROUPS + 1, :]),
    ]
    value = None
    for index, products in zip(wanted, (mine, other)):
        for term, product in enumerate(products):
            chosen = choose(index, pieces, term, rows).astype(jnp.float32)
            value = chosen * product if value is None else value + chosen * product
    return value


def row_ranges(total):
    half = total // PAIR
    step = half // GROUPS
    return [
        [slice(part * half + group * step, part * half + (group + 1) * step) for part in range(PAIR)]
        for group in range(GROUPS)
    ]


def partial_kernel(table, kept, received, *refs):
    *pieces, sent = refs
    total = kept.shape[1]
    wanted = wanted_blocks(table, len(pieces) // PAIR)
    for group, parts in enumerate(row_ranges(total)):
        codes = []
        for part, rows in enumerate(parts):
            code, exponent = encode(blocks_times_products(wanted, kept, received, pieces, rows, total))
            codes.append(code)
            place = total // PAIR + part * GROUPS + group
            sent[place:place + 1, :] = exponent
        sent[parts[0], :] = pack(*codes)


def merge_kernel(*refs):
    *coming, merged = refs
    total = merged.shape[0]
    for group, parts in enumerate(row_ranges(total)):
        for part, (rows, unpack) in enumerate(zip(parts, (unpack_high, unpack_low))):
            place = total // PAIR + part * GROUPS + group
            values = [unpack(ref[parts[0], :], ref[place:place + 1, :]) for ref in coming]
            merged[rows, :] = functools.reduce(jnp.add, values)


def own_kernel(table, kept, received, merged, *refs):
    *pieces, result = refs
    total = kept.shape[1]
    wanted = wanted_blocks(table, len(pieces) // PAIR)
    for parts in row_ranges(total):
        for rows in parts:
            result[rows, :] = merged[rows, :] + blocks_times_products(wanted, kept, received, pieces, rows, total)


def final_kernel(own, last, gain):
    total = own.shape[0]
    for group, parts in enumerate(row_ranges(total)):
        for part, (rows, unpack) in enumerate(zip(parts, (unpack_high, unpack_low))):
            place = total // PAIR + part * GROUPS + group
            value = own[rows, :] + unpack(last[parts[0], :], last[place:place + 1, :])
            gain[rows, :] = value.astype(gain.dtype)


def partial_sums(table, kept, received, pieces):
    terms, rows, cells = kept.shape
    shape = (rows // PAIR + PAIR * GROUPS, cells)
    return kernel_call(
        partial_kernel, "partial_sums", [table, kept, received, *pieces], 1,
        [pltpu.VMEM(shape, jnp.int32)], [], 8 * terms * rows * cells, rows * cells,
    )[0]


def merged_sums(coming, rows):
    cells = coming[0].shape[1]
    return kernel_call(
        merge_kernel, "merged_sums", coming, 0,
        [pltpu.VMEM((rows, cells), jnp.float32)], [], MERGE_COST * rows * cells, 0,
    )[0]


def own_sums(table, kept, received, merged, pieces):
    terms, rows, cells = kept.shape
    return kernel_call(
        own_kernel, "own_sums", [table, kept, received, merged, *pieces], 1,
        [pltpu.VMEM((rows, cells), jnp.float32)], [], 8 * terms * rows * cells, 0,
    )[0]


def final_sums(own, last):
    rows, cells = own.shape
    return kernel_call(
        final_kernel, "final_sums", [own, last], 0,
        [jax.ShapeDtypeStruct((rows, cells), jnp.bfloat16)], [], 4 * rows * cells, 0,
    )[0]


def after(value, *earlier):
    return lax.optimization_barrier((value, *earlier))[0]


def gathered_shards(out_count, in_count, kernel_weights, mode_field, diff_blocks, block_table):
    columns = in_count // PAIR

    def across_cores(value):
        return lax.ppermute(value, "out", [(r, r ^ 1) for r in range(out_count)])

    def along_chips(value):
        return lax.ppermute(value, "out", [(r, (r + PAIR) % out_count) for r in range(out_count)])

    def across_sides(value):
        return lax.ppermute(value, "in", [(s, s ^ 1) for s in range(in_count)])

    def along_columns(value, shift):
        return lax.ppermute(value, "in", [(s, (s + PAIR * shift) % in_count) for s in range(in_count)])

    order = list(range(1, columns)) + [0]
    weights, own_field, own_blocks = load([kernel_weights, mode_field, diff_blocks])
    far_field = after(along_chips(mode_field), weights)
    fields = [own_field] + [near(field) for field in (far_field, across_cores(mode_field), across_cores(far_field))]

    rings = [diff_blocks]
    for step in range(1, columns):
        rings.append(along_columns(rings[-1], 1))
    kept, sent = {}, {}
    for step in order:
        kept[step], sent[step] = multiply(step, columns, weights, fields)
    core_own = across_cores(diff_blocks)
    far_own = along_chips(after(diff_blocks, far_field))
    far, pieces = [far_own], {}
    for place, step in enumerate(order[:-1]):
        earlier = [[far_field], [*sent.values(), core_own, far[-1]]][place] if place < 2 else far[-1:]
        far.append(along_chips(after(rings[step], *earlier)))

    received, coming, partials = {}, [], []

    def send_sums(place):
        step = order[place]
        swapped = [received[step]] if place == 1 else []
        made = partials if place == 1 else []
        pieces[step] = [near(rings[step]), near(far[place + 1]), near(across_cores(after(rings[step], *made)))]
        pieces[step].append(near(across_cores(after(far[place + 1], *swapped))))
        ready = after(kept[step], *(coming[-1:] if place < columns - 2 else []))
        partial = partial_sums(block_table, ready, received[step], pieces[step])
        partials.append(partial)
        coming.append(near(along_columns(partial, -step)))
        return partial

    for place, step in enumerate(order):
        earlier = [received[order[place - 1]]] if place > 0 else []
        if place > 1:
            earlier.append(send_sums(place - 2))
        received[step] = near(across_sides(after(sent[step], *earlier)))
    latest = send_sums(columns - 2)
    pieces[0] = [own_blocks, near(far_own), near(core_own), near(across_cores(after(far_own, latest)))]
    merged = near(merged_sums(coming[:-1], kernel_weights.shape[1]))
    own = near(own_sums(block_table, kept[0], received[0], merged, pieces[0]))
    return final_sums(own, coming[-1])


def solution(mesh):
    out_count, in_count = mesh.shape["out"], mesh.shape["in"]
    in_specs = (P(None, "out", "in"), P("in", "out"), P(None, "out", "in"), P())
    out_specs = P("out", "in")

    def shards(kernel_weights, mode_field, diff_blocks, block_table):
        own_cells = diff_blocks.shape[2]
        gather = (
            kernel_weights.shape[0] == PAIR
            and own_cells % LANES == 0
            and mode_field.shape[1] == PAIR * own_cells
            and out_count == PAIR * PAIR
            and in_count == PAIR * out_count
        )
        if gather:
            return gathered_shards(out_count, in_count, kernel_weights, mode_field, diff_blocks, block_table)
        return routed_shards(kernel_weights, mode_field, diff_blocks, block_table)

    return jax.shard_map(shards, mesh=mesh, in_specs=in_specs, out_specs=out_specs, check_vma=False)
```

```python
import functools
import math

import jax
import jax.numpy as jnp
from jax import lax
from jax.experimental import pallas as pl
from jax.experimental.pallas import tpu as pltpu
from jax.sharding import PartitionSpec as P

PAIR = 2
TOP = 32767.0
GROUPS = 4
MERGE_COST = 100000
KERNEL_MEMORY = 24 << 20
LANES = 128


def routed_shards(kernel_weights, mode_field, diff_blocks, block_table):
    out_index = lax.axis_index("out")
    tile_rows = kernel_weights.shape[1]
    term_count = kernel_weights.shape[0]
    own_cells = diff_blocks.shape[2]
    needed_row = block_table[out_index]
    whole_field = lax.all_gather(mode_field, "out", axis=1, tiled=True)
    every_block = lax.all_gather(diff_blocks, "out", axis=1, tiled=True)
    block_count = every_block.shape[1] // tile_rows
    every_block = every_block.reshape(term_count, block_count, tile_rows, own_cells)
    arranged = jnp.take(every_block, needed_row, axis=1)
    routed = lax.all_to_all(arranged, "in", split_axis=1, concat_axis=3, tiled=True)
    partial_value = jnp.zeros((tile_rows, whole_field.shape[1]), jnp.float32)
    for term_index in range(term_count):
        product = jnp.dot(kernel_weights[term_index], whole_field, preferred_element_type=jnp.float32)
        partial_value = partial_value + routed[term_index, 0].astype(jnp.float32) * product
    summed = lax.psum_scatter(partial_value, "in", scatter_dimension=1, tiled=True)
    return summed.astype(jnp.bfloat16)


def encode(values):
    largest = jnp.maximum(jnp.max(jnp.abs(values), axis=0, keepdims=True), 1e-25)
    exponent = jnp.floor(jnp.log2(largest)) + 1.0
    share = values * (jnp.exp2(-exponent) * (TOP * TOP))
    root = share * lax.rsqrt(jnp.abs(share) + 1e-9)
    return jnp.round(root).astype(jnp.int32), exponent.astype(jnp.int32)


def pack(high, low):
    return (high << 16) | (low & 0xFFFF)


def decode(codes, exponent):
    root = codes.astype(jnp.float32)
    return root * jnp.abs(root) * (jnp.exp2(exponent.astype(jnp.float32)) * (1.0 / (TOP * TOP)))


def unpack_high(packed, exponent):
    return decode(packed >> 16, exponent)


def unpack_low(packed, exponent):
    return decode((packed << 16) >> 16, exponent)


def position(index, out_index, chips):
    crossed = jnp.where(index % PAIR != out_index % PAIR, chips, 0)
    return crossed + (out_index // PAIR - index // PAIR + chips) % chips


def choose(index, refs, *at):
    value = refs[0][at]
    for place in range(1, len(refs)):
        value = jnp.where(index == place, refs[place][at], value)
    return value


def near(value):
    return pltpu.with_memory_space_constraint(value, pltpu.VMEM)


def kernel_call(kernel, name, inputs, in_table, outputs, scratch, flops, transcendentals):
    moved = sum(math.prod(array.shape) * jnp.dtype(array.dtype).itemsize for array in [*inputs, *outputs])
    memory = pl.BlockSpec(memory_space=pltpu.VMEM)
    return pl.pallas_call(
        kernel,
        name=name,
        out_shape=outputs,
        in_specs=[pl.BlockSpec(memory_space=pltpu.SMEM)] * in_table + [memory] * (len(inputs) - in_table),
        out_specs=[memory] * len(outputs),
        scratch_shapes=scratch,
        compiler_params=pltpu.CompilerParams(vmem_limit_bytes=KERNEL_MEMORY),
        cost_estimate=pl.CostEstimate(flops=flops, bytes_accessed=moved, transcendentals=transcendentals),
    )(*inputs)


def load_kernel(*refs):
    count = len(refs) // 2
    for source, place in zip(refs[:count], refs[count:]):
        place[...] = source[...]


def load(arrays):
    return kernel_call(
        load_kernel, "load", [near(array) for array in arrays], 0,
        [pltpu.VMEM(array.shape, array.dtype) for array in arrays], [], 0, 0,
    )


def multiply_kernel(shift, columns, weights, *refs):
    *fields, kept, sent, field = refs
    terms, total, _ = weights.shape
    rows = total // GROUPS
    half = kept.shape[2]
    in_index = lax.axis_index("in")
    target = (in_index // PAIR - shift + columns) % columns
    source = position(target, lax.axis_index("out"), len(fields) // PAIR)
    side = in_index % PAIR

    for place, ref in enumerate(fields):
        for first in range(PAIR):
            @pl.when((source == place) & (side == first))
            def _():
                field[:, :half] = ref[:, first * half:(first + 1) * half]
                field[:, half:] = ref[:, (1 - first) * half:(2 - first) * half]

    for group in range(GROUPS):
        chosen = slice(group * rows, (group + 1) * rows)
        codes = []
        for term in range(terms):
            product = jnp.dot(weights[term, chosen], field[...], preferred_element_type=jnp.float32)
            kept[term, chosen] = product[:, :half]
            code, exponent = encode(product[:, half:])
            codes.append(code)
            place = total + term * GROUPS + group
            sent[place:place + 1, :] = exponent
        sent[chosen, :] = pack(*codes)


def multiply(shift, columns, weights, fields):
    terms, rows, depth = weights.shape
    width = fields[0].shape[1]
    half = width // PAIR
    return kernel_call(
        functools.partial(multiply_kernel, shift, columns),
        "products",
        [weights, *fields],
        0,
        [
            pltpu.VMEM((terms, rows, half), jnp.float32),
            pltpu.VMEM((rows + terms * GROUPS, half), jnp.int32),
        ],
        [pltpu.VMEM((depth, width), jnp.bfloat16)],
        2 * terms * rows * depth * width,
        rows * half * terms,
    )


def wanted_blocks(table, chips):
    out_index, in_index = lax.axis_index("out"), lax.axis_index("in")
    column, side = in_index // PAIR, in_index % PAIR
    return [position(table[out_index, column * PAIR + which], out_index, chips) for which in (side, 1 - side)]


def blocks_times_products(wanted, kept, received, pieces, rows, total):
    packed = received[rows, :]
    scale = total + rows.start // (total // GROUPS)
    mine = [kept[0, rows], kept[1, rows]]
    other = [
        unpack_high(packed, received[scale:scale + 1, :]),
        unpack_low(packed, received[scale + GROUPS:scale + GROUPS + 1, :]),
    ]
    value = None
    for index, products in zip(wanted, (mine, other)):
        for term, product in enumerate(products):
            chosen = choose(index, pieces, term, rows).astype(jnp.float32)
            value = chosen * product if value is None else value + chosen * product
    return value


def row_ranges(total):
    half = total // PAIR
    step = half // GROUPS
    return [
        [slice(part * half + group * step, part * half + (group + 1) * step) for part in range(PAIR)]
        for group in range(GROUPS)
    ]


def partial_kernel(table, kept, received, *refs):
    *pieces, sent = refs
    total = kept.shape[1]
    wanted = wanted_blocks(table, len(pieces) // PAIR)
    for group, parts in enumerate(row_ranges(total)):
        codes = []
        for part, rows in enumerate(parts):
            code, exponent = encode(blocks_times_products(wanted, kept, received, pieces, rows, total))
            codes.append(code)
            place = total // PAIR + part * GROUPS + group
            sent[place:place + 1, :] = exponent
        sent[parts[0], :] = pack(*codes)


def merge_kernel(*refs):
    *coming, merged = refs
    total = merged.shape[0]
    for group, parts in enumerate(row_ranges(total)):
        for part, (rows, unpack) in enumerate(zip(parts, (unpack_high, unpack_low))):
            place = total // PAIR + part * GROUPS + group
            values = [unpack(ref[parts[0], :], ref[place:place + 1, :]) for ref in coming]
            merged[rows, :] = functools.reduce(jnp.add, values)


def own_kernel(table, kept, received, merged, *refs):
    *pieces, result = refs
    total = kept.shape[1]
    wanted = wanted_blocks(table, len(pieces) // PAIR)
    for parts in row_ranges(total):
        for rows in parts:
            result[rows, :] = merged[rows, :] + blocks_times_products(wanted, kept, received, pieces, rows, total)


def final_kernel(own, last, gain):
    total = own.shape[0]
    for group, parts in enumerate(row_ranges(total)):
        for part, (rows, unpack) in enumerate(zip(parts, (unpack_high, unpack_low))):
            place = total // PAIR + part * GROUPS + group
            value = own[rows, :] + unpack(last[parts[0], :], last[place:place + 1, :])
            gain[rows, :] = value.astype(gain.dtype)


def partial_sums(table, kept, received, pieces):
    terms, rows, cells = kept.shape
    shape = (rows // PAIR + PAIR * GROUPS, cells)
    return kernel_call(
        partial_kernel, "partial_sums", [table, kept, received, *pieces], 1,
        [pltpu.VMEM(shape, jnp.int32)], [], 8 * terms * rows * cells, rows * cells,
    )[0]


def merged_sums(coming, rows):
    cells = coming[0].shape[1]
    return kernel_call(
        merge_kernel, "merged_sums", coming, 0,
        [pltpu.VMEM((rows, cells), jnp.float32)], [], MERGE_COST * rows * cells, 0,
    )[0]


def own_sums(table, kept, received, merged, pieces):
    terms, rows, cells = kept.shape
    return kernel_call(
        own_kernel, "own_sums", [table, kept, received, merged, *pieces], 1,
        [pltpu.VMEM((rows, cells), jnp.float32)], [], 8 * terms * rows * cells, 0,
    )[0]


def final_sums(own, last):
    rows, cells = own.shape
    return kernel_call(
        final_kernel, "final_sums", [own, last], 0,
        [jax.ShapeDtypeStruct((rows, cells), jnp.bfloat16)], [], 4 * rows * cells, 0,
    )[0]


def after(value, *earlier):
    return lax.optimization_barrier((value, *earlier))[0]


def gathered_shards(out_count, in_count, kernel_weights, mode_field, diff_blocks, block_table):
    columns = in_count // PAIR

    def across_cores(value):
        return lax.ppermute(value, "out", [(r, r ^ 1) for r in range(out_count)])

    def along_chips(value):
        return lax.ppermute(value, "out", [(r, (r + PAIR) % out_count) for r in range(out_count)])

    def across_sides(value):
        return lax.ppermute(value, "in", [(s, s ^ 1) for s in range(in_count)])

    def along_columns(value, shift):
        return lax.ppermute(value, "in", [(s, (s + PAIR * shift) % in_count) for s in range(in_count)])

    order = list(range(1, columns)) + [0]
    weights, own_field, own_blocks = load([kernel_weights, mode_field, diff_blocks])
    far_field = after(along_chips(mode_field), weights)
    fields = [own_field] + [near(field) for field in (far_field, across_cores(mode_field), across_cores(far_field))]

    rings = [diff_blocks]
    for step in range(1, columns):
        rings.append(along_columns(rings[-1], 1))
    kept, sent = {}, {}
    for step in order:
        kept[step], sent[step] = multiply(step, columns, weights, fields)
    core_own = across_cores(diff_blocks)
    far_own = along_chips(after(diff_blocks, far_field))
    far, pieces = [far_own], {}
    for place, step in enumerate(order[:-1]):
        earlier = [[far_field], [*sent.values(), core_own, far[-1]]][place] if place < 2 else far[-1:]
        far.append(along_chips(after(rings[step], *earlier)))

    received, coming = {}, []

    def send_sums(place):
        step = order[place]
        swapped = [received[step]] if place == 1 else []
        pieces[step] = [near(rings[step]), near(far[place + 1]), near(across_cores(rings[step]))]
        pieces[step].append(near(across_cores(after(far[place + 1], *swapped))))
        ready = after(kept[step], *(coming[-1:] if place < columns - 2 else []))
        partial = partial_sums(block_table, ready, received[step], pieces[step])
        coming.append(near(along_columns(partial, -step)))
        return partial

    for place, step in enumerate(order):
        earlier = [received[order[place - 1]]] if place > 0 else []
        if place > 1:
            earlier.append(send_sums(place - 2))
        received[step] = near(across_sides(after(sent[step], *earlier)))
    latest = send_sums(columns - 2)
    pieces[0] = [own_blocks, near(far_own), near(core_own), near(across_cores(after(far_own, latest)))]
    merged = near(merged_sums(coming[:-1], kernel_weights.shape[1]))
    own = near(own_sums(block_table, kept[0], received[0], merged, pieces[0]))
    return final_sums(own, coming[-1])


def solution(mesh):
    out_count, in_count = mesh.shape["out"], mesh.shape["in"]
    in_specs = (P(None, "out", "in"), P("in", "out"), P(None, "out", "in"), P())
    out_specs = P("out", "in")

    def shards(kernel_weights, mode_field, diff_blocks, block_table):
        own_cells = diff_blocks.shape[2]
        gather = (
            kernel_weights.shape[0] == PAIR
            and own_cells % LANES == 0
            and mode_field.shape[1] == PAIR * own_cells
            and out_count == PAIR * PAIR
            and in_count == PAIR * out_count
        )
        if gather:
            return gathered_shards(out_count, in_count, kernel_weights, mode_field, diff_blocks, block_table)
        return routed_shards(kernel_weights, mode_field, diff_blocks, block_table)

    return jax.shard_map(shards, mesh=mesh, in_specs=in_specs, out_specs=out_specs, check_vma=False)
```

```python
import functools
import math

import jax
import jax.numpy as jnp
from jax import lax
from jax.experimental import pallas as pl
from jax.experimental.pallas import tpu as pltpu
from jax.sharding import PartitionSpec as P

PAIR = 2
TOP = 32767.0
GROUPS = 4
MERGE_COST = 100000
KERNEL_MEMORY = 24 << 20
LANES = 128


def routed_shards(kernel_weights, mode_field, diff_blocks, block_table):
    out_index = lax.axis_index("out")
    tile_rows = kernel_weights.shape[1]
    term_count = kernel_weights.shape[0]
    own_cells = diff_blocks.shape[2]
    needed_row = block_table[out_index]
    whole_field = lax.all_gather(mode_field, "out", axis=1, tiled=True)
    every_block = lax.all_gather(diff_blocks, "out", axis=1, tiled=True)
    block_count = every_block.shape[1] // tile_rows
    every_block = every_block.reshape(term_count, block_count, tile_rows, own_cells)
    arranged = jnp.take(every_block, needed_row, axis=1)
    routed = lax.all_to_all(arranged, "in", split_axis=1, concat_axis=3, tiled=True)
    partial_value = jnp.zeros((tile_rows, whole_field.shape[1]), jnp.float32)
    for term_index in range(term_count):
        product = jnp.dot(kernel_weights[term_index], whole_field, preferred_element_type=jnp.float32)
        partial_value = partial_value + routed[term_index, 0].astype(jnp.float32) * product
    summed = lax.psum_scatter(partial_value, "in", scatter_dimension=1, tiled=True)
    return summed.astype(jnp.bfloat16)


def encode(values):
    largest = jnp.maximum(jnp.max(jnp.abs(values), axis=0, keepdims=True), 1e-25)
    exponent = jnp.floor(jnp.log2(largest)) + 1.0
    share = values * (jnp.exp2(-exponent) * (TOP * TOP))
    root = share * lax.rsqrt(jnp.abs(share) + 1e-9)
    return jnp.round(root).astype(jnp.int32), exponent.astype(jnp.int32)


def pack(high, low):
    return (high << 16) | (low & 0xFFFF)


def decode(codes, exponent):
    root = codes.astype(jnp.float32)
    return root * jnp.abs(root) * (jnp.exp2(exponent.astype(jnp.float32)) * (1.0 / (TOP * TOP)))


def unpack_high(packed, exponent):
    return decode(packed >> 16, exponent)


def unpack_low(packed, exponent):
    return decode((packed << 16) >> 16, exponent)


def position(index, out_index, chips):
    crossed = jnp.where(index % PAIR != out_index % PAIR, chips, 0)
    return crossed + (out_index // PAIR - index // PAIR + chips) % chips


def choose(index, refs, *at):
    value = refs[0][at]
    for place in range(1, len(refs)):
        value = jnp.where(index == place, refs[place][at], value)
    return value


def near(value):
    return pltpu.with_memory_space_constraint(value, pltpu.VMEM)


def kernel_call(kernel, name, inputs, in_table, outputs, scratch, flops, transcendentals):
    moved = sum(math.prod(array.shape) * jnp.dtype(array.dtype).itemsize for array in [*inputs, *outputs])
    memory = pl.BlockSpec(memory_space=pltpu.VMEM)
    return pl.pallas_call(
        kernel,
        name=name,
        out_shape=outputs,
        in_specs=[pl.BlockSpec(memory_space=pltpu.SMEM)] * in_table + [memory] * (len(inputs) - in_table),
        out_specs=[memory] * len(outputs),
        scratch_shapes=scratch,
        compiler_params=pltpu.CompilerParams(vmem_limit_bytes=KERNEL_MEMORY),
        cost_estimate=pl.CostEstimate(flops=flops, bytes_accessed=moved, transcendentals=transcendentals),
    )(*inputs)


def load_kernel(*refs):
    count = len(refs) // 2
    for source, place in zip(refs[:count], refs[count:]):
        place[...] = source[...]


def load(arrays):
    return kernel_call(
        load_kernel, "load", [near(array) for array in arrays], 0,
        [pltpu.VMEM(array.shape, array.dtype) for array in arrays], [], 0, 0,
    )


def multiply_kernel(shift, columns, weights, *refs):
    *fields, kept, sent, field = refs
    terms, total, _ = weights.shape
    rows = total // GROUPS
    half = kept.shape[2]
    in_index = lax.axis_index("in")
    target = (in_index // PAIR - shift + columns) % columns
    source = position(target, lax.axis_index("out"), len(fields) // PAIR)
    side = in_index % PAIR

    for place, ref in enumerate(fields):
        for first in range(PAIR):
            @pl.when((source == place) & (side == first))
            def _():
                field[:, :half] = ref[:, first * half:(first + 1) * half]
                field[:, half:] = ref[:, (1 - first) * half:(2 - first) * half]

    for group in range(GROUPS):
        chosen = slice(group * rows, (group + 1) * rows)
        codes = []
        for term in range(terms):
            product = jnp.dot(weights[term, chosen], field[...], preferred_element_type=jnp.float32)
            kept[term, chosen] = product[:, :half]
            code, exponent = encode(product[:, half:])
            codes.append(code)
            place = total + term * GROUPS + group
            sent[place:place + 1, :] = exponent
        sent[chosen, :] = pack(*codes)


def multiply(shift, columns, weights, fields):
    terms, rows, depth = weights.shape
    width = fields[0].shape[1]
    half = width // PAIR
    return kernel_call(
        functools.partial(multiply_kernel, shift, columns),
        "products",
        [weights, *fields],
        0,
        [
            pltpu.VMEM((terms, rows, half), jnp.float32),
            pltpu.VMEM((rows + terms * GROUPS, half), jnp.int32),
        ],
        [pltpu.VMEM((depth, width), jnp.bfloat16)],
        2 * terms * rows * depth * width,
        rows * half * terms,
    )


def wanted_blocks(table, chips):
    out_index, in_index = lax.axis_index("out"), lax.axis_index("in")
    column, side = in_index // PAIR, in_index % PAIR
    return [position(table[out_index, column * PAIR + which], out_index, chips) for which in (side, 1 - side)]


def blocks_times_products(wanted, kept, received, pieces, rows, total):
    packed = received[rows, :]
    scale = total + rows.start // (total // GROUPS)
    mine = [kept[0, rows], kept[1, rows]]
    other = [
        unpack_high(packed, received[scale:scale + 1, :]),
        unpack_low(packed, received[scale + GROUPS:scale + GROUPS + 1, :]),
    ]
    value = None
    for index, products in zip(wanted, (mine, other)):
        for term, product in enumerate(products):
            chosen = choose(index, pieces, term, rows).astype(jnp.float32)
            value = chosen * product if value is None else value + chosen * product
    return value


def row_ranges(total):
    half = total // PAIR
    step = half // GROUPS
    return [
        [slice(part * half + group * step, part * half + (group + 1) * step) for part in range(PAIR)]
        for group in range(GROUPS)
    ]


def partial_kernel(table, kept, received, *refs):
    *pieces, sent = refs
    total = kept.shape[1]
    wanted = wanted_blocks(table, len(pieces) // PAIR)
    for group, parts in enumerate(row_ranges(total)):
        codes = []
        for part, rows in enumerate(parts):
            code, exponent = encode(blocks_times_products(wanted, kept, received, pieces, rows, total))
            codes.append(code)
            place = total // PAIR + part * GROUPS + group
            sent[place:place + 1, :] = exponent
        sent[parts[0], :] = pack(*codes)


def merge_kernel(*refs):
    *coming, merged = refs
    total = merged.shape[0]
    for group, parts in enumerate(row_ranges(total)):
        for part, (rows, unpack) in enumerate(zip(parts, (unpack_high, unpack_low))):
            place = total // PAIR + part * GROUPS + group
            values = [unpack(ref[parts[0], :], ref[place:place + 1, :]) for ref in coming]
            merged[rows, :] = functools.reduce(jnp.add, values)


def own_kernel(table, kept, received, merged, *refs):
    *pieces, result = refs
    total = kept.shape[1]
    wanted = wanted_blocks(table, len(pieces) // PAIR)
    for parts in row_ranges(total):
        for rows in parts:
            result[rows, :] = merged[rows, :] + blocks_times_products(wanted, kept, received, pieces, rows, total)


def final_kernel(own, last, gain):
    total = own.shape[0]
    for group, parts in enumerate(row_ranges(total)):
        for part, (rows, unpack) in enumerate(zip(parts, (unpack_high, unpack_low))):
            place = total // PAIR + part * GROUPS + group
            value = own[rows, :] + unpack(last[parts[0], :], last[place:place + 1, :])
            gain[rows, :] = value.astype(gain.dtype)


def partial_sums(table, kept, received, pieces):
    terms, rows, cells = kept.shape
    shape = (rows // PAIR + PAIR * GROUPS, cells)
    return kernel_call(
        partial_kernel, "partial_sums", [table, kept, received, *pieces], 1,
        [pltpu.VMEM(shape, jnp.int32)], [], 8 * terms * rows * cells, rows * cells,
    )[0]


def merged_sums(coming, rows):
    cells = coming[0].shape[1]
    return kernel_call(
        merge_kernel, "merged_sums", coming, 0,
        [pltpu.VMEM((rows, cells), jnp.float32)], [], MERGE_COST * rows * cells, 0,
    )[0]


def own_sums(table, kept, received, merged, pieces):
    terms, rows, cells = kept.shape
    return kernel_call(
        own_kernel, "own_sums", [table, kept, received, merged, *pieces], 1,
        [pltpu.VMEM((rows, cells), jnp.float32)], [], 8 * terms * rows * cells, 0,
    )[0]


def final_sums(own, last):
    rows, cells = own.shape
    return kernel_call(
        final_kernel, "final_sums", [own, last], 0,
        [jax.ShapeDtypeStruct((rows, cells), jnp.bfloat16)], [], 4 * rows * cells, 0,
    )[0]


def after(value, *earlier):
    return lax.optimization_barrier((value, *earlier))[0]


def gathered_shards(out_count, in_count, kernel_weights, mode_field, diff_blocks, block_table):
    columns = in_count // PAIR

    def across_cores(value):
        return lax.ppermute(value, "out", [(r, r ^ 1) for r in range(out_count)])

    def along_chips(value):
        return lax.ppermute(value, "out", [(r, (r + PAIR) % out_count) for r in range(out_count)])

    def across_sides(value):
        return lax.ppermute(value, "in", [(s, s ^ 1) for s in range(in_count)])

    def along_columns(value, shift):
        return lax.ppermute(value, "in", [(s, (s + PAIR * shift) % in_count) for s in range(in_count)])

    order = list(range(1, columns)) + [0]
    weights, own_field, own_blocks = load([kernel_weights, mode_field, diff_blocks])
    far_field = after(along_chips(mode_field), weights)
    fields = [own_field] + [near(field) for field in (far_field, across_cores(mode_field), across_cores(far_field))]

    rings = [diff_blocks]
    for step in range(1, columns):
        rings.append(along_columns(rings[-1], 1))
    kept, sent = {}, {}
    for step in order:
        kept[step], sent[step] = multiply(step, columns, weights, fields)
    core_own = across_cores(diff_blocks)
    far_own = along_chips(after(diff_blocks, far_field))
    far, pieces = [far_own], {}
    for place, step in enumerate(order[:-1]):
        earlier = [[far_field], [*sent.values(), core_own, far[-1]]][place] if place < 2 else far[-1:]
        far.append(along_chips(after(rings[step], *earlier)))

    received, coming = {}, []

    def send_sums(place):
        step = order[place]
        swapped = [received[step]] if place == 1 else []
        pieces[step] = [near(rings[step]), near(far[place + 1]), near(across_cores(rings[step]))]
        pieces[step].append(near(across_cores(after(far[place + 1], *swapped))))
        ready = after(kept[step], *(coming[-1:] if place < columns - 2 else []))
        partial = partial_sums(block_table, ready, received[step], pieces[step])
        coming.append(near(along_columns(partial, -step)))
        return partial

    for place, step in enumerate(order):
        earlier = [received[order[place - (2 if place == columns - 1 else 1)]]] if place > 0 else []
        if place > 1:
            earlier.append(send_sums(place - 2))
        received[step] = near(across_sides(after(sent[step], *earlier)))
    latest = send_sums(columns - 2)
    pieces[0] = [own_blocks, near(far_own), near(core_own), near(across_cores(after(far_own, latest)))]
    merged = near(merged_sums(coming[:-1], kernel_weights.shape[1]))
    own = near(own_sums(block_table, kept[0], received[0], merged, pieces[0]))
    return final_sums(own, coming[-1])


def solution(mesh):
    out_count, in_count = mesh.shape["out"], mesh.shape["in"]
    in_specs = (P(None, "out", "in"), P("in", "out"), P(None, "out", "in"), P())
    out_specs = P("out", "in")

    def shards(kernel_weights, mode_field, diff_blocks, block_table):
        own_cells = diff_blocks.shape[2]
        gather = (
            kernel_weights.shape[0] == PAIR
            and own_cells % LANES == 0
            and mode_field.shape[1] == PAIR * own_cells
            and out_count == PAIR * PAIR
            and in_count == PAIR * out_count
        )
        if gather:
            return gathered_shards(out_count, in_count, kernel_weights, mode_field, diff_blocks, block_table)
        return routed_shards(kernel_weights, mode_field, diff_blocks, block_table)

    return jax.shard_map(shards, mesh=mesh, in_specs=in_specs, out_specs=out_specs, check_vma=False)
```
